128 devices in a mesh: lon: 16 (over y_hi, z, core), lat: 8 (over y_lo, x).
Axes of the slice: x: 4, y: 4 (y_hi: 2, y_lo: 2; y = y_hi * 2 + y_lo), z: 4, core: 2. Of those that a mesh axis runs over, the one named last changes fastest.
Arguments:
- tracers: float32 [32, 64, 32768], P(None, 'lat', 'lon'), may hold values from 0.1 to 10
- courant: float32 [2, 64, 512], P(None, 'lat', 'lon'), may hold values from -0.45 to 0.45
- switches: int32 [2, 64, 512], P(None, 'lat', 'lon'), may hold values 0 or 1
- day_flags: int32 [64, 512], P('lat', 'lon'), may hold values from 0 to 1, as said below
- diffusion_counts: int32 [64, 512], P('lat', 'lon'), may hold values from 1 to 8
- night_rates: float32 [32, 32], replicated, may hold values from -0.18 to 0.18
- photo_rates: float32 [32, 32], replicated, may hold values from -0.24 to 0.24
- level_light: float32 [64], replicated, may hold values from 0.1 to 1
- self_loss: float32 [32], replicated, may hold values from 0.001 to 0.05
- vertical_mixing: float32 [63], replicated, may hold values from 0.05 to 0.45
Outputs:
- tracers_out: float32 [32, 64, 32768], P(None, 'lat', 'lon')
The draws below stay inside these ranges and needn't reach their ends.
Inputs may be any that keep to these rules, and one draw needn't show every extreme that they name: `day_flags`: in every latitude row exactly half of the 512 columns are day columns, forming one contiguous band around the longitude cycle.
All inputs are finite; a program needn't handle non-finite values. No bound on the sum of `switches` on one device may be relied on, other than what follows from the above.
Results may differ from the reference program's by a relative error of at most 0.0003.
Values sent between devices are 32-bit elements; how exact they have to be, the bound alone decides.
No kernel may reach another device: no remote copies, remote signals or barrier semaphores. Data moves between devices by JAX's collectives and lax.ppermute only.
A program may use at most 64 MiB of HBM per device.

```python
import math
import jax
import jax.numpy as jnp
from jax import lax

SPECIES = 32
LEVELS = 64
CHEM = 6
KMAX = 8
NLAT = 64
NLON = 512


def column_plan(key):
    base_key = jax.random.fold_in(key, 4099)
    key_offset, key_jitter, key_night, key_day = jax.random.split(base_key, 4)
    offset = jax.random.randint(key_offset, (), 0, NLON)
    jitter = jax.random.randint(key_jitter, (NLAT, 1), -2, 3)
    longitude = jnp.arange(NLON, dtype=jnp.int32)[None, :]
    daylight = ((longitude - offset - jitter) % NLON < NLON // 2).astype(jnp.int32)
    night_counts = jax.random.randint(key_night, (NLAT, NLON), 1, KMAX // 2 + 1)
    day_counts = jax.random.randint(key_day, (NLAT, NLON), KMAX // 2, KMAX + 1)
    substeps = jnp.where(daylight == 1, day_counts, night_counts).astype(jnp.int32)
    substeps = substeps.at[0, 0].set(KMAX).at[NLAT - 1, NLON - 1].set(1)
    return (daylight, substeps)


def draw_day_flags(key, part):
    return column_plan(key)[0]


def draw_diffusion_counts(key, part):
    return column_plan(key)[1]


def set_ends(values, stream_key, low, top_value):
    index_at = [jax.random.randint(jax.random.fold_in(stream_key, axis), (), 0, length) for axis, length in enumerate(values.shape)]
    main_axis = values.shape.index(max(values.shape))
    next_to = index_at[:main_axis] + [(index_at[main_axis] + 1) % values.shape[main_axis]] + index_at[main_axis + 1:]
    return values.at[tuple(index_at)].set(low).at[tuple(next_to)].set(top_value)


def block_scale(rng, dims, cuts, smallest, top_value):
    def one(position, blocks):
        heights = jax.random.uniform(jax.random.fold_in(jax.random.fold_in(rng, 6), position), (blocks,), jnp.float32, smallest / len(cuts), top_value / len(cuts))
        return jnp.repeat(jnp.exp(heights), dims[position] // blocks).reshape((-1,) + (1,) * (len(dims) - position - 1))

    factor_of = one(*cuts[0])
    for cut in cuts[1:]:
        factor_of = factor_of * one(*cut)
    return factor_of


def bell_draw(key, shape, spread, most, held_as=jnp.bfloat16):
    entries = jax.random.normal(key, shape, jnp.float32) * spread
    return jnp.minimum(jnp.maximum(entries, -most), most).astype(held_as)


def setup_inputs(seed: int = 0) -> dict:
    streams_of = jax.random.split(jax.random.key(seed), 11)
    return {
        "tracers": jnp.clip(jnp.exp(math.log(10.0) - 4.6051702 * jax.random.uniform(streams_of[0], (SPECIES, NLAT, NLON * LEVELS), jnp.float32) ** block_scale(streams_of[0], (SPECIES, NLAT, NLON * LEVELS), ((1, 8), (2, 16)), -0.2, 0.2)), 0.1, 10.0),
        "courant": jnp.clip(jax.random.uniform(streams_of[1], (2, NLAT, NLON), jnp.float32, -0.45, 0.45) * block_scale(streams_of[1], (2, NLAT, NLON), ((1, 8), (2, 16)), -0.4, 0.0), -0.45, 0.45),
        "switches": set_ends((jax.random.randint(streams_of[2], (2, NLAT, NLON), 0, 4) < 3).astype(jnp.int32), jax.random.fold_in(streams_of[2], 1), 0, 1),
        "day_flags": draw_day_flags(jax.random.fold_in(streams_of[10], 71), 0),
        "diffusion_counts": draw_diffusion_counts(jax.random.fold_in(streams_of[10], 71), 0),
        "night_rates": bell_draw(streams_of[5], (SPECIES, SPECIES), 0.03, 0.18, jnp.float32),
        "photo_rates": bell_draw(streams_of[6], (SPECIES, SPECIES), 0.04, 0.24, jnp.float32),
        "level_light": jnp.clip(jnp.exp(jax.random.uniform(streams_of[7], (LEVELS,), jnp.float32, math.log(0.1), math.log(1.0))), 0.1, 1.0),
        "self_loss": jnp.clip(jnp.exp(jax.random.uniform(streams_of[8], (SPECIES,), jnp.float32, math.log(0.001), math.log(0.05))), 0.001, 0.05),
        "vertical_mixing": jnp.clip(jax.random.uniform(streams_of[9], (LEVELS - 1,), jnp.float32, 0.05, 0.45), 0.05, 0.45),
    }


def minmod(left, right):
    return 0.5 * (jnp.sign(left) + jnp.sign(right)) * jnp.minimum(jnp.abs(left), jnp.abs(right))


def advect_sweep(extended, cour, switch, along_axis, cell_count, cell_unit):
    def take_cells(first_cell, number):
        return lax.slice_in_dim(extended, first_cell * cell_unit, (first_cell + number) * cell_unit, axis=along_axis)

    second_left = take_cells(0, cell_count + 1)
    first_left = take_cells(1, cell_count + 1)
    first_right = take_cells(2, cell_count + 1)
    second_right = take_cells(3, cell_count + 1)
    plus_flux = cour * (first_left + 0.5 * (1.0 - cour) * switch * minmod(first_left - second_left, first_right - first_left))
    minus_flux = cour * (first_right - 0.5 * (1.0 + cour) * switch * minmod(first_right - first_left, second_right - first_right))
    face_flux = jnp.where(cour >= 0.0, plus_flux, minus_flux)
    upper_faces = lax.slice_in_dim(face_flux, cell_unit, (cell_count + 1) * cell_unit, axis=along_axis)
    lower_faces = lax.slice_in_dim(face_flux, 0, cell_count * cell_unit, axis=along_axis)
    return take_cells(2, cell_count) - (upper_faces - lower_faces)


def react_mix(tracer_block, daylight, substeps, rate_rows, level_light, self_loss, vertical_mixing, loop_count):
    species = tracer_block.shape[0]
    levels = level_light.shape[0]
    column = daylight.shape[-1]
    sunlight = jnp.repeat(daylight.astype(jnp.float32), levels, axis=-1) * jnp.tile(level_light, column)
    self_term = self_loss.reshape((species,) + (1,) * (tracer_block.ndim - 1))
    for _ in range(CHEM):
        flat = tracer_block.reshape(species, -1)
        joined = jnp.dot(rate_rows, flat, precision=lax.Precision.HIGHEST).reshape((2,) + tracer_block.shape)
        tracer_block = (tracer_block + joined[0] + sunlight * joined[1]) / (1.0 + self_term * tracer_block * tracer_block)
    mixing_faces = jnp.tile(jnp.concatenate([vertical_mixing, jnp.zeros((1,), vertical_mixing.dtype)]), column)
    step_limits = jnp.repeat(substeps, levels, axis=-1)

    def mix_step(step_index, tracer_field):
        edge = jnp.zeros_like(tracer_field[..., :1])
        above_cells = jnp.concatenate([tracer_field[..., 1:], edge], -1)
        level_flux = mixing_faces * (above_cells - tracer_field)
        below_flux = jnp.concatenate([edge, level_flux[..., :-1]], -1)
        return jnp.where(step_index < step_limits, tracer_field + level_flux - below_flux, tracer_field)

    return lax.fori_loop(0, loop_count, mix_step, tracer_block)


def reference(tracers, courant, switches, day_flags, diffusion_counts, night_rates, photo_rates, level_light, self_loss, vertical_mixing):
    switch_float = switches.astype(jnp.float32)
    lon_cour = jnp.concatenate([courant[0], courant[0][:, :1]], 1)
    lon_switch = jnp.concatenate([switch_float[0], switch_float[0][:, :1]], 1)
    row_valid = (jnp.arange(NLAT) >= 1).astype(jnp.float32)[:, None]
    lat_cour = jnp.concatenate([courant[1] * row_valid, jnp.zeros((1, NLON), jnp.float32)], 0)
    lat_switch = jnp.concatenate([switch_float[1], jnp.zeros((1, NLON), jnp.float32)], 0)
    lon_cour = jnp.repeat(lon_cour, LEVELS, axis=1)
    lon_switch = jnp.repeat(lon_switch, LEVELS, axis=1)
    lat_cour = jnp.repeat(lat_cour, LEVELS, axis=1)
    lat_switch = jnp.repeat(lat_switch, LEVELS, axis=1)

    def transport(tracer_field):
        extended = jnp.concatenate([tracer_field[:, -2 * LEVELS:], tracer_field, tracer_field[:, :2 * LEVELS]], 1)
        midway = advect_sweep(extended, lon_cour, lon_switch, 1, NLON, LEVELS)
        extended = jnp.pad(midway, ((2, 2), (0, 0)))
        return advect_sweep(extended, lat_cour, lat_switch, 0, NLAT, 1)

    rate_rows = jnp.concatenate([night_rates, photo_rates], 0)
    advected = lax.map(transport, tracers)

    def column_work(item):
        tracer_block, daylight, substeps = item
        return react_mix(tracer_block, daylight, substeps, rate_rows, level_light, self_loss, vertical_mixing, KMAX)

    reacted = lax.map(column_work, (jnp.moveaxis(advected, 1, 0), day_flags, diffusion_counts))
    return lax.map(transport, jnp.moveaxis(reacted, 0, 1))
```

```python
import jax
import jax.numpy as jnp
from jax import lax
from jax.experimental import pallas as pl
from jax.experimental.pallas import tpu as pltpu
from jax.sharding import PartitionSpec as P

CHEM = 6
KMAX = 8
PIECE = 128
HALF = 64
VMEM_LIMIT = 24 * 1024 * 1024
F32 = jnp.float32
BF16 = jnp.bfloat16
LON_C, LON_G, LAT_C, LAT_G, DAY, COUNT = range(6)


def ring(value, axis, steps):
    count = lax.axis_size(axis)
    return lax.ppermute(value, axis, [(i, (i + steps) % count) for i in range(count)])


def half_roll(value):
    return pltpu.roll(value, HALF, 1)


def minmod(x, y):
    return jnp.minimum(jnp.maximum(x, jnp.minimum(y, 0.0)), jnp.maximum(y, 0.0))


def gain(cour, switch):
    return 0.5 * cour * switch * jnp.where(cour >= 0.0, 1.0 - cour, -1.0 - cour)


def lon_sweep(cells, cours, gains):
    n = len(cells)
    low = lax.broadcasted_iota(jnp.int32, cells[0].shape, 1) < HALF
    turned = [half_roll(q) for q in cells]
    west = [turned[0]] + [jnp.where(low, turned[i - 1], turned[i]) for i in range(1, n)]
    step = [q - w for q, w in zip(cells, west)]
    turned = [half_roll(d) for d in step]
    ahead = [jnp.where(low, turned[i], turned[i + 1]) for i in range(n - 1)] + [turned[n - 1]]
    slope = [minmod(d, a) for d, a in zip(step, ahead)]
    turned = [half_roll(s) for s in slope]
    flux = [None]
    for i in range(1, n):
        forward = cours[i - 1] >= 0.0
        behind = jnp.where(low, turned[i - 1], turned[i])
        flux.append(
            cours[i - 1] * jnp.where(forward, west[i], cells[i])
            + gains[i - 1] * jnp.where(forward, behind, slope[i])
        )
    turned = [None] + [half_roll(f) for f in flux[1:]]
    return [
        cells[i] - (jnp.where(low, turned[i], turned[i + 1]) - flux[i]) for i in range(1, n - 1)
    ]


def lat_sweep(rows, cours, gains):
    n = len(rows) - 4
    step = [rows[i + 1] - rows[i] for i in range(n + 3)]
    slope = [minmod(step[i], step[i + 1]) for i in range(n + 2)]
    flux = []
    for i in range(n + 1):
        forward = cours[i] >= 0.0
        flux.append(
            cours[i] * jnp.where(forward, rows[i + 1], rows[i + 2])
            + gains[i] * jnp.where(forward, slope[i], slope[i + 1])
        )
    return [rows[i + 2] - (flux[i + 1] - flux[i]) for i in range(n)]


def expand(compact, first):
    rows = compact.shape[0]
    low = lax.broadcasted_iota(jnp.int32, (rows, PIECE), 1) < HALF
    left = jnp.broadcast_to(compact[:, first : first + 1], (rows, PIECE))
    right = jnp.broadcast_to(compact[:, first + 1 : first + 2], (rows, PIECE))
    return jnp.where(low, left, right)


def rate_pieces(night_ref, photo_ref):
    rates = jnp.concatenate([night_ref[...], photo_ref[...]], 0)
    high = rates.astype(BF16)
    low = (rates - high.astype(F32)).astype(BF16)
    return jnp.concatenate([high, high, low], 1)


def react(rows, suns, rates, loss):
    species = rows[0].shape[0]
    for _ in range(CHEM):
        nexts = []
        for q, sun in zip(rows, suns):
            high = q.astype(BF16)
            low = (q - high.astype(F32)).astype(BF16)
            both = jnp.dot(
                rates, jnp.concatenate([high, low, high], 0), preferred_element_type=F32
            )
            top = q + both[:species] + sun * both[species:]
            bottom = 1.0 + loss * q * q
            inverse = pl.reciprocal(bottom, approx=True)
            inverse = inverse * (2.0 - bottom * inverse)
            nexts.append(top * inverse)
        rows = nexts
    return rows


def diffuse(q, count, mixing):
    for step in range(KMAX):
        number = jnp.where(count > step, mixing, 0.0)
        flux = number * (pltpu.roll(q, PIECE - 1, 1) - q)
        q = q + flux - pltpu.roll(flux, 1, 1)
    return q


def column_block(rows, days, counts, rates, loss, level, mixing):
    suns = [day * level for day in days]
    rows = react(rows, suns, rates, loss)
    done = []
    for q, count in zip(rows, counts):
        done.append(
            jnp.concatenate(
                [
                    diffuse(q[:, h : h + PIECE], count[:, h : h + PIECE], mixing)
                    for h in (0, PIECE)
                ],
                1,
            )
        )
    return done


def call(kernel, outs, ins, *args, scratch=(), cost=1e7):
    return pl.pallas_call(
        kernel,
        out_shape=[jax.ShapeDtypeStruct(s, F32) for s in outs],
        in_specs=ins,
        out_specs=[pl.BlockSpec(memory_space=pltpu.VMEM)] * len(outs),
        scratch_shapes=list(scratch),
        compiler_params=pltpu.CompilerParams(vmem_limit_bytes=VMEM_LIMIT),
        cost_estimate=pl.CostEstimate(flops=int(cost), bytes_accessed=4000000, transcendentals=0),
    )(*args)


WHOLE = pl.BlockSpec(memory_space=pltpu.VMEM)


def first_kernel(x_ref, cour_ref, sw_ref, day_ref, cnt_ref, south_ref, north_ref, west_ref, east_ref, coef_ref):
    species, rows, width = x_ref.shape
    pieces = width // PIECE
    cour = [cour_ref[0], cour_ref[1]]
    switch = [sw_ref[0].astype(F32), sw_ref[1].astype(F32)]
    fields = [
        cour[0],
        gain(cour[0], switch[0]),
        cour[1],
        gain(cour[1], switch[1]),
        day_ref[...].astype(F32),
        cnt_ref[...].astype(F32),
    ]
    for i, field in enumerate(fields):
        for j in range(pieces):
            coef_ref[i, :, j * PIECE : (j + 1) * PIECE] = expand(field, 2 * j)
    columns = 2 * pieces
    edge = 2 * PIECE
    for ref, first, at in ((west_ref, 0, 0), (east_ref, columns - 4, width - edge)):
        for s in range(species):
            ref[s] = x_ref[s, :, at : at + edge]
        for i, field in enumerate(fields):
            for half in (0, 1):
                ref[species + i, :, half * PIECE : (half + 1) * PIECE] = expand(field, first + 2 * half)

    def tile(s, carry):
        at = pl.multiple_of(s * 8, 8)
        for r in (0, 1, rows - 2, rows - 1):
            cells = [x_ref[pl.ds(at, 8), r, j * PIECE : (j + 1) * PIECE] for j in range(pieces)]
            cours = [coef_ref[LON_C, r : r + 1, j * PIECE : (j + 1) * PIECE] for j in range(1, pieces)]
            gains = [coef_ref[LON_G, r : r + 1, j * PIECE : (j + 1) * PIECE] for j in range(1, pieces)]
            out = lon_sweep(cells, cours, gains)
            ref, row = (south_ref, r) if r < 2 else (north_ref, r - rows + 2)
            for j, value in enumerate(out):
                ref[row, pl.ds(at, 8), j * PIECE : (j + 1) * PIECE] = value
        return carry

    lax.fori_loop(0, species // 8, tile, 0)


def inner_kernel(x_ref, coef_ref, par_ref, loss_ref, night_ref, photo_ref, mid_ref, done_ref):
    species, rows, width = x_ref.shape
    pieces = width // PIECE

    def tile(s, carry):
        at = pl.multiple_of(s * 8, 8)
        for r in range(rows):
            cells = [x_ref[pl.ds(at, 8), r, j * PIECE : (j + 1) * PIECE] for j in range(pieces)]
            cours = [coef_ref[LON_C, r : r + 1, j * PIECE : (j + 1) * PIECE] for j in range(1, pieces)]
            gains = [coef_ref[LON_G, r : r + 1, j * PIECE : (j + 1) * PIECE] for j in range(1, pieces)]
            for j, value in enumerate(lon_sweep(cells, cours, gains)):
                mid_ref[r, pl.ds(at, 8), j * PIECE : (j + 1) * PIECE] = value
        return carry

    lax.fori_loop(0, species // 8, tile, 0)
    rates = rate_pieces(night_ref, photo_ref)
    level = jnp.concatenate([par_ref[0:1]] * 2, 1)
    loss = jnp.concatenate([loss_ref[...]] * 2, 1)
    mixing = par_ref[1:2]
    wide = 2 * PIECE

    def block(b, carry):
        at = pl.multiple_of(b * wide, wide)
        here = pl.ds(at, wide)
        own = pl.ds(pl.multiple_of(at + PIECE, PIECE), wide)
        cells = [mid_ref[r, :, here] for r in range(rows)]
        faces = range(2, rows - 1)
        cells = lat_sweep(
            cells,
            [coef_ref[LAT_C, f : f + 1, own] for f in faces],
            [coef_ref[LAT_G, f : f + 1, own] for f in faces],
        )
        inner = range(2, rows - 2)
        cells = column_block(
            cells,
            [coef_ref[DAY, r : r + 1, own] for r in inner],
            [coef_ref[COUNT, r : r + 1, own] for r in inner],
            rates,
            loss,
            level,
            mixing,
        )
        for i, q in enumerate(cells):
            done_ref[i, :, here] = q
        return carry

    lax.fori_loop(0, (pieces - 2) // 2, block, 0)


def side_kernel(xw_ref, xe_ref, hw_ref, he_ref, coef_ref, mid_ref, south_ref, north_ref, side_ref):
    species, rows = xw_ref.shape[0] - 6, xw_ref.shape[1]
    width = coef_ref.shape[2]
    for i in range(6):
        side_ref[i, :, 0:PIECE] = hw_ref[species + i, :, PIECE : 2 * PIECE]
        side_ref[i, :, PIECE : 2 * PIECE] = coef_ref[i, :, 0:PIECE]
        side_ref[i, :, 2 * PIECE : 3 * PIECE] = coef_ref[i, :, width - PIECE : width]
        side_ref[i, :, 3 * PIECE : 4 * PIECE] = he_ref[species + i, :, 0:PIECE]

    def tile(s, carry):
        at = pl.multiple_of(s * 8, 8)
        block = pl.ds(at, 8)
        for r in range(rows):
            row = slice(r, r + 1)
            cells = [ref[block, r, h : h + PIECE] for ref in (hw_ref, xw_ref) for h in (0, PIECE)]
            faces = [
                [side_ref[i, row, 0:PIECE], side_ref[i, row, PIECE : 2 * PIECE], coef_ref[i, row, PIECE : 2 * PIECE]]
                for i in (LON_C, LON_G)
            ]
            out = lon_sweep(cells, *faces)
            cells = [ref[block, r, h : h + PIECE] for ref in (xe_ref, he_ref) for h in (0, PIECE)]
            faces = [
                [
                    side_ref[i, row, 2 * PIECE : 3 * PIECE],
                    side_ref[i, row, 3 * PIECE : 4 * PIECE],
                    he_ref[species + i, row, PIECE : 2 * PIECE],
                ]
                for i in (LON_C, LON_G)
            ]
            out = out + lon_sweep(cells, *faces)
            for j, value in enumerate(out):
                lanes = slice(j * PIECE, (j + 1) * PIECE)
                mid_ref[r, block, lanes] = value
                if r < 2:
                    south_ref[pl.ds(r * species + at, 8), lanes] = value
                if r >= rows - 2:
                    north_ref[pl.ds((r - rows + 2) * species + at, 8), lanes] = value
        return carry

    lax.fori_loop(0, species // 8, tile, 0)
    for j in range(4):
        lanes = slice(j * PIECE, (j + 1) * PIECE)
        two = [side_ref[i, 0:1, lanes] for i in (LAT_C, LAT_G)]
        south_ref[2 * species : 2 * species + 8, lanes] = jnp.concatenate([two[0]] * 4 + [two[1]] * 4, 0)


def edge_kernel(
    mid_ref, south_ref, north_ref, done_ref, midc_ref, southc_ref, northc_ref, coef_ref, side_ref, row_ref,
    par_ref, loss_ref, night_ref, photo_ref, sent_south_ref, sent_north_ref, swept_ref, field_ref,
):
    rows, species, inner_width = mid_ref.shape
    rates = rate_pieces(night_ref, photo_ref)
    level = jnp.concatenate([par_ref[0:1]] * 2, 1)
    loss = jnp.concatenate([loss_ref[...]] * 2, 1)
    mixing = par_ref[1:2]
    wide = 2 * PIECE
    valid_south = jnp.concatenate([par_ref[2:3]] * 2, 1)
    valid_north = jnp.concatenate([par_ref[3:4]] * 2, 1)

    def block(b, carry):
        at = pl.multiple_of(b * wide, wide)
        here = pl.ds(at, wide)
        own = pl.ds(pl.multiple_of(at + PIECE, PIECE), wide)
        lower = [south_ref[i, :, here] * valid_south for i in (0, 1)] + [mid_ref[r, :, here] for r in range(4)]
        upper = [mid_ref[r, :, here] for r in range(4, 8)] + [north_ref[i, :, here] * valid_north for i in (0, 1)]
        faces = [
            [
                [coef_ref[i, 0:1, own] * valid_south, coef_ref[i, 1:2, own], coef_ref[i, 2:3, own]],
                [coef_ref[i, 6:7, own], coef_ref[i, 7:8, own], row_ref[i - LAT_C, 0:1, own] * valid_north],
            ]
            for i in (LAT_C, LAT_G)
        ]
        cells = lat_sweep(lower, faces[0][0], faces[1][0]) + lat_sweep(upper, faces[0][1], faces[1][1])
        edge = (0, 1, 6, 7)
        cells = column_block(
            cells,
            [coef_ref[DAY, r : r + 1, own] for r in edge],
            [coef_ref[COUNT, r : r + 1, own] for r in edge],
            rates,
            loss,
            level,
            mixing,
        )
        out = pl.ds(pl.multiple_of(at + wide, PIECE), wide)
        for r, q in zip(edge, cells):
            field_ref[r, :, out] = q
        for i in range(4):
            field_ref[i + 2, :, out] = done_ref[i, :, here]
        return carry

    lax.fori_loop(0, inner_width // wide, block, 0)

    def side(b, carry):
        here = pl.ds(pl.multiple_of(b * wide, wide), wide)
        cells = (
            [southc_ref[i * species : (i + 1) * species, here] * valid_south for i in (0, 1)]
            + [midc_ref[r, :, here] for r in range(rows)]
            + [northc_ref[i * species : (i + 1) * species, here] * valid_north for i in (0, 1)]
        )
        faces = [
            [side_ref[i, 0:1, here] * valid_south]
            + [side_ref[i, r : r + 1, here] for r in range(1, rows)]
            + [northc_ref[2 * species + 4 * (i - LAT_C) : 2 * species + 4 * (i - LAT_C) + 1, here] * valid_north]
            for i in (LAT_C, LAT_G)
        ]
        cells = lat_sweep(cells, *faces)
        for part in (slice(0, 4), slice(4, 8)):
            done = column_block(
                cells[part],
                [side_ref[DAY, r : r + 1, here] for r in range(rows)[part]],
                [side_ref[COUNT, r : r + 1, here] for r in range(rows)[part]],
                rates,
                loss,
                level,
                mixing,
            )
            out = pl.ds(pl.multiple_of(b * (inner_width + wide), PIECE), wide)
            for r, q in zip(range(rows)[part], done):
                field_ref[r, :, out] = q
        return carry

    lax.fori_loop(0, 2, side, 0)
    pieces = (inner_width + 4 * PIECE) // PIECE

    def tile(s, carry):
        block = pl.ds(pl.multiple_of(s * 8, 8), 8)
        for r in range(rows):
            row = slice(r, r + 1)
            cells = [field_ref[r, block, j * PIECE : (j + 1) * PIECE] for j in range(pieces)]
            faces = [
                [coef_ref[i, row, j * PIECE : (j + 1) * PIECE] for j in range(pieces - 2)]
                + [side_ref[i, row, 3 * PIECE : 4 * PIECE]]
                for i in (LON_C, LON_G)
            ]
            for j, value in enumerate(lon_sweep(cells, *faces)):
                lanes = slice(j * PIECE, (j + 1) * PIECE)
                swept_ref[r, block, lanes] = value
                if r < 2:
                    sent_south_ref[r, block, lanes] = value
                if r >= rows - 2:
                    sent_north_ref[r - rows + 2, block, lanes] = value
        return carry

    lax.fori_loop(0, species // 8, tile, 0)


def last_kernel(swept_ref, south_ref, north_ref, coef_ref, row_ref, par_ref, out_ref):
    rows, species, width = swept_ref.shape
    valid_south, valid_north = par_ref[2:3], par_ref[3:4]

    def piece(j, carry):
        here = pl.ds(pl.multiple_of(j * PIECE, PIECE), PIECE)
        cells = (
            [south_ref[i, :, here] * valid_south for i in (0, 1)]
            + [swept_ref[r, :, here] for r in range(rows)]
            + [north_ref[i, :, here] * valid_north for i in (0, 1)]
        )
        faces = [
            [coef_ref[i, 0:1, here] * valid_south]
            + [coef_ref[i, r : r + 1, here] for r in range(1, rows)]
            + [row_ref[i - LAT_C, 0:1, here] * valid_north]
            for i in (LAT_C, LAT_G)
        ]
        for r, q in enumerate(lat_sweep(cells, *faces)):
            out_ref[:, r, here] = q
        return carry

    lax.fori_loop(0, width // PIECE, piece, 0)


def shards(
    tracers,
    courant,
    switches,
    day_flags,
    diffusion_counts,
    night_rates,
    photo_rates,
    level_light,
    self_loss,
    vertical_mixing,
):
    species, rows, width = tracers.shape
    inner = width - 2 * PIECE
    lat_count = lax.axis_size("lat")
    lat = lax.axis_index("lat")
    two = 2 * PIECE

    sent_south, sent_north, sent_west, sent_east, coef = call(
        first_kernel,
        [(2, species, inner), (2, species, inner), (species + 6, rows, two), (species + 6, rows, two), (6, rows, width)],
        [WHOLE] * 5,
        tracers,
        courant,
        switches,
        day_flags,
        diffusion_counts,
    )
    south = ring(sent_north, "lat", 1)
    north = ring(sent_south, "lat", -1)
    halo_west = ring(sent_east, "lon", 1)
    halo_east = ring(sent_west, "lon", -1)
    row = ring(coef[LAT_C : LAT_G + 1, 0:1], "lat", -1)

    edge = jnp.zeros((1,), F32)
    mixing = jnp.concatenate([vertical_mixing, edge])
    ones = jnp.ones((PIECE,), F32)
    par = jnp.stack(
        [
            jnp.tile(level_light, 2),
            jnp.tile(mixing, 2),
            ones * (lat > 0).astype(F32),
            ones * (lat < lat_count - 1).astype(F32),
        ]
    )
    loss = jnp.broadcast_to(self_loss[:, None], (species, PIECE))
    rates = (night_rates, photo_rates)

    mid, done = call(
        inner_kernel,
        [(rows, species, inner), (rows - 4, species, inner)],
        [WHOLE] * 6,
        tracers,
        coef,
        par,
        loss,
        *rates,
    )
    mid_side, side_south, side_north, side = call(
        side_kernel,
        [(rows, species, 2 * two), (2 * species + 8, 2 * two), (2 * species, 2 * two), (6, rows, 2 * two)],
        [WHOLE] * 5,
        sent_west,
        sent_east,
        halo_west,
        halo_east,
        coef,
    )
    side_from_south = ring(side_north, "lat", 1)
    side_from_north = ring(side_south, "lat", -1)
    sent_south, sent_north, swept = call(
        edge_kernel,
        [(2, species, width), (2, species, width), (rows, species, width)],
        [WHOLE] * 14,
        mid,
        south,
        north,
        done,
        mid_side,
        side_from_south,
        side_from_north,
        coef,
        side,
        row,
        par,
        loss,
        *rates,
        scratch=[pltpu.VMEM((rows, species, width + two), F32)],
    )
    south = ring(sent_north, "lat", 1)
    north = ring(sent_south, "lat", -1)
    (out,) = call(
        last_kernel, [(species, rows, width)], [WHOLE] * 6, swept, south, north, coef, row, par
    )
    return out


def solution(mesh):
    in_specs = (
        P(None, "lat", "lon"),
        P(None, "lat", "lon"),
        P(None, "lat", "lon"),
        P("lat", "lon"),
        P("lat", "lon"),
        P(),
        P(),
        P(),
        P(),
        P(),
    )
    out_specs = P(None, "lat", "lon")
    return jax.shard_map(shards, mesh=mesh, in_specs=in_specs, out_specs=out_specs, check_vma=False)
```

```python
import jax
import jax.numpy as jnp
from jax import lax
from jax.experimental import pallas as pl
from jax.experimental.pallas import tpu as pltpu
from jax.sharding import PartitionSpec as P

CHEM = 6
KMAX = 8
PIECE = 128
HALF = 64
LEVELS = 64
VMEM_LIMIT = 24 * 1024 * 1024
F32 = jnp.float32
BF16 = jnp.bfloat16
LON_C, LON_G, LAT_C, LAT_G, DAY, COUNT = range(6)


def ring(value, axis, steps):
    count = lax.axis_size(axis)
    return lax.ppermute(value, axis, [(i, (i + steps) % count) for i in range(count)])


def half_roll(value):
    return pltpu.roll(value, HALF, 1)


def minmod(x, y):
    return jnp.minimum(jnp.maximum(x, jnp.minimum(y, 0.0)), jnp.maximum(y, 0.0))


def gain(cour, switch):
    return 0.5 * cour * switch * jnp.where(cour >= 0.0, 1.0 - cour, -1.0 - cour)


def lon_sweep(cells, cours, gains):
    n = len(cells)
    low = lax.broadcasted_iota(jnp.int32, cells[0].shape, 1) < HALF
    turned = [half_roll(q) for q in cells]
    flux = [None]
    for i in range(1, n):
        west = jnp.where(low, turned[i - 1], turned[i])
        east = jnp.where(low, turned[i], turned[i + 1]) if i < n - 1 else turned[i]
        step = cells[i] - west
        slope = minmod(step, east - cells[i])
        behind = minmod(west - cells[i - 1], step)
        forward = cours[i - 1] >= 0.0
        flux.append(
            cours[i - 1] * jnp.where(forward, west, cells[i])
            + gains[i - 1] * jnp.where(forward, behind, slope)
        )
    turned = [None] + [half_roll(f) for f in flux[1:]]
    return [
        cells[i] - (jnp.where(low, turned[i], turned[i + 1]) - flux[i]) for i in range(1, n - 1)
    ]


def lat_sweep(rows, cours, gains):
    n = len(rows) - 4
    step = [rows[i + 1] - rows[i] for i in range(n + 3)]
    slope = [minmod(step[i], step[i + 1]) for i in range(n + 2)]
    flux = []
    for i in range(n + 1):
        forward = cours[i] >= 0.0
        flux.append(
            cours[i] * jnp.where(forward, rows[i + 1], rows[i + 2])
            + gains[i] * jnp.where(forward, slope[i], slope[i + 1])
        )
    return [rows[i + 2] - (flux[i + 1] - flux[i]) for i in range(n)]


def expand(compact, first):
    rows = compact.shape[0]
    low = lax.broadcasted_iota(jnp.int32, (rows, PIECE), 1) < HALF
    left = jnp.broadcast_to(compact[:, first : first + 1], (rows, PIECE))
    right = jnp.broadcast_to(compact[:, first + 1 : first + 2], (rows, PIECE))
    return jnp.where(low, left, right)


def rate_pieces(night_ref, photo_ref):
    rates = jnp.concatenate([night_ref[...], photo_ref[...]], 0)
    high = rates.astype(BF16)
    low = (rates - high.astype(F32)).astype(BF16)
    return jnp.concatenate([high, high, low], 1)


def react(rows, suns, rates, loss):
    species = rows[0].shape[0]
    for _ in range(CHEM):
        nexts = []
        for q, sun in zip(rows, suns):
            high = q.astype(BF16)
            low = (q - high.astype(F32)).astype(BF16)
            both = jnp.dot(
                rates, jnp.concatenate([high, low, high], 0), preferred_element_type=F32
            )
            top = q + both[:species] + sun * both[species:]
            bottom = 1.0 + loss * q * q
            inverse = pl.reciprocal(bottom, approx=True)
            inverse = inverse * (2.0 - bottom * inverse)
            nexts.append(top * inverse)
        rows = nexts
    return rows


def fill_table(mixing, table_ref):
    shape = (HALF, PIECE)
    lane = lax.broadcasted_iota(jnp.int32, shape, 1)
    low = lane < HALF
    q = jnp.where((lane & (HALF - 1)) == lax.broadcasted_iota(jnp.int32, shape, 0), 1.0, 0.0)
    for n in range(KMAX):
        flux = mixing * (pltpu.roll(q, PIECE - 1, 1) - q)
        q = q + flux - pltpu.roll(flux, 1, 1)
        high = q.astype(BF16).astype(F32)
        for i, term in enumerate((high, q - high)):
            table_ref[0, n, i] = jnp.where(low, term, 0.0).astype(BF16)
            table_ref[1, n, i] = jnp.where(low, 0.0, term).astype(BF16)


def diffuse(q, first, second, table_ref):
    species = q.shape[0]
    high = q.astype(BF16)
    low = (q - high.astype(F32)).astype(BF16)
    state = jnp.concatenate(
        [jnp.concatenate([high, high], 1), jnp.concatenate([low, low], 1)], 0
    )
    powers = jnp.concatenate(
        [table_ref[0, first - 1, i] if side == 0 else table_ref[1, second - 1, i] for i in (0, 1) for side in (0, 1)], 0
    )
    both = jnp.dot(state, powers, preferred_element_type=F32)
    return both[:species] + both[species:]


def column_block(rows, days, counts, rates, loss, level, table_ref):
    pieces = rows[0].shape[1] // PIECE
    level = jnp.concatenate([level] * pieces, 1)
    loss = jnp.concatenate([loss] * pieces, 1)
    rows = react(rows, [day * level for day in days], rates, loss)
    return [
        [
            diffuse(q[:, j * PIECE : (j + 1) * PIECE], counts(i, 2 * j), counts(i, 2 * j + 1), table_ref)
            for j in range(pieces)
        ]
        for i, q in enumerate(rows)
    ]


WHOLE = pl.BlockSpec(memory_space=pltpu.VMEM)
SCALARS = pl.BlockSpec(memory_space=pltpu.SMEM)
FAR = pl.BlockSpec(memory_space=pl.ANY)
BLOCK = 4 * PIECE


def call(kernel, outs, ins, *args, scratch=(), out_specs=None, cost=10.0):
    return pl.pallas_call(
        kernel,
        out_shape=[s if isinstance(s, jax.ShapeDtypeStruct) else jax.ShapeDtypeStruct(s, F32) for s in outs],
        in_specs=ins,
        out_specs=out_specs or [WHOLE] * len(outs),
        scratch_shapes=list(scratch),
        compiler_params=pltpu.CompilerParams(vmem_limit_bytes=VMEM_LIMIT),
        cost_estimate=pl.CostEstimate(flops=0, bytes_accessed=int(cost * 3.0e6), transcendentals=0),
    )(*args)


def lanes_of(j, count=1):
    return slice(j * PIECE, (j + count) * PIECE)


def blocks(width, body):
    full = width // BLOCK

    def step(b, carry):
        body(pl.multiple_of(b * BLOCK, BLOCK), BLOCK)
        return carry

    if full:
        lax.fori_loop(0, full, step, 0)
    if width % BLOCK:
        body(full * BLOCK, width % BLOCK)


def tiles(species, body):
    def step(s, carry):
        body(pl.ds(pl.multiple_of(s * 8, 8), 8))
        return carry

    lax.fori_loop(0, species // 8, step, 0)


def wide(row, lanes):
    return jnp.concatenate([row] * (lanes // PIECE), 1)


def first_kernel(
    x_ref, cour_in, sw_in, day_in, cnt_in,
    xt_ref, south_ref, north_ref, west_ref, east_ref, coef_ref, row_ref,
    cour_ref, sw_ref, day_ref, cnt_ref, row_sems, sems,
):
    rows, species, width = xt_ref.shape
    pieces = width // PIECE
    edge = (0, 1, rows - 2, rows - 1)
    small = [
        pltpu.make_async_copy(a, b, sems.at[i])
        for i, (a, b) in enumerate(((cour_in, cour_ref), (sw_in, sw_ref), (day_in, day_ref), (cnt_in, cnt_ref)))
    ]
    big = [pltpu.make_async_copy(x_ref.at[:, r, :], xt_ref.at[r], row_sems.at[r]) for r in range(rows)]
    for copy in small:
        copy.start()
    for r in edge + tuple(range(2, rows - 2)):
        big[r].start()
    for copy in small:
        copy.wait()
    cour = [cour_ref[0], cour_ref[1]]
    switch = [sw_ref[0].astype(F32), sw_ref[1].astype(F32)]
    fields = [
        cour[0],
        gain(cour[0], switch[0]),
        cour[1],
        gain(cour[1], switch[1]),
        day_ref[...].astype(F32),
        cnt_ref[...].astype(F32),
    ]
    for i, field in enumerate(fields):
        for j in range(pieces):
            coef_ref[i, :, lanes_of(j)] = expand(field, 2 * j)
    row_ref[0:8] = coef_ref[LAT_C]
    row_ref[8:16] = coef_ref[LAT_G]
    for r in edge:
        big[r].wait()

    def tile(block):
        for r in edge:
            cells = [xt_ref[r, block, lanes_of(j)] for j in range(pieces)]
            faces = [
                [coef_ref[i, r : r + 1, lanes_of(j)] for j in range(1, pieces)] for i in (LON_C, LON_G)
            ]
            ref, row = (south_ref, r) if r < 2 else (north_ref, r - rows + 2)
            for j, value in enumerate(lon_sweep(cells, *faces)):
                ref[row, block, lanes_of(j)] = value

    tiles(species, tile)
    for r in range(2, rows - 2):
        big[r].wait()
    for ref, j in ((west_ref, 0), (east_ref, pieces - 2)):
        for r in range(rows):
            ref[r * species : (r + 1) * species] = xt_ref[r, :, lanes_of(j, 2)]
        for i in range(6):
            at = rows * species + i * rows
            ref[at : at + rows] = coef_ref[i, :, lanes_of(j, 2)]


def inner_kernel(
    xt_ref, south_ref, north_ref, coef_ref, par_ref, loss_ref, night_ref, photo_ref, cnt_ref,
    mid_ref, done_ref, table_ref,
):
    rows, species, width = xt_ref.shape
    pieces = width // PIECE
    inner = range(2, rows - 2)

    def tile(block):
        for r in inner:
            cells = [xt_ref[r, block, lanes_of(j)] for j in range(pieces)]
            faces = [
                [coef_ref[i, r : r + 1, lanes_of(j)] for j in range(1, pieces)] for i in (LON_C, LON_G)
            ]
            for j, value in enumerate(lon_sweep(cells, *faces)):
                mid_ref[r - 2, block, lanes_of(j)] = value

    tiles(species, tile)
    fill_table(par_ref[1:2], table_ref)
    rates = rate_pieces(night_ref, photo_ref)

    def block(at, lanes):
        here = pl.ds(at, lanes)
        own = pl.ds(at + PIECE if isinstance(at, int) else pl.multiple_of(at + PIECE, PIECE), lanes)
        column = 2 + at // LEVELS
        cells = (
            [south_ref[i, :, here] for i in (0, 1)]
            + [mid_ref[i, :, here] for i in range(rows - 4)]
            + [north_ref[i, :, here] for i in (0, 1)]
        )
        faces = [[coef_ref[i, f : f + 1, own] for f in range(2, rows - 1)] for i in (LAT_C, LAT_G)]
        done = column_block(
            lat_sweep(cells, *faces),
            [coef_ref[DAY, r : r + 1, own] for r in inner],
            lambda i, j: cnt_ref[2 + i, column + j],
            rates,
            loss_ref[...],
            par_ref[0:1],
            table_ref,
        )
        for i, row in enumerate(done):
            done_ref[i, :, here] = jnp.concatenate(row, 1)

    blocks(width - 2 * PIECE, block)


def side_kernel(
    done_ref, xw_ref, xe_ref, hw_ref, he_ref, coef_ref, mid_ref, south_ref, north_ref, side_ref
):
    rows, species = mid_ref.shape[:2]
    width = coef_ref.shape[2]
    base = rows * species
    for i in range(6):
        here = slice(base + i * rows, base + (i + 1) * rows)
        side_ref[i, :, lanes_of(0)] = hw_ref[here, lanes_of(1)]
        side_ref[i, :, lanes_of(1)] = coef_ref[i, :, 0:PIECE]
        side_ref[i, :, lanes_of(2)] = coef_ref[i, :, width - PIECE : width]
        side_ref[i, :, lanes_of(3)] = he_ref[here, lanes_of(0)]

    def tile(s, carry):
        for r in range(rows):
            row = slice(r, r + 1)
            from_row = pl.ds(pl.multiple_of(r * species + s * 8, 8), 8)
            block = pl.ds(pl.multiple_of(s * 8, 8), 8)
            faces = [
                [side_ref[i, row, lanes_of(0)], side_ref[i, row, lanes_of(1)], coef_ref[i, row, lanes_of(1)]]
                for i in (LON_C, LON_G)
            ]
            out = lon_sweep([ref[from_row, lanes_of(h)] for ref in (hw_ref, xw_ref) for h in (0, 1)], *faces)
            faces = [
                [
                    side_ref[i, row, lanes_of(2)],
                    side_ref[i, row, lanes_of(3)],
                    he_ref[base + i * rows + r : base + i * rows + r + 1, lanes_of(1)],
                ]
                for i in (LON_C, LON_G)
            ]
            out = out + lon_sweep([ref[from_row, lanes_of(h)] for ref in (xe_ref, he_ref) for h in (0, 1)], *faces)
            for j, value in enumerate(out):
                mid_ref[r, block, lanes_of(j)] = value
                if r < 2:
                    south_ref[pl.ds(pl.multiple_of(r * species + s * 8, 8), 8), lanes_of(j)] = value
                if r >= rows - 2:
                    north_ref[pl.ds(pl.multiple_of((r - rows + 2) * species + s * 8, 8), 8), lanes_of(j)] = value
        return carry

    lax.fori_loop(0, species // 8, tile, 0)
    for j in range(4):
        two = [side_ref[i, 0:1, lanes_of(j)] for i in (LAT_C, LAT_G)]
        south_ref[2 * species : 2 * species + 8, lanes_of(j)] = jnp.concatenate([two[0]] * 4 + [two[1]] * 4, 0)


def edge_kernel(
    mid_ref, own_south_ref, own_north_ref, south_ref, north_ref, coef_ref, row_ref,
    par_ref, loss_ref, night_ref, photo_ref, table_ref, cnt_ref,
    done_ref, sent_south_ref, sent_north_ref,
):
    species, inner_width = mid_ref.shape[1:]
    rows = coef_ref.shape[1]
    rates = rate_pieces(night_ref, photo_ref)
    edge = (0, 1, rows - 2, rows - 1)

    def block(at, lanes):
        here = pl.ds(at, lanes)
        own = pl.ds(at + PIECE if isinstance(at, int) else pl.multiple_of(at + PIECE, PIECE), lanes)
        column = 2 + at // LEVELS
        valid_south, valid_north = wide(par_ref[2:3], lanes), wide(par_ref[3:4], lanes)
        lower = (
            [south_ref[i, :, here] * valid_south for i in (0, 1)]
            + [own_south_ref[i, :, here] for i in (0, 1)]
            + [mid_ref[i, :, here] for i in (0, 1)]
        )
        upper = (
            [mid_ref[i, :, here] for i in (2, 3)]
            + [own_north_ref[i, :, here] for i in (0, 1)]
            + [north_ref[i, :, here] * valid_north for i in (0, 1)]
        )
        lower_faces = [
            [coef_ref[i, 0:1, own] * valid_south, coef_ref[i, 1:2, own], coef_ref[i, 2:3, own]]
            for i in (LAT_C, LAT_G)
        ]
        upper_faces = [
            [
                coef_ref[i, rows - 2 : rows - 1, own],
                coef_ref[i, rows - 1 : rows, own],
                row_ref[8 * (i - LAT_C) : 8 * (i - LAT_C) + 1, own] * valid_north,
            ]
            for i in (LAT_C, LAT_G)
        ]
        done = column_block(
            lat_sweep(lower, *lower_faces) + lat_sweep(upper, *upper_faces),
            [coef_ref[DAY, r : r + 1, own] for r in edge],
            lambda i, j: cnt_ref[edge[i], column + j],
            rates,
            loss_ref[...],
            par_ref[0:1],
            table_ref,
        )
        for i, row in enumerate(done):
            done_ref[i, :, here] = jnp.concatenate(row, 1)

    blocks(inner_width, block)
    pieces = inner_width // PIECE

    def tile(block):
        for k, r in enumerate(edge):
            cells = [done_ref[k, block, lanes_of(j)] for j in range(pieces)]
            faces = [
                [coef_ref[i, r : r + 1, lanes_of(j + 1)] for j in range(1, pieces)] for i in (LON_C, LON_G)
            ]
            ref = sent_south_ref if k < 2 else sent_north_ref
            for j, value in enumerate(lon_sweep(cells, *faces)):
                ref[k % 2, block, lanes_of(j)] = value

    tiles(species, tile)


def corner_kernel(
    mid_ref, south_ref, north_ref, edge_ref, coef_ref, side_ref,
    par_ref, loss_ref, night_ref, photo_ref, table_ref, cnt_ref,
    done_ref, sent_south_ref, sent_north_ref,
):
    rows, species, width = mid_ref.shape
    rates = rate_pieces(night_ref, photo_ref)
    valid_south, valid_north = wide(par_ref[2:3], width), wide(par_ref[3:4], width)
    cells = (
        [south_ref[i * species : (i + 1) * species] * valid_south for i in (0, 1)]
        + [mid_ref[r] for r in range(rows)]
        + [north_ref[i * species : (i + 1) * species] * valid_north for i in (0, 1)]
    )
    faces = [
        [side_ref[i, 0:1] * valid_south]
        + [side_ref[i, r : r + 1] for r in range(1, rows)]
        + [north_ref[2 * species + 4 * (i - LAT_C) : 2 * species + 4 * (i - LAT_C) + 1] * valid_north]
        for i in (LAT_C, LAT_G)
    ]
    for r, q in enumerate(lat_sweep(cells, *faces)):
        done_ref[r] = q
    for part in (0, rows // 2):
        done = column_block(
            [done_ref[part + i] for i in range(rows // 2)],
            [side_ref[DAY, part + i : part + i + 1] for i in range(rows // 2)],
            lambda i, j: cnt_ref[part + i, j],
            rates,
            loss_ref[...],
            par_ref[0:1],
            table_ref,
        )
        for i, row in enumerate(done):
            done_ref[part + i] = jnp.concatenate(row, 1)
    last = edge_ref.shape[2] // PIECE
    total = coef_ref.shape[2] // PIECE

    def tile(block):
        for k, r in enumerate((0, 1, rows - 2, rows - 1)):
            row = slice(r, r + 1)
            ref = sent_south_ref if k < 2 else sent_north_ref
            cells = [done_ref[r, block, lanes_of(j)] for j in (0, 1)] + [
                edge_ref[k, block, lanes_of(j)] for j in (0, 1)
            ]
            faces = [[coef_ref[i, row, lanes_of(j)] for j in range(3)] for i in (LON_C, LON_G)]
            out = lon_sweep(cells, *faces)
            cells = [edge_ref[k, block, lanes_of(j)] for j in (last - 2, last - 1)] + [
                done_ref[r, block, lanes_of(j)] for j in (2, 3)
            ]
            faces = [
                [coef_ref[i, row, lanes_of(j)] for j in (total - 2, total - 1)] + [side_ref[i, row, lanes_of(3)]]
                for i in (LON_C, LON_G)
            ]
            for j, value in enumerate(out + lon_sweep(cells, *faces)):
                ref[k % 2, block, lanes_of(j)] = value

    tiles(species, tile)


def rest_kernel(
    done_ref, corner_ref, south_a_ref, north_a_ref, south_c_ref, north_c_ref, coef_ref, side_ref, swept_ref, out_ref
):
    count, species = done_ref.shape[:2]
    width = coef_ref.shape[2]
    pieces = width // PIECE

    def tile(block):
        for k in range(count):
            row = slice(k + 2, k + 3)
            cells = (
                [corner_ref[k + 2, block, lanes_of(j)] for j in (0, 1)]
                + [done_ref[k, block, lanes_of(j)] for j in range(pieces - 2)]
                + [corner_ref[k + 2, block, lanes_of(j)] for j in (2, 3)]
            )
            faces = [
                [coef_ref[i, row, lanes_of(j)] for j in range(pieces)] + [side_ref[i, row, lanes_of(3)]]
                for i in (LON_C, LON_G)
            ]
            for j, value in enumerate(lon_sweep(cells, *faces)):
                swept_ref[k, block, lanes_of(j)] = value

    tiles(species, tile)

    for j in range(pieces):
        own = lanes_of(j)
        (a, c), at = join(j, pieces)
        south, north = ((south_c_ref, north_c_ref) if c else (south_a_ref, north_a_ref))
        cells = (
            [south[i, :, at] for i in (0, 1)]
            + [swept_ref[i, :, own] for i in range(count)]
            + [north[i, :, at] for i in (0, 1)]
        )
        faces = [[coef_ref[i, f : f + 1, own] for f in range(2, count + 3)] for i in (LAT_C, LAT_G)]
        for i, q in enumerate(lat_sweep(cells, *faces)):
            out_ref[i, :, own] = q


def join(j, pieces):
    if 2 <= j < pieces - 2:
        return (True, False), lanes_of(j - 2)
    return (False, True), lanes_of(j if j < 2 else j - pieces + 4)


def last_kernel(
    inner_ref, swept_ref, own_south_a, own_north_a, own_south_c, own_north_c,
    south_a, north_a, south_c, north_c, coef_ref, row_ref, par_ref,
    out_ref, edge_ref, sems,
):
    count, species, width = inner_ref.shape
    rows = count + 4
    pieces = width // PIECE
    edge = (0, 1, rows - 2, rows - 1)
    copies = [
        pltpu.make_async_copy(inner_ref.at[i], out_ref.at[:, i + 2, :], sems.at[i]) for i in range(count)
    ]
    for copy in copies:
        copy.start()
    valid_south, valid_north = par_ref[2:3], par_ref[3:4]
    for j in range(pieces):
        own = lanes_of(j)
        (_, c), at = join(j, pieces)
        south, own_south, own_north, north = (
            (south_c, own_south_c, own_north_c, north_c) if c else (south_a, own_south_a, own_north_a, north_a)
        )
        lower = (
            [south[i, :, at] * valid_south for i in (0, 1)]
            + [own_south[i, :, at] for i in (0, 1)]
            + [swept_ref[i, :, own] for i in (0, 1)]
        )
        upper = (
            [swept_ref[i, :, own] for i in (2, 3)]
            + [own_north[i, :, at] for i in (0, 1)]
            + [north[i, :, at] * valid_north for i in (0, 1)]
        )
        lower_faces = [
            [coef_ref[i, 0:1, own] * valid_south, coef_ref[i, 1:2, own], coef_ref[i, 2:3, own]]
            for i in (LAT_C, LAT_G)
        ]
        upper_faces = [
            [
                coef_ref[i, rows - 2 : rows - 1, own],
                coef_ref[i, rows - 1 : rows, own],
                row_ref[8 * (i - LAT_C) : 8 * (i - LAT_C) + 1, own] * valid_north,
            ]
            for i in (LAT_C, LAT_G)
        ]
        for k, q in enumerate(lat_sweep(lower, *lower_faces) + lat_sweep(upper, *upper_faces)):
            edge_ref[k, :, own] = q
    more = [
        pltpu.make_async_copy(edge_ref.at[k], out_ref.at[:, r, :], sems.at[count + k]) for k, r in enumerate(edge)
    ]
    for copy in more:
        copy.start()
    for copy in copies + more:
        copy.wait()


def shards(
    tracers,
    courant,
    switches,
    day_flags,
    diffusion_counts,
    night_rates,
    photo_rates,
    level_light,
    self_loss,
    vertical_mixing,
):
    species, rows, width = tracers.shape
    inner = width - 2 * PIECE
    lat_count = lax.axis_size("lat")
    lat = lax.axis_index("lat")
    two = 2 * PIECE
    four = 4 * PIECE
    message = (rows * species + 6 * rows, two)

    xt, own_south, own_north, west, east, coef, own_row = call(
        first_kernel,
        [(rows, species, width), (2, species, inner), (2, species, inner), message, message, (6, rows, width), (16, width)],
        [FAR] * 5,
        tracers,
        courant,
        switches,
        day_flags,
        diffusion_counts,
        scratch=[
            pltpu.VMEM(courant.shape, F32),
            pltpu.VMEM(switches.shape, jnp.int32),
            pltpu.VMEM(day_flags.shape, jnp.int32),
            pltpu.VMEM(diffusion_counts.shape, jnp.int32),
            pltpu.SemaphoreType.DMA((rows,)),
            pltpu.SemaphoreType.DMA((4,)),
        ],
        cost=3,
    )
    south = ring(own_north, "lat", 1)
    north = ring(own_south, "lat", -1)
    halo_west = ring(east, "lon", 1)
    halo_east = ring(west, "lon", -1)
    row = ring(own_row, "lat", -1)

    edge = jnp.zeros((1,), F32)
    mixing = jnp.concatenate([vertical_mixing, edge])
    ones = jnp.ones((PIECE,), F32)
    par = jnp.stack(
        [
            jnp.tile(level_light, 2),
            jnp.tile(mixing, 2),
            ones * (lat > 0).astype(F32),
            ones * (lat < lat_count - 1).astype(F32),
        ]
    )
    loss = jnp.broadcast_to(self_loss[:, None], (species, PIECE))
    chem = (par, loss, night_rates, photo_rates)

    mid, done, table = call(
        inner_kernel,
        [
            (rows - 4, species, inner),
            (rows - 4, species, inner),
            jax.ShapeDtypeStruct((2, KMAX, 2, HALF, PIECE), BF16),
        ],
        [WHOLE] * 8 + [SCALARS],
        xt,
        own_south,
        own_north,
        coef,
        *chem,
        diffusion_counts,
        cost=9,
    )
    mid_side, side_south, side_north, side = call(
        side_kernel,
        [(rows, species, four), (2 * species + 8, four), (2 * species, four), (6, rows, four)],
        [pl.BlockSpec(memory_space=pl.ANY)] + [WHOLE] * 5,
        done,
        west,
        east,
        halo_west,
        halo_east,
        coef,
        cost=3,
    )
    counts = side[COUNT][:, ::LEVELS].astype(jnp.int32)
    side_from_south = ring(side_north, "lat", 1)
    side_from_north = ring(side_south, "lat", -1)
    edge_done, main_south, main_north = call(
        edge_kernel,
        [(4, species, inner), (2, species, inner - two), (2, species, inner - two)],
        [WHOLE] * 12 + [SCALARS],
        mid,
        own_south,
        own_north,
        south,
        north,
        coef,
        row,
        *chem,
        table,
        diffusion_counts,
        cost=9,
    )
    main_from_south = ring(main_north, "lat", 1)
    main_from_north = ring(main_south, "lat", -1)
    corner, corner_south, corner_north = call(
        corner_kernel,
        [(rows, species, four), (2, species, four), (2, species, four)],
        [WHOLE] * 11 + [SCALARS],
        mid_side,
        side_from_south,
        side_from_north,
        edge_done,
        coef,
        side,
        *chem,
        table,
        counts,
        cost=5,
    )
    corner_from_south = ring(corner_north, "lat", 1)
    corner_from_north = ring(corner_south, "lat", -1)
    swept, inner_out = call(
        rest_kernel,
        [(rows - 4, species, width), (rows - 4, species, width)],
        [WHOLE] * 8,
        done,
        corner,
        main_south,
        main_north,
        corner_south,
        corner_north,
        coef,
        side,
        cost=4,
    )
    (out,) = call(
        last_kernel,
        [(species, rows, width)],
        [WHOLE] * 13,
        inner_out,
        swept,
        main_south,
        main_north,
        corner_south,
        corner_north,
        main_from_south,
        main_from_north,
        corner_from_south,
        corner_from_north,
        coef,
        row,
        par,
        scratch=[pltpu.VMEM((4, species, width), F32), pltpu.SemaphoreType.DMA((rows,))],
        out_specs=[FAR],
        cost=3,
    )
    return out


def solution(mesh):
    in_specs = (
        P(None, "lat", "lon"),
        P(None, "lat", "lon"),
        P(None, "lat", "lon"),
        P("lat", "lon"),
        P("lat", "lon"),
        P(),
        P(),
        P(),
        P(),
        P(),
    )
    out_specs = P(None, "lat", "lon")
    return jax.shard_map(shards, mesh=mesh, in_specs=in_specs, out_specs=out_specs, check_vma=False)
```

```python
import jax
import jax.numpy as jnp
from jax import lax
from jax.experimental import pallas as pl
from jax.experimental.pallas import tpu as pltpu
from jax.sharding import PartitionSpec as P

CHEM = 6
KMAX = 8
PIECE = 128
HALF = 64
LEVELS = 64
VMEM_LIMIT = 24 * 1024 * 1024
VMEM_ALL = 60 * 1024 * 1024
F32 = jnp.float32
BF16 = jnp.bfloat16
LON_C, LON_G, LAT_C, LAT_G, DAY, COUNT = range(6)


def ring(value, axis, steps):
    count = lax.axis_size(axis)
    return lax.ppermute(value, axis, [(i, (i + steps) % count) for i in range(count)])


def half_roll(value):
    return pltpu.roll(value, HALF, 1)


def minmod(x, y):
    return jnp.minimum(jnp.maximum(x, jnp.minimum(y, 0.0)), jnp.maximum(y, 0.0))


def gain(cour, switch):
    return 0.5 * cour * switch * jnp.where(cour >= 0.0, 1.0 - cour, -1.0 - cour)


def lon_sweep(cells, cours, gains):
    n = len(cells)
    low = lax.broadcasted_iota(jnp.int32, cells[0].shape, 1) < HALF
    turned = [half_roll(q) for q in cells]
    flux = [None]
    for i in range(1, n):
        west = jnp.where(low, turned[i - 1], turned[i])
        east = jnp.where(low, turned[i], turned[i + 1]) if i < n - 1 else turned[i]
        step = cells[i] - west
        slope = minmod(step, east - cells[i])
        behind = minmod(west - cells[i - 1], step)
        forward = cours[i - 1] >= 0.0
        flux.append(
            cours[i - 1] * jnp.where(forward, west, cells[i])
            + gains[i - 1] * jnp.where(forward, behind, slope)
        )
    turned = [None] + [half_roll(f) for f in flux[1:]]
    return [
        cells[i] - (jnp.where(low, turned[i], turned[i + 1]) - flux[i]) for i in range(1, n - 1)
    ]


def lat_sweep(rows, cours, gains):
    n = len(rows) - 4
    step = [rows[i + 1] - rows[i] for i in range(n + 3)]
    slope = [minmod(step[i], step[i + 1]) for i in range(n + 2)]
    flux = []
    for i in range(n + 1):
        forward = cours[i] >= 0.0
        flux.append(
            cours[i] * jnp.where(forward, rows[i + 1], rows[i + 2])
            + gains[i] * jnp.where(forward, slope[i], slope[i + 1])
        )
    return [rows[i + 2] - (flux[i + 1] - flux[i]) for i in range(n)]


def expand(compact, first):
    rows = compact.shape[0]
    low = lax.broadcasted_iota(jnp.int32, (rows, PIECE), 1) < HALF
    left = jnp.broadcast_to(compact[:, first : first + 1], (rows, PIECE))
    right = jnp.broadcast_to(compact[:, first + 1 : first + 2], (rows, PIECE))
    return jnp.where(low, left, right)


def rate_pieces(chem_ref, species):
    rates = chem_ref[0 : 2 * species, 0:species]
    high = rates.astype(BF16)
    low = (rates - high.astype(F32)).astype(BF16)
    return jnp.concatenate([high, high, low], 1)


def react(rows, suns, rates, loss):
    species = rows[0].shape[0]
    for _ in range(CHEM):
        nexts = []
        for q, sun in zip(rows, suns):
            high = q.astype(BF16)
            low = (q - high.astype(F32)).astype(BF16)
            both = jnp.dot(
                rates, jnp.concatenate([high, low, high], 0), preferred_element_type=F32
            )
            top = q + both[:species] + sun * both[species:]
            bottom = 1.0 + loss * q * q
            inverse = pl.reciprocal(bottom, approx=True)
            inverse = inverse * (2.0 - bottom * inverse)
            nexts.append(top * inverse)
        rows = nexts
    return rows


def fill_table(mixing, table_ref):
    shape = (HALF, PIECE)
    lane = lax.broadcasted_iota(jnp.int32, shape, 1)
    low = lane < HALF
    q = jnp.where((lane & (HALF - 1)) == lax.broadcasted_iota(jnp.int32, shape, 0), 1.0, 0.0)
    for n in range(KMAX):
        flux = mixing * (pltpu.roll(q, PIECE - 1, 1) - q)
        q = q + flux - pltpu.roll(flux, 1, 1)
        high = q.astype(BF16).astype(F32)
        for i, term in enumerate((high, q - high)):
            table_ref[0, n, i] = jnp.where(low, term, 0.0).astype(BF16)
            table_ref[1, n, i] = jnp.where(low, 0.0, term).astype(BF16)


def diffuse(q, first, second, table_ref):
    species = q.shape[0]
    high = q.astype(BF16)
    low = (q - high.astype(F32)).astype(BF16)
    state = jnp.concatenate(
        [jnp.concatenate([high, high], 1), jnp.concatenate([low, low], 1)], 0
    )
    powers = jnp.concatenate(
        [table_ref[0, first - 1, i] if side == 0 else table_ref[1, second - 1, i] for i in (0, 1) for side in (0, 1)], 0
    )
    both = jnp.dot(state, powers, preferred_element_type=F32)
    return both[:species] + both[species:]


def column_block(rows, days, counts, rates, loss, level, table_ref):
    pieces = rows[0].shape[1] // PIECE
    level = jnp.concatenate([level] * pieces, 1)
    loss = jnp.concatenate([loss] * pieces, 1)
    rows = react(rows, [day * level for day in days], rates, loss)
    return [
        [
            diffuse(q[:, j * PIECE : (j + 1) * PIECE], counts(i, 2 * j), counts(i, 2 * j + 1), table_ref)
            for j in range(pieces)
        ]
        for i, q in enumerate(rows)
    ]


WHOLE = pl.BlockSpec(memory_space=pltpu.VMEM)
SCALARS = pl.BlockSpec(memory_space=pltpu.SMEM)
FAR = pl.BlockSpec(memory_space=pl.ANY)
BLOCK = 4 * PIECE


def call(kernel, outs, ins, *args, scratch=(), out_specs=None, cost=10.0, limit=VMEM_LIMIT):
    return pl.pallas_call(
        kernel,
        out_shape=[s if isinstance(s, jax.ShapeDtypeStruct) else jax.ShapeDtypeStruct(s, F32) for s in outs],
        in_specs=ins,
        out_specs=out_specs or [WHOLE] * len(outs),
        scratch_shapes=list(scratch),
        compiler_params=pltpu.CompilerParams(vmem_limit_bytes=limit),
        cost_estimate=pl.CostEstimate(flops=int(cost * 1.0e9), bytes_accessed=int(cost * 3.0e6), transcendentals=0),
    )(*args)


def lanes_of(j, count=1):
    return slice(j * PIECE, (j + count) * PIECE)


def blocks(width, body):
    full = width // BLOCK

    def step(b, carry):
        body(pl.multiple_of(b * BLOCK, BLOCK), BLOCK)
        return carry

    if full:
        lax.fori_loop(0, full, step, 0)
    if width % BLOCK:
        body(full * BLOCK, width % BLOCK)


def tiles(species, body):
    def step(s, carry):
        body(pl.ds(pl.multiple_of(s * 8, 8), 8))
        return carry

    lax.fori_loop(0, species // 8, step, 0)


def wide(row, lanes):
    return jnp.concatenate([row] * (lanes // PIECE), 1)


def fill_chem(night_ref, photo_ref, level_ref, loss_ref, mixing_ref, chem_ref):
    species = night_ref.shape[0]
    chem_ref[0:species, 0:species] = night_ref[...]
    chem_ref[species : 2 * species, 0:species] = photo_ref[...]
    square = (species, species)
    own = lax.broadcasted_iota(jnp.int32, square, 0) == lax.broadcasted_iota(jnp.int32, square, 1)
    loss = jnp.sum(jnp.where(own, loss_ref[...], 0.0), axis=1, keepdims=True)
    chem_ref[2 * species : 3 * species] = jnp.broadcast_to(loss, (species, PIECE))
    at = 3 * species
    chem_ref[at : at + 8] = jnp.zeros((8, PIECE), F32)
    for i, ref in enumerate((level_ref, mixing_ref)):
        row = slice(at + i, at + i + 1)
        chem_ref[row, 0 : ref.shape[1]] = ref[...]
        low = lax.broadcasted_iota(jnp.int32, (1, PIECE), 1) < HALF
        value = chem_ref[row]
        chem_ref[row] = jnp.where(low, value, half_roll(value))
    lat = lax.axis_index("lat")
    for i, there in ((2, lat > 0), (3, lat < lax.axis_size("lat") - 1)):
        chem_ref[at + i : at + i + 1] = jnp.where(there, 1.0, 0.0) * jnp.ones((1, PIECE), F32)


def first_kernel(
    x_ref, cour_in, sw_in, day_in, cnt_in, night_in, photo_in, level_in, loss_in, mixing_in,
    south_ref, north_ref, west_ref, east_ref, coef_ref, row_ref, chem_ref,
    xt_ref, sides_ref, cour_ref, sw_ref, day_ref, cnt_ref, night_ref, photo_ref, level_ref, loss_ref, mixing_ref,
    row_sems, sems,
):
    rows, species, width = xt_ref.shape
    pieces = width // PIECE
    edge = (0, 1, rows - 2, rows - 1)
    small = [
        pltpu.make_async_copy(a, b, sems.at[i])
        for i, (a, b) in enumerate(
            (
                (cour_in, cour_ref),
                (sw_in, sw_ref),
                (day_in, day_ref),
                (cnt_in, cnt_ref),
                (night_in, night_ref),
                (photo_in, photo_ref),
                (level_in, level_ref),
                (loss_in, loss_ref),
                (mixing_in, mixing_ref),
            )
        )
    ]
    big = {r: pltpu.make_async_copy(x_ref.at[:, r, :], xt_ref.at[r], row_sems.at[r]) for r in edge}
    for j in (0, pieces - 2):
        big[rows + j] = pltpu.make_async_copy(
            x_ref.at[:, :, lanes_of(j, 2)], sides_ref.at[:, :, lanes_of(2 if j else 0, 2)], row_sems.at[4 + (1 if j else 0)]
        )
    for copy in small:
        copy.start()
    for copy in big.values():
        copy.start()
    for copy in small:
        copy.wait()
    cour = [cour_ref[0], cour_ref[1]]
    switch = [sw_ref[0].astype(F32), sw_ref[1].astype(F32)]
    fields = [
        cour[0],
        gain(cour[0], switch[0]),
        cour[1],
        gain(cour[1], switch[1]),
        day_ref[...].astype(F32),
        cnt_ref[...].astype(F32),
    ]
    for i, field in enumerate(fields):
        for j in range(pieces):
            coef_ref[i, :, lanes_of(j)] = expand(field, 2 * j)
    fill_chem(night_ref, photo_ref, level_ref, loss_ref, mixing_ref, chem_ref)
    row_ref[0:8] = coef_ref[LAT_C]
    row_ref[8:16] = coef_ref[LAT_G]
    for r in edge:
        big[r].wait()

    def tile(block):
        for r in edge:
            cells = [xt_ref[r, block, lanes_of(j)] for j in range(pieces)]
            faces = [
                [coef_ref[i, r : r + 1, lanes_of(j)] for j in range(1, pieces)] for i in (LON_C, LON_G)
            ]
            ref, row = (south_ref, r) if r < 2 else (north_ref, r - rows + 2)
            for j, value in enumerate(lon_sweep(cells, *faces)):
                ref[row, block, lanes_of(j)] = value

    tiles(species, tile)
    big[rows].wait()
    big[rows + pieces - 2].wait()
    for ref, j in ((west_ref, 0), (east_ref, pieces - 2)):
        for r in range(rows):
            ref[r * species : (r + 1) * species] = sides_ref[:, r, lanes_of(2 if j else 0, 2)]
        for i in range(6):
            at = rows * species + i * rows
            ref[at : at + rows] = coef_ref[i, :, lanes_of(j, 2)]


def inner_kernel(
    x_ref, south_ref, north_ref, coef_ref, chem_ref, cnt_ref,
    mid_ref, done_ref, table_ref, xt_ref, sems,
):
    species, rows, width = x_ref.shape
    pieces = width // PIECE
    inner = range(2, rows - 2)
    copies = [pltpu.make_async_copy(x_ref.at[:, r, :], xt_ref.at[r - 2], sems.at[r - 2]) for r in inner]
    for copy in copies:
        copy.start()
    fill_table(chem_ref[3 * species + 1 : 3 * species + 2], table_ref)
    for copy in copies:
        copy.wait()

    def tile(block):
        for r in inner:
            cells = [xt_ref[r - 2, block, lanes_of(j)] for j in range(pieces)]
            faces = [
                [coef_ref[i, r : r + 1, lanes_of(j)] for j in range(1, pieces)] for i in (LON_C, LON_G)
            ]
            for j, value in enumerate(lon_sweep(cells, *faces)):
                mid_ref[r - 2, block, lanes_of(j)] = value

    tiles(species, tile)
    rates = rate_pieces(chem_ref, species)

    def block(at, lanes):
        here = pl.ds(at, lanes)
        own = pl.ds(at + PIECE if isinstance(at, int) else pl.multiple_of(at + PIECE, PIECE), lanes)
        column = 2 + at // LEVELS
        cells = (
            [south_ref[i, :, here] for i in (0, 1)]
            + [mid_ref[i, :, here] for i in range(rows - 4)]
            + [north_ref[i, :, here] for i in (0, 1)]
        )
        faces = [[coef_ref[i, f : f + 1, own] for f in range(2, rows - 1)] for i in (LAT_C, LAT_G)]
        done = column_block(
            lat_sweep(cells, *faces),
            [coef_ref[DAY, r : r + 1, own] for r in inner],
            lambda i, j: cnt_ref[2 + i, column + j],
            rates,
            chem_ref[2 * species : 3 * species],
            chem_ref[3 * species + 0 : 3 * species + 1],
            table_ref,
        )
        for i, row in enumerate(done):
            done_ref[i, :, here] = jnp.concatenate(row, 1)

    blocks(width - 2 * PIECE, block)


def side_kernel(
    edge_ref, xw_ref, xe_ref, hw_ref, he_ref, coef_ref, mid_ref, south_ref, north_ref, side_ref, cnt_ref
):
    rows, species = mid_ref.shape[:2]
    width = coef_ref.shape[2]
    base = rows * species
    for i in range(6):
        here = slice(base + i * rows, base + (i + 1) * rows)
        side_ref[i, :, lanes_of(0)] = hw_ref[here, lanes_of(1)]
        side_ref[i, :, lanes_of(1)] = coef_ref[i, :, 0:PIECE]
        side_ref[i, :, lanes_of(2)] = coef_ref[i, :, width - PIECE : width]
        side_ref[i, :, lanes_of(3)] = he_ref[here, lanes_of(0)]

    cnt_ref[...] = side_ref[COUNT].astype(jnp.int32)

    def tile(s, carry):
        for r in range(rows):
            row = slice(r, r + 1)
            from_row = pl.ds(pl.multiple_of(r * species + s * 8, 8), 8)
            block = pl.ds(pl.multiple_of(s * 8, 8), 8)
            faces = [
                [side_ref[i, row, lanes_of(0)], side_ref[i, row, lanes_of(1)], coef_ref[i, row, lanes_of(1)]]
                for i in (LON_C, LON_G)
            ]
            out = lon_sweep([ref[from_row, lanes_of(h)] for ref in (hw_ref, xw_ref) for h in (0, 1)], *faces)
            faces = [
                [
                    side_ref[i, row, lanes_of(2)],
                    side_ref[i, row, lanes_of(3)],
                    he_ref[base + i * rows + r : base + i * rows + r + 1, lanes_of(1)],
                ]
                for i in (LON_C, LON_G)
            ]
            out = out + lon_sweep([ref[from_row, lanes_of(h)] for ref in (xe_ref, he_ref) for h in (0, 1)], *faces)
            for j, value in enumerate(out):
                mid_ref[r, block, lanes_of(j)] = value
                if r < 2:
                    south_ref[pl.ds(pl.multiple_of(r * species + s * 8, 8), 8), lanes_of(j)] = value
                if r >= rows - 2:
                    north_ref[pl.ds(pl.multiple_of((r - rows + 2) * species + s * 8, 8), 8), lanes_of(j)] = value
        return carry

    lax.fori_loop(0, species // 8, tile, 0)
    for j in range(4):
        two = [side_ref[i, 0:1, lanes_of(j)] for i in (LAT_C, LAT_G)]
        south_ref[2 * species : 2 * species + 8, lanes_of(j)] = jnp.concatenate([two[0]] * 4 + [two[1]] * 4, 0)


def edge_kernel(
    mid_ref, own_south_ref, own_north_ref, south_ref, north_ref, coef_ref, row_ref,
    chem_ref, table_ref, cnt_ref,
    done_ref, sent_south_ref, sent_north_ref,
):
    species, inner_width = mid_ref.shape[1:]
    rows = coef_ref.shape[1]
    rates = rate_pieces(chem_ref, species)
    edge = (0, 1, rows - 2, rows - 1)

    def block(at, lanes):
        here = pl.ds(at, lanes)
        own = pl.ds(at + PIECE if isinstance(at, int) else pl.multiple_of(at + PIECE, PIECE), lanes)
        column = 2 + at // LEVELS
        valid_south, valid_north = wide(chem_ref[3 * species + 2 : 3 * species + 3], lanes), wide(chem_ref[3 * species + 3 : 3 * species + 4], lanes)
        lower = (
            [south_ref[i, :, here] * valid_south for i in (0, 1)]
            + [own_south_ref[i, :, here] for i in (0, 1)]
            + [mid_ref[i, :, here] for i in (0, 1)]
        )
        upper = (
            [mid_ref[i, :, here] for i in (2, 3)]
            + [own_north_ref[i, :, here] for i in (0, 1)]
            + [north_ref[i, :, here] * valid_north for i in (0, 1)]
        )
        lower_faces = [
            [coef_ref[i, 0:1, own] * valid_south, coef_ref[i, 1:2, own], coef_ref[i, 2:3, own]]
            for i in (LAT_C, LAT_G)
        ]
        upper_faces = [
            [
                coef_ref[i, rows - 2 : rows - 1, own],
                coef_ref[i, rows - 1 : rows, own],
                row_ref[8 * (i - LAT_C) : 8 * (i - LAT_C) + 1, own] * valid_north,
            ]
            for i in (LAT_C, LAT_G)
        ]
        done = column_block(
            lat_sweep(lower, *lower_faces) + lat_sweep(upper, *upper_faces),
            [coef_ref[DAY, r : r + 1, own] for r in edge],
            lambda i, j: cnt_ref[edge[i], column + j],
            rates,
            chem_ref[2 * species : 3 * species],
            chem_ref[3 * species + 0 : 3 * species + 1],
            table_ref,
        )
        for i, row in enumerate(done):
            done_ref[i, :, here] = jnp.concatenate(row, 1)

    blocks(inner_width, block)
    pieces = inner_width // PIECE

    def tile(block):
        for k, r in enumerate(edge):
            cells = [done_ref[k, block, lanes_of(j)] for j in range(pieces)]
            faces = [
                [coef_ref[i, r : r + 1, lanes_of(j + 1)] for j in range(1, pieces)] for i in (LON_C, LON_G)
            ]
            ref = sent_south_ref if k < 2 else sent_north_ref
            for j, value in enumerate(lon_sweep(cells, *faces)):
                ref[k % 2, block, lanes_of(j)] = value

    tiles(species, tile)


def corner_kernel(
    mid_ref, south_ref, north_ref, edge_ref, coef_ref, side_ref,
    chem_ref, table_ref, cnt_ref,
    done_ref, sent_south_ref, sent_north_ref,
):
    rows, species, width = mid_ref.shape
    rates = rate_pieces(chem_ref, species)
    valid_south, valid_north = wide(chem_ref[3 * species + 2 : 3 * species + 3], width), wide(chem_ref[3 * species + 3 : 3 * species + 4], width)
    cells = (
        [south_ref[i * species : (i + 1) * species] * valid_south for i in (0, 1)]
        + [mid_ref[r] for r in range(rows)]
        + [north_ref[i * species : (i + 1) * species] * valid_north for i in (0, 1)]
    )
    faces = [
        [side_ref[i, 0:1] * valid_south]
        + [side_ref[i, r : r + 1] for r in range(1, rows)]
        + [north_ref[2 * species + 4 * (i - LAT_C) : 2 * species + 4 * (i - LAT_C) + 1] * valid_north]
        for i in (LAT_C, LAT_G)
    ]
    for r, q in enumerate(lat_sweep(cells, *faces)):
        done_ref[r] = q
    for part in (0, rows // 2):
        done = column_block(
            [done_ref[part + i] for i in range(rows // 2)],
            [side_ref[DAY, part + i : part + i + 1] for i in range(rows // 2)],
            lambda i, j: cnt_ref[part + i, LEVELS * j],
            rates,
            chem_ref[2 * species : 3 * species],
            chem_ref[3 * species + 0 : 3 * species + 1],
            table_ref,
        )
        for i, row in enumerate(done):
            done_ref[part + i] = jnp.concatenate(row, 1)
    last = edge_ref.shape[2] // PIECE

    def tile(block):
        for k, r in enumerate((0, 1, rows - 2, rows - 1)):
            row = slice(r, r + 1)
            ref = sent_south_ref if k < 2 else sent_north_ref
            out = corner_sweep(
                [done_ref[r, block, lanes_of(j)] for j in range(4)],
                [edge_ref[k, block, lanes_of(j)] for j in (0, 1, last - 2, last - 1)],
                row,
                coef_ref,
                side_ref,
            )
            for j, value in enumerate(out):
                ref[k % 2, block, lanes_of(j)] = value

    tiles(species, tile)


def rest_kernel(done_ref, south_ref, north_ref, coef_ref, swept_ref, out_ref):
    count, species, width = done_ref.shape
    pieces = width // PIECE

    def tile(block):
        for k in range(count):
            row = slice(k + 2, k + 3)
            cells = [done_ref[k, block, lanes_of(j)] for j in range(pieces)]
            faces = [[coef_ref[i, row, lanes_of(j + 1)] for j in range(1, pieces)] for i in (LON_C, LON_G)]
            for j, value in enumerate(lon_sweep(cells, *faces)):
                swept_ref[k, block, lanes_of(j)] = value

    tiles(species, tile)
    for j in range(pieces - 2):
        inner_lat(swept_ref, south_ref, north_ref, coef_ref, out_ref, j, j + 2)


def inner_lat(swept_ref, south_ref, north_ref, coef_ref, out_ref, j, own):
    count = swept_ref.shape[0]
    at = lanes_of(j)
    cells = (
        [south_ref[i, :, at] for i in (0, 1)]
        + [swept_ref[i, :, at] for i in range(count)]
        + [north_ref[i, :, at] for i in (0, 1)]
    )
    faces = [[coef_ref[i, f : f + 1, lanes_of(own)] for f in range(2, count + 3)] for i in (LAT_C, LAT_G)]
    for i, q in enumerate(lat_sweep(cells, *faces)):
        out_ref[i, :, at] = q


def rest_corner_kernel(done_ref, corner_ref, south_ref, north_ref, coef_ref, side_ref, swept_ref, out_ref):
    count, species, width = done_ref.shape
    last = width // PIECE
    total = coef_ref.shape[2] // PIECE

    def tile(block):
        for k in range(count):
            row = slice(k + 2, k + 3)
            out = corner_sweep(
                [corner_ref[k + 2, block, lanes_of(j)] for j in range(4)],
                [done_ref[k, block, lanes_of(j)] for j in (0, 1, last - 2, last - 1)],
                row,
                coef_ref,
                side_ref,
            )
            for j, value in enumerate(out):
                swept_ref[k, block, lanes_of(j)] = value

    tiles(species, tile)
    for j, own in enumerate((0, 1, total - 2, total - 1)):
        inner_lat(swept_ref, south_ref, north_ref, coef_ref, out_ref, j, own)


def corner_sweep(corner, inner, row, coef_ref, side_ref):
    total = coef_ref.shape[2] // PIECE
    faces = [[coef_ref[i, row, lanes_of(j)] for j in range(3)] for i in (LON_C, LON_G)]
    out = lon_sweep(corner[:2] + inner[:2], *faces)
    faces = [
        [coef_ref[i, row, lanes_of(j)] for j in (total - 2, total - 1)] + [side_ref[i, row, lanes_of(3)]]
        for i in (LON_C, LON_G)
    ]
    return out + lon_sweep(inner[2:] + corner[2:], *faces)


def join(j, pieces):
    if 2 <= j < pieces - 2:
        return False, lanes_of(j - 2)
    return True, lanes_of(j if j < 2 else j - pieces + 4)


def last_kernel(
    inner_a, inner_c, swept_a, swept_c, own_south_a, own_north_a, own_south_c, own_north_c,
    south_a, north_a, south_c, north_c, coef_ref, row_ref, chem_ref,
    out_ref, edge_ref, sems,
):
    count, species, main = inner_a.shape
    rows = count + 4
    width = coef_ref.shape[2]
    pieces = width // PIECE
    edge = (0, 1, rows - 2, rows - 1)
    two = 2 * PIECE
    copies = []
    for i in range(count):
        for k, (source, at) in enumerate(
            (
                (inner_a.at[i], two),
                (inner_c.at[i, :, 0:two], 0),
                (inner_c.at[i, :, two : 2 * two], width - two),
            )
        ):
            lanes = main if k == 0 else two
            copies.append(
                pltpu.make_async_copy(source, out_ref.at[:, i + 2, at : at + lanes], sems.at[3 * i + k])
            )
    for copy in copies:
        copy.start()
    valid_south, valid_north = chem_ref[3 * species + 2 : 3 * species + 3], chem_ref[3 * species + 3 : 3 * species + 4]
    for j in range(pieces):
        own = lanes_of(j)
        side, at = join(j, pieces)
        south, own_south, own_north, north, swept_ref = (
            (south_c, own_south_c, own_north_c, north_c, swept_c)
            if side
            else (south_a, own_south_a, own_north_a, north_a, swept_a)
        )
        lower = (
            [south[i, :, at] * valid_south for i in (0, 1)]
            + [own_south[i, :, at] for i in (0, 1)]
            + [swept_ref[i, :, at] for i in (0, 1)]
        )
        upper = (
            [swept_ref[i, :, at] for i in (2, 3)]
            + [own_north[i, :, at] for i in (0, 1)]
            + [north[i, :, at] * valid_north for i in (0, 1)]
        )
        lower_faces = [
            [coef_ref[i, 0:1, own] * valid_south, coef_ref[i, 1:2, own], coef_ref[i, 2:3, own]]
            for i in (LAT_C, LAT_G)
        ]
        upper_faces = [
            [
                coef_ref[i, rows - 2 : rows - 1, own],
                coef_ref[i, rows - 1 : rows, own],
                row_ref[8 * (i - LAT_C) : 8 * (i - LAT_C) + 1, own] * valid_north,
            ]
            for i in (LAT_C, LAT_G)
        ]
        for k, q in enumerate(lat_sweep(lower, *lower_faces) + lat_sweep(upper, *upper_faces)):
            edge_ref[k, :, own] = q
    more = [
        pltpu.make_async_copy(edge_ref.at[k], out_ref.at[:, r, :], sems.at[3 * count + k]) for k, r in enumerate(edge)
    ]
    for copy in more:
        copy.start()
    for copy in copies + more:
        copy.wait()


def shards(
    tracers,
    courant,
    switches,
    day_flags,
    diffusion_counts,
    night_rates,
    photo_rates,
    level_light,
    self_loss,
    vertical_mixing,
):
    species, rows, width = tracers.shape
    inner = width - 2 * PIECE
    two = 2 * PIECE
    four = 4 * PIECE
    message = (rows * species + 6 * rows, two)

    own_south, own_north, west, east, coef, own_row, chem = call(
        first_kernel,
        [(2, species, inner), (2, species, inner), message, message, (6, rows, width), (16, width), (3 * species + 8, PIECE)],
        [FAR] * 10,
        tracers,
        courant,
        switches,
        day_flags,
        diffusion_counts,
        night_rates,
        photo_rates,
        level_light[None],
        self_loss[None],
        vertical_mixing[None],
        scratch=[
            pltpu.VMEM((rows, species, width), F32),
            pltpu.VMEM((species, rows, four), F32),
            pltpu.VMEM(courant.shape, F32),
            pltpu.VMEM(switches.shape, jnp.int32),
            pltpu.VMEM(day_flags.shape, jnp.int32),
            pltpu.VMEM(diffusion_counts.shape, jnp.int32),
            pltpu.VMEM(night_rates.shape, F32),
            pltpu.VMEM(photo_rates.shape, F32),
            pltpu.VMEM((1,) + level_light.shape, F32),
            pltpu.VMEM((1,) + self_loss.shape, F32),
            pltpu.VMEM((1,) + vertical_mixing.shape, F32),
            pltpu.SemaphoreType.DMA((rows,)),
            pltpu.SemaphoreType.DMA((9,)),
        ],
        cost=3,
        limit=VMEM_ALL,
    )
    south = ring(own_north, "lat", 1)
    north = ring(own_south, "lat", -1)
    halo_west = ring(east, "lon", 1)
    halo_east = ring(west, "lon", -1)
    row = ring(own_row, "lat", -1)

    mid, done, table = call(
        inner_kernel,
        [
            (rows - 4, species, inner),
            (rows - 4, species, inner),
            jax.ShapeDtypeStruct((2, KMAX, 2, HALF, PIECE), BF16),
        ],
        [FAR] + [WHOLE] * 4 + [SCALARS],
        tracers,
        own_south,
        own_north,
        coef,
        chem,
        diffusion_counts,
        scratch=[pltpu.VMEM((rows - 4, species, width), F32), pltpu.SemaphoreType.DMA((rows - 4,))],
        cost=9,
        limit=VMEM_ALL,
    )
    edge_done, main_south, main_north = call(
        edge_kernel,
        [(4, species, inner), (2, species, inner - two), (2, species, inner - two)],
        [WHOLE] * 9 + [SCALARS],
        mid,
        own_south,
        own_north,
        south,
        north,
        coef,
        row,
        chem,
        table,
        diffusion_counts,
        cost=9,
    )
    main_from_south = ring(main_north, "lat", 1)
    main_from_north = ring(main_south, "lat", -1)
    mid_side, side_south, side_north, side, counts = call(
        side_kernel,
        [(rows, species, four), (2 * species + 8, four), (2 * species, four), (6, rows, four), jax.ShapeDtypeStruct((rows, four), jnp.int32)],
        [FAR] + [WHOLE] * 5,
        edge_done,
        west,
        east,
        halo_west,
        halo_east,
        coef,
        cost=3,
    )
    side_from_south = ring(side_north, "lat", 1)
    side_from_north = ring(side_south, "lat", -1)
    swept_main, main_out = call(
        rest_kernel,
        [(rows - 4, species, inner - two)] * 2,
        [WHOLE] * 4,
        done,
        main_south,
        main_north,
        coef,
        cost=3,
    )
    corner, corner_south, corner_north = call(
        corner_kernel,
        [(rows, species, four), (2, species, four), (2, species, four)],
        [WHOLE] * 8 + [SCALARS],
        mid_side,
        side_from_south,
        side_from_north,
        edge_done,
        coef,
        side,
        chem,
        table,
        counts,
        cost=5,
    )
    corner_from_south = ring(corner_north, "lat", 1)
    corner_from_north = ring(corner_south, "lat", -1)
    swept_corner, corner_out = call(
        rest_corner_kernel,
        [(rows - 4, species, four)] * 2,
        [WHOLE] * 6,
        done,
        corner,
        corner_south,
        corner_north,
        coef,
        side,
        cost=2,
    )
    (out,) = call(
        last_kernel,
        [(species, rows, width)],
        [WHOLE] * 15,
        main_out,
        corner_out,
        swept_main,
        swept_corner,
        main_south,
        main_north,
        corner_south,
        corner_north,
        main_from_south,
        main_from_north,
        corner_from_south,
        corner_from_north,
        coef,
        row,
        chem,
        scratch=[pltpu.VMEM((4, species, width), F32), pltpu.SemaphoreType.DMA((3 * rows,))],
        out_specs=[FAR],
        cost=3,
    )
    return out


def solution(mesh):
    in_specs = (
        P(None, "lat", "lon"),
        P(None, "lat", "lon"),
        P(None, "lat", "lon"),
        P("lat", "lon"),
        P("lat", "lon"),
        P(),
        P(),
        P(),
        P(),
        P(),
    )
    out_specs = P(None, "lat", "lon")
    return jax.shard_map(shards, mesh=mesh, in_specs=in_specs, out_specs=out_specs, check_vma=False)
```

```python
import jax
import jax.numpy as jnp
from jax import lax
from jax.experimental import pallas as pl
from jax.experimental.pallas import tpu as pltpu
from jax.sharding import PartitionSpec as P

CHEM = 6
KMAX = 8
PIECE = 128
HALF = 64
LEVELS = 64
VMEM_LIMIT = 24 * 1024 * 1024
VMEM_ALL = 60 * 1024 * 1024
F32 = jnp.float32
BF16 = jnp.bfloat16
LON_C, LON_G, LAT_C, LAT_G, DAY, COUNT = range(6)


def ring(value, axis, steps):
    count = lax.axis_size(axis)
    return lax.ppermute(value, axis, [(i, (i + steps) % count) for i in range(count)])


def half_roll(value):
    return pltpu.roll(value, HALF, 1)


def minmod(x, y):
    return jnp.minimum(jnp.maximum(x, jnp.minimum(y, 0.0)), jnp.maximum(y, 0.0))


def gain(cour, switch):
    return 0.5 * cour * switch * jnp.where(cour >= 0.0, 1.0 - cour, -1.0 - cour)


def lon_sweep(cells, cours, gains):
    n = len(cells)
    low = lax.broadcasted_iota(jnp.int32, cells[0].shape, 1) < HALF
    turned = [half_roll(q) for q in cells]
    flux = [None]
    for i in range(1, n):
        west = jnp.where(low, turned[i - 1], turned[i])
        east = jnp.where(low, turned[i], turned[i + 1]) if i < n - 1 else turned[i]
        step = cells[i] - west
        slope = minmod(step, east - cells[i])
        behind = minmod(west - cells[i - 1], step)
        forward = cours[i - 1] >= 0.0
        flux.append(
            cours[i - 1] * jnp.where(forward, west, cells[i])
            + gains[i - 1] * jnp.where(forward, behind, slope)
        )
    turned = [None] + [half_roll(f) for f in flux[1:]]
    return [
        cells[i] - (jnp.where(low, turned[i], turned[i + 1]) - flux[i]) for i in range(1, n - 1)
    ]


def lat_sweep(rows, cours, gains):
    n = len(rows) - 4
    step = [rows[i + 1] - rows[i] for i in range(n + 3)]
    slope = [minmod(step[i], step[i + 1]) for i in range(n + 2)]
    flux = []
    for i in range(n + 1):
        forward = cours[i] >= 0.0
        flux.append(
            cours[i] * jnp.where(forward, rows[i + 1], rows[i + 2])
            + gains[i] * jnp.where(forward, slope[i], slope[i + 1])
        )
    return [rows[i + 2] - (flux[i + 1] - flux[i]) for i in range(n)]


def expand(compact, first):
    rows = compact.shape[0]
    low = lax.broadcasted_iota(jnp.int32, (rows, PIECE), 1) < HALF
    left = jnp.broadcast_to(compact[:, first : first + 1], (rows, PIECE))
    right = jnp.broadcast_to(compact[:, first + 1 : first + 2], (rows, PIECE))
    return jnp.where(low, left, right)


def rate_pieces(chem_ref, species):
    square = (2 * species, species)
    own = lax.broadcasted_iota(jnp.int32, square, 0) == lax.broadcasted_iota(jnp.int32, square, 1)
    rates = chem_ref[0 : 2 * species, 0:species] + jnp.where(own, 1.0, 0.0)
    high = rates.astype(BF16)
    low = (rates - high.astype(F32)).astype(BF16)
    return jnp.concatenate([high, high, low], 1)


def react(rows, suns, rates, loss):
    species = rows[0].shape[0]
    for _ in range(CHEM):
        nexts = []
        for q, sun in zip(rows, suns):
            high = q.astype(BF16)
            low = (q - high.astype(F32)).astype(BF16)
            both = jnp.dot(
                rates, jnp.concatenate([high, low, high], 0), preferred_element_type=F32
            )
            top = both[:species] + sun * both[species:]
            nexts.append(top * pl.reciprocal(1.0 + loss * q * q, approx=True))
        rows = nexts
    return rows


def fill_table(mixing, table_ref):
    shape = (HALF, PIECE)
    lane = lax.broadcasted_iota(jnp.int32, shape, 1)
    low = lane < HALF
    q = jnp.where((lane & (HALF - 1)) == lax.broadcasted_iota(jnp.int32, shape, 0), 1.0, 0.0)
    for n in range(KMAX):
        flux = mixing * (pltpu.roll(q, PIECE - 1, 1) - q)
        q = q + flux - pltpu.roll(flux, 1, 1)
        high = q.astype(BF16).astype(F32)
        for i, term in enumerate((high, q - high)):
            table_ref[0, n, i] = jnp.where(low, term, 0.0).astype(BF16)
            table_ref[1, n, i] = jnp.where(low, 0.0, term).astype(BF16)


def diffuse(q, first, second, table_ref):
    species = q.shape[0]
    high = q.astype(BF16)
    low = (q - high.astype(F32)).astype(BF16)
    state = jnp.concatenate(
        [jnp.concatenate([high, high], 1), jnp.concatenate([low, low], 1)], 0
    )
    powers = jnp.concatenate(
        [table_ref[0, first - 1, i] if side == 0 else table_ref[1, second - 1, i] for i in (0, 1) for side in (0, 1)], 0
    )
    both = jnp.dot(state, powers, preferred_element_type=F32)
    return both[:species] + both[species:]


def column_block(rows, days, counts, rates, loss, level, table_ref):
    pieces = rows[0].shape[1] // PIECE
    level = jnp.concatenate([level] * pieces, 1)
    loss = jnp.concatenate([loss] * pieces, 1)
    rows = react(rows, [day * level for day in days], rates, loss)
    return [
        [
            diffuse(q[:, j * PIECE : (j + 1) * PIECE], counts(i, 2 * j), counts(i, 2 * j + 1), table_ref)
            for j in range(pieces)
        ]
        for i, q in enumerate(rows)
    ]


WHOLE = pl.BlockSpec(memory_space=pltpu.VMEM)
SCALARS = pl.BlockSpec(memory_space=pltpu.SMEM)
FAR = pl.BlockSpec(memory_space=pl.ANY)
BLOCK = 4 * PIECE


def call(kernel, outs, ins, *args, scratch=(), out_specs=None, cost=10.0, limit=VMEM_LIMIT):
    return pl.pallas_call(
        kernel,
        out_shape=[s if isinstance(s, jax.ShapeDtypeStruct) else jax.ShapeDtypeStruct(s, F32) for s in outs],
        in_specs=ins,
        out_specs=out_specs or [WHOLE] * len(outs),
        scratch_shapes=list(scratch),
        compiler_params=pltpu.CompilerParams(vmem_limit_bytes=limit),
        cost_estimate=pl.CostEstimate(flops=int(cost * 1.0e9), bytes_accessed=int(cost * 3.0e6), transcendentals=0),
    )(*args)


def lanes_of(j, count=1):
    return slice(j * PIECE, (j + count) * PIECE)


def blocks(width, body):
    full = width // BLOCK

    def step(b, carry):
        body(pl.multiple_of(b * BLOCK, BLOCK), BLOCK)
        return carry

    if full:
        lax.fori_loop(0, full, step, 0)
    if width % BLOCK:
        body(full * BLOCK, width % BLOCK)


def tiles(species, body):
    def step(s, carry):
        body(pl.ds(pl.multiple_of(s * 8, 8), 8))
        return carry

    lax.fori_loop(0, species // 8, step, 0)


def wide(row, lanes):
    return jnp.concatenate([row] * (lanes // PIECE), 1)


def fill_chem(night_ref, photo_ref, level_ref, loss_ref, mixing_ref, chem_ref):
    species = night_ref.shape[0]
    chem_ref[0:species, 0:species] = night_ref[...]
    chem_ref[species : 2 * species, 0:species] = photo_ref[...]
    square = (species, species)
    own = lax.broadcasted_iota(jnp.int32, square, 0) == lax.broadcasted_iota(jnp.int32, square, 1)
    loss = jnp.sum(jnp.where(own, loss_ref[...], 0.0), axis=1, keepdims=True)
    chem_ref[2 * species : 3 * species] = jnp.broadcast_to(loss, (species, PIECE))
    at = 3 * species
    chem_ref[at : at + 8] = jnp.zeros((8, PIECE), F32)
    for i, ref in enumerate((level_ref, mixing_ref)):
        row = slice(at + i, at + i + 1)
        chem_ref[row, 0 : ref.shape[1]] = ref[...]
        low = lax.broadcasted_iota(jnp.int32, (1, PIECE), 1) < HALF
        value = chem_ref[row]
        chem_ref[row] = jnp.where(low, value, half_roll(value))
    lat = lax.axis_index("lat")
    for i, there in ((2, lat > 0), (3, lat < lax.axis_size("lat") - 1)):
        chem_ref[at + i : at + i + 1] = jnp.where(there, 1.0, 0.0) * jnp.ones((1, PIECE), F32)


def face_fields(cour_ref, sw_ref, day_ref, cnt_ref):
    cour = [cour_ref[0], cour_ref[1]]
    switch = [sw_ref[0].astype(F32), sw_ref[1].astype(F32)]
    return [
        cour[0],
        gain(cour[0], switch[0]),
        cour[1],
        gain(cour[1], switch[1]),
        day_ref[...].astype(F32),
        cnt_ref[...].astype(F32),
    ]


def start_kernel(
    x_ref, cour_in, sw_in, day_in, cnt_in, west_ref, east_ref, sides_ref, cour_ref, sw_ref, day_ref, cnt_ref, sems
):
    species, rows, width = x_ref.shape
    two = 2 * PIECE
    copies = [
        pltpu.make_async_copy(a, b, sems.at[i])
        for i, (a, b) in enumerate(
            (
                (cour_in, cour_ref),
                (sw_in, sw_ref),
                (day_in, day_ref),
                (cnt_in, cnt_ref),
                (x_ref.at[:, :, 0:two], sides_ref.at[:, :, 0:two]),
                (x_ref.at[:, :, width - two : width], sides_ref.at[:, :, two : 2 * two]),
            )
        )
    ]
    for copy in copies:
        copy.start()
    for copy in copies[:4]:
        copy.wait()
    fields = face_fields(cour_ref, sw_ref, day_ref, cnt_ref)
    columns = cour_ref.shape[2]
    for ref, first in ((west_ref, 0), (east_ref, columns - 4)):
        for i, field in enumerate(fields):
            at = rows * species + i * rows
            for half in (0, 1):
                ref[at : at + rows, lanes_of(half)] = expand(field, first + 2 * half)
    for copy in copies[4:]:
        copy.wait()
    for j, ref in enumerate((west_ref, east_ref)):
        for r in range(rows):
            ref[r * species : (r + 1) * species] = sides_ref[:, r, lanes_of(2 * j, 2)]


def first_kernel(
    west_ref, x_ref, cour_in, sw_in, day_in, cnt_in, night_in, photo_in, level_in, loss_in, mixing_in,
    south_ref, north_ref, coef_ref, row_ref, chem_ref,
    xt_ref, cour_ref, sw_ref, day_ref, cnt_ref, night_ref, photo_ref, level_ref, loss_ref, mixing_ref,
    row_sems, sems,
):
    rows, species, width = xt_ref.shape
    pieces = width // PIECE
    edge = (0, 1, rows - 2, rows - 1)
    small = [
        pltpu.make_async_copy(a, b, sems.at[i])
        for i, (a, b) in enumerate(
            (
                (cour_in, cour_ref),
                (sw_in, sw_ref),
                (day_in, day_ref),
                (cnt_in, cnt_ref),
                (night_in, night_ref),
                (photo_in, photo_ref),
                (level_in, level_ref),
                (loss_in, loss_ref),
                (mixing_in, mixing_ref),
            )
        )
    ]
    big = {r: pltpu.make_async_copy(x_ref.at[:, r, :], xt_ref.at[r], row_sems.at[r]) for r in edge}
    for copy in small:
        copy.start()
    for copy in big.values():
        copy.start()
    for copy in small:
        copy.wait()
    fields = face_fields(cour_ref, sw_ref, day_ref, cnt_ref)
    for i, field in enumerate(fields):
        for j in range(pieces):
            coef_ref[i, :, lanes_of(j)] = expand(field, 2 * j)
    fill_chem(night_ref, photo_ref, level_ref, loss_ref, mixing_ref, chem_ref)
    row_ref[0:8] = coef_ref[LAT_C]
    row_ref[8:16] = coef_ref[LAT_G]
    for r in edge:
        big[r].wait()

    def tile(block):
        for r in edge:
            cells = [xt_ref[r, block, lanes_of(j)] for j in range(pieces)]
            faces = [
                [coef_ref[i, r : r + 1, lanes_of(j)] for j in range(1, pieces)] for i in (LON_C, LON_G)
            ]
            ref, row = (south_ref, r) if r < 2 else (north_ref, r - rows + 2)
            for j, value in enumerate(lon_sweep(cells, *faces)):
                ref[row, block, lanes_of(j)] = value

    tiles(species, tile)


def inner_kernel(
    x_ref, south_ref, north_ref, coef_ref, chem_ref, cnt_ref,
    mid_ref, done_ref, table_ref, xt_ref, sems,
):
    species, rows, width = x_ref.shape
    pieces = width // PIECE
    inner = range(2, rows - 2)
    copies = [pltpu.make_async_copy(x_ref.at[:, r, :], xt_ref.at[r - 2], sems.at[r - 2]) for r in inner]
    for copy in copies:
        copy.start()
    fill_table(chem_ref[3 * species + 1 : 3 * species + 2], table_ref)
    for copy in copies:
        copy.wait()

    def tile(block):
        for r in inner:
            cells = [xt_ref[r - 2, block, lanes_of(j)] for j in range(pieces)]
            faces = [
                [coef_ref[i, r : r + 1, lanes_of(j)] for j in range(1, pieces)] for i in (LON_C, LON_G)
            ]
            for j, value in enumerate(lon_sweep(cells, *faces)):
                mid_ref[r - 2, block, lanes_of(j)] = value

    tiles(species, tile)
    rates = rate_pieces(chem_ref, species)

    def block(at, lanes):
        here = pl.ds(at, lanes)
        own = pl.ds(at + PIECE if isinstance(at, int) else pl.multiple_of(at + PIECE, PIECE), lanes)
        column = 2 + at // LEVELS
        cells = (
            [south_ref[i, :, here] for i in (0, 1)]
            + [mid_ref[i, :, here] for i in range(rows - 4)]
            + [north_ref[i, :, here] for i in (0, 1)]
        )
        faces = [[coef_ref[i, f : f + 1, own] for f in range(2, rows - 1)] for i in (LAT_C, LAT_G)]
        done = column_block(
            lat_sweep(cells, *faces),
            [coef_ref[DAY, r : r + 1, own] for r in inner],
            lambda i, j: cnt_ref[2 + i, column + j],
            rates,
            chem_ref[2 * species : 3 * species],
            chem_ref[3 * species + 0 : 3 * species + 1],
            table_ref,
        )
        for i, row in enumerate(done):
            done_ref[i, :, here] = jnp.concatenate(row, 1)

    blocks(width - 2 * PIECE, block)


def side_kernel(
    done_ref, xw_ref, xe_ref, hw_ref, he_ref, coef_ref, mid_ref, south_ref, north_ref, side_ref, cnt_ref
):
    rows, species = mid_ref.shape[:2]
    width = coef_ref.shape[2]
    base = rows * species
    for i in range(6):
        here = slice(base + i * rows, base + (i + 1) * rows)
        side_ref[i, :, lanes_of(0)] = hw_ref[here, lanes_of(1)]
        side_ref[i, :, lanes_of(1)] = coef_ref[i, :, 0:PIECE]
        side_ref[i, :, lanes_of(2)] = coef_ref[i, :, width - PIECE : width]
        side_ref[i, :, lanes_of(3)] = he_ref[here, lanes_of(0)]

    cnt_ref[...] = side_ref[COUNT].astype(jnp.int32)

    def tile(s, carry):
        for r in range(rows):
            row = slice(r, r + 1)
            from_row = pl.ds(pl.multiple_of(r * species + s * 8, 8), 8)
            block = pl.ds(pl.multiple_of(s * 8, 8), 8)
            faces = [
                [side_ref[i, row, lanes_of(0)], side_ref[i, row, lanes_of(1)], coef_ref[i, row, lanes_of(1)]]
                for i in (LON_C, LON_G)
            ]
            out = lon_sweep([ref[from_row, lanes_of(h)] for ref in (hw_ref, xw_ref) for h in (0, 1)], *faces)
            faces = [
                [
                    side_ref[i, row, lanes_of(2)],
                    side_ref[i, row, lanes_of(3)],
                    he_ref[base + i * rows + r : base + i * rows + r + 1, lanes_of(1)],
                ]
                for i in (LON_C, LON_G)
            ]
            out = out + lon_sweep([ref[from_row, lanes_of(h)] for ref in (xe_ref, he_ref) for h in (0, 1)], *faces)
            for j, value in enumerate(out):
                mid_ref[r, block, lanes_of(j)] = value
                if r < 2:
                    south_ref[pl.ds(pl.multiple_of(r * species + s * 8, 8), 8), lanes_of(j)] = value
                if r >= rows - 2:
                    north_ref[pl.ds(pl.multiple_of((r - rows + 2) * species + s * 8, 8), 8), lanes_of(j)] = value
        return carry

    lax.fori_loop(0, species // 8, tile, 0)
    for j in range(4):
        two = [side_ref[i, 0:1, lanes_of(j)] for i in (LAT_C, LAT_G)]
        south_ref[2 * species : 2 * species + 8, lanes_of(j)] = jnp.concatenate([two[0]] * 4 + [two[1]] * 4, 0)


def edge_kernel(
    side_ref, mid_ref, own_south_ref, own_north_ref, south_ref, north_ref, coef_ref, row_ref,
    chem_ref, table_ref, cnt_ref,
    done_ref, sent_south_ref, sent_north_ref,
):
    species, inner_width = mid_ref.shape[1:]
    rows = coef_ref.shape[1]
    rates = rate_pieces(chem_ref, species)
    edge = (0, 1, rows - 2, rows - 1)

    def block(at, lanes):
        here = pl.ds(at, lanes)
        own = pl.ds(at + PIECE if isinstance(at, int) else pl.multiple_of(at + PIECE, PIECE), lanes)
        column = 2 + at // LEVELS
        valid_south, valid_north = wide(chem_ref[3 * species + 2 : 3 * species + 3], lanes), wide(chem_ref[3 * species + 3 : 3 * species + 4], lanes)
        lower = (
            [south_ref[i, :, here] * valid_south for i in (0, 1)]
            + [own_south_ref[i, :, here] for i in (0, 1)]
            + [mid_ref[i, :, here] for i in (0, 1)]
        )
        upper = (
            [mid_ref[i, :, here] for i in (2, 3)]
            + [own_north_ref[i, :, here] for i in (0, 1)]
            + [north_ref[i, :, here] * valid_north for i in (0, 1)]
        )
        lower_faces = [
            [coef_ref[i, 0:1, own] * valid_south, coef_ref[i, 1:2, own], coef_ref[i, 2:3, own]]
            for i in (LAT_C, LAT_G)
        ]
        upper_faces = [
            [
                coef_ref[i, rows - 2 : rows - 1, own],
                coef_ref[i, rows - 1 : rows, own],
                row_ref[8 * (i - LAT_C) : 8 * (i - LAT_C) + 1, own] * valid_north,
            ]
            for i in (LAT_C, LAT_G)
        ]
        done = column_block(
            lat_sweep(lower, *lower_faces) + lat_sweep(upper, *upper_faces),
            [coef_ref[DAY, r : r + 1, own] for r in edge],
            lambda i, j: cnt_ref[edge[i], column + j],
            rates,
            chem_ref[2 * species : 3 * species],
            chem_ref[3 * species + 0 : 3 * species + 1],
            table_ref,
        )
        for i, row in enumerate(done):
            done_ref[i, :, here] = jnp.concatenate(row, 1)

    blocks(inner_width, block)
    pieces = inner_width // PIECE

    def tile(block):
        for k, r in enumerate(edge):
            cells = [done_ref[k, block, lanes_of(j)] for j in range(pieces)]
            faces = [
                [coef_ref[i, r : r + 1, lanes_of(j + 1)] for j in range(1, pieces)] for i in (LON_C, LON_G)
            ]
            ref = sent_south_ref if k < 2 else sent_north_ref
            for j, value in enumerate(lon_sweep(cells, *faces)):
                ref[k % 2, block, lanes_of(j)] = value

    tiles(species, tile)


def corner_kernel(
    mid_ref, south_ref, north_ref, edge_ref, coef_ref, side_ref,
    chem_ref, table_ref, cnt_ref,
    done_ref, sent_south_ref, sent_north_ref,
):
    rows, species, width = mid_ref.shape
    rates = rate_pieces(chem_ref, species)
    valid_south, valid_north = wide(chem_ref[3 * species + 2 : 3 * species + 3], width), wide(chem_ref[3 * species + 3 : 3 * species + 4], width)
    cells = (
        [south_ref[i * species : (i + 1) * species] * valid_south for i in (0, 1)]
        + [mid_ref[r] for r in range(rows)]
        + [north_ref[i * species : (i + 1) * species] * valid_north for i in (0, 1)]
    )
    faces = [
        [side_ref[i, 0:1] * valid_south]
        + [side_ref[i, r : r + 1] for r in range(1, rows)]
        + [north_ref[2 * species + 4 * (i - LAT_C) : 2 * species + 4 * (i - LAT_C) + 1] * valid_north]
        for i in (LAT_C, LAT_G)
    ]
    for r, q in enumerate(lat_sweep(cells, *faces)):
        done_ref[r] = q
    for part in (0, rows // 2):
        done = column_block(
            [done_ref[part + i] for i in range(rows // 2)],
            [side_ref[DAY, part + i : part + i + 1] for i in range(rows // 2)],
            lambda i, j: cnt_ref[part + i, LEVELS * j],
            rates,
            chem_ref[2 * species : 3 * species],
            chem_ref[3 * species + 0 : 3 * species + 1],
            table_ref,
        )
        for i, row in enumerate(done):
            done_ref[part + i] = jnp.concatenate(row, 1)
    last = edge_ref.shape[2] // PIECE

    def tile(block):
        for k, r in enumerate((0, 1, rows - 2, rows - 1)):
            row = slice(r, r + 1)
            ref = sent_south_ref if k < 2 else sent_north_ref
            out = corner_sweep(
                [done_ref[r, block, lanes_of(j)] for j in range(4)],
                [edge_ref[k, block, lanes_of(j)] for j in (0, 1, last - 2, last - 1)],
                row,
                coef_ref,
                side_ref,
            )
            for j, value in enumerate(out):
                ref[k % 2, block, lanes_of(j)] = value

    tiles(species, tile)


def rest_kernel(corner_ref, done_ref, south_ref, north_ref, coef_ref, swept_ref, out_ref):
    count, species, width = done_ref.shape
    pieces = width // PIECE

    def tile(block):
        for k in range(count):
            row = slice(k + 2, k + 3)
            cells = [done_ref[k, block, lanes_of(j)] for j in range(pieces)]
            faces = [[coef_ref[i, row, lanes_of(j + 1)] for j in range(1, pieces)] for i in (LON_C, LON_G)]
            for j, value in enumerate(lon_sweep(cells, *faces)):
                swept_ref[k, block, lanes_of(j)] = value

    tiles(species, tile)
    for j in range(pieces - 2):
        inner_lat(swept_ref, south_ref, north_ref, coef_ref, out_ref, j, j + 2)


def inner_lat(swept_ref, south_ref, north_ref, coef_ref, out_ref, j, own):
    count = swept_ref.shape[0]
    at = lanes_of(j)
    cells = (
        [south_ref[i, :, at] for i in (0, 1)]
        + [swept_ref[i, :, at] for i in range(count)]
        + [north_ref[i, :, at] for i in (0, 1)]
    )
    faces = [[coef_ref[i, f : f + 1, lanes_of(own)] for f in range(2, count + 3)] for i in (LAT_C, LAT_G)]
    for i, q in enumerate(lat_sweep(cells, *faces)):
        out_ref[i, :, at] = q


def rest_corner_kernel(done_ref, corner_ref, south_ref, north_ref, coef_ref, side_ref, swept_ref, out_ref):
    count, species, width = done_ref.shape
    last = width // PIECE
    total = coef_ref.shape[2] // PIECE

    def tile(block):
        for k in range(count):
            row = slice(k + 2, k + 3)
            out = corner_sweep(
                [corner_ref[k + 2, block, lanes_of(j)] for j in range(4)],
                [done_ref[k, block, lanes_of(j)] for j in (0, 1, last - 2, last - 1)],
                row,
                coef_ref,
                side_ref,
            )
            for j, value in enumerate(out):
                swept_ref[k, block, lanes_of(j)] = value

    tiles(species, tile)
    for j, own in enumerate((0, 1, total - 2, total - 1)):
        inner_lat(swept_ref, south_ref, north_ref, coef_ref, out_ref, j, own)


def corner_sweep(corner, inner, row, coef_ref, side_ref):
    total = coef_ref.shape[2] // PIECE
    faces = [[coef_ref[i, row, lanes_of(j)] for j in range(3)] for i in (LON_C, LON_G)]
    out = lon_sweep(corner[:2] + inner[:2], *faces)
    faces = [
        [coef_ref[i, row, lanes_of(j)] for j in (total - 2, total - 1)] + [side_ref[i, row, lanes_of(3)]]
        for i in (LON_C, LON_G)
    ]
    return out + lon_sweep(inner[2:] + corner[2:], *faces)


def edge_lat(swept, own_south, own_north, south, north, coef_ref, row_ref, chem_ref, out_ref, j, own):
    count, species = swept.shape[:2]
    rows = count + 4
    at, lanes = lanes_of(j), lanes_of(own)
    valid_south = chem_ref[3 * species + 2 : 3 * species + 3]
    valid_north = chem_ref[3 * species + 3 : 3 * species + 4]
    lower = (
        [south[i, :, at] * valid_south for i in (0, 1)]
        + [own_south[i, :, at] for i in (0, 1)]
        + [swept[i, :, at] for i in (0, 1)]
    )
    upper = (
        [swept[i, :, at] for i in (2, 3)]
        + [own_north[i, :, at] for i in (0, 1)]
        + [north[i, :, at] * valid_north for i in (0, 1)]
    )
    lower_faces = [
        [coef_ref[i, 0:1, lanes] * valid_south, coef_ref[i, 1:2, lanes], coef_ref[i, 2:3, lanes]]
        for i in (LAT_C, LAT_G)
    ]
    upper_faces = [
        [
            coef_ref[i, rows - 2 : rows - 1, lanes],
            coef_ref[i, rows - 1 : rows, lanes],
            row_ref[8 * (i - LAT_C) : 8 * (i - LAT_C) + 1, lanes] * valid_north,
        ]
        for i in (LAT_C, LAT_G)
    ]
    for k, q in enumerate(lat_sweep(lower, *lower_faces) + lat_sweep(upper, *upper_faces)):
        out_ref[k, :, at] = q


def edge_last_kernel(
    inner_c, swept, own_south, own_north, south, north, coef_ref, row_ref, chem_ref, out_ref
):
    for j in range(swept.shape[2] // PIECE):
        edge_lat(swept, own_south, own_north, south, north, coef_ref, row_ref, chem_ref, out_ref, j, j + 2)


def last_kernel(
    inner_a, inner_c, edge_a, swept, own_south, own_north, south, north, coef_ref, row_ref, chem_ref,
    out_ref, edge_c, sems,
):
    count, species, main = inner_a.shape
    width = coef_ref.shape[2]
    rows = count + 4
    pieces = width // PIECE
    two = 2 * PIECE

    def copies(array, row, source, first):
        return [
            pltpu.make_async_copy(array.at[source, :, 0:two], out_ref.at[:, row, 0:two], sems.at[first]),
            pltpu.make_async_copy(
                array.at[source, :, two : 2 * two], out_ref.at[:, row, width - two : width], sems.at[first + 1]
            ),
        ]

    started = []
    edge = (0, 1, rows - 2, rows - 1)
    for i in range(count):
        started.append(pltpu.make_async_copy(inner_a.at[i], out_ref.at[:, i + 2, two : two + main], sems.at[i]))
        started.append(
            pltpu.make_async_copy(edge_a.at[i], out_ref.at[:, edge[i], two : two + main], sems.at[count + i])
        )
        started += copies(inner_c, i + 2, i, 2 * count + 2 * i)
    for copy in started:
        copy.start()
    for j, own in enumerate((0, 1, pieces - 2, pieces - 1)):
        edge_lat(swept, own_south, own_north, south, north, coef_ref, row_ref, chem_ref, edge_c, j, own)
    more = []
    for k, r in enumerate(edge):
        more += copies(edge_c, r, k, 4 * count + 2 * k)
    for copy in more:
        copy.start()
    for copy in started + more:
        copy.wait()


def shards(
    tracers,
    courant,
    switches,
    day_flags,
    diffusion_counts,
    night_rates,
    photo_rates,
    level_light,
    self_loss,
    vertical_mixing,
):
    species, rows, width = tracers.shape
    inner = width - 2 * PIECE
    two = 2 * PIECE
    four = 4 * PIECE
    message = (rows * species + 6 * rows, two)

    columns = [
        pltpu.VMEM(courant.shape, F32),
        pltpu.VMEM(switches.shape, jnp.int32),
        pltpu.VMEM(day_flags.shape, jnp.int32),
        pltpu.VMEM(diffusion_counts.shape, jnp.int32),
    ]
    west, east = call(
        start_kernel,
        [message, message],
        [FAR] * 5,
        tracers,
        courant,
        switches,
        day_flags,
        diffusion_counts,
        scratch=[pltpu.VMEM((species, rows, four), F32)] + columns + [pltpu.SemaphoreType.DMA((6,))],
        cost=2,
        limit=VMEM_ALL,
    )
    halo_west = ring(east, "lon", 1)
    halo_east = ring(west, "lon", -1)
    own_south, own_north, coef, own_row, chem = call(
        first_kernel,
        [(2, species, inner), (2, species, inner), (6, rows, width), (16, width), (3 * species + 8, PIECE)],
        [FAR] * 11,
        west,
        tracers,
        courant,
        switches,
        day_flags,
        diffusion_counts,
        night_rates,
        photo_rates,
        level_light[None],
        self_loss[None],
        vertical_mixing[None],
        scratch=[
            pltpu.VMEM((rows, species, width), F32),
            *columns,
            pltpu.VMEM(night_rates.shape, F32),
            pltpu.VMEM(photo_rates.shape, F32),
            pltpu.VMEM((1,) + level_light.shape, F32),
            pltpu.VMEM((1,) + self_loss.shape, F32),
            pltpu.VMEM((1,) + vertical_mixing.shape, F32),
            pltpu.SemaphoreType.DMA((rows,)),
            pltpu.SemaphoreType.DMA((9,)),
        ],
        cost=3,
        limit=VMEM_ALL,
    )
    south = ring(own_north, "lat", 1)
    north = ring(own_south, "lat", -1)
    row = ring(own_row, "lat", -1)

    mid, done, table = call(
        inner_kernel,
        [
            (rows - 4, species, inner),
            (rows - 4, species, inner),
            jax.ShapeDtypeStruct((2, KMAX, 2, HALF, PIECE), BF16),
        ],
        [FAR] + [WHOLE] * 4 + [SCALARS],
        tracers,
        own_south,
        own_north,
        coef,
        chem,
        diffusion_counts,
        scratch=[pltpu.VMEM((rows - 4, species, width), F32), pltpu.SemaphoreType.DMA((rows - 4,))],
        cost=9,
        limit=VMEM_ALL,
    )
    mid_side, side_south, side_north, side, counts = call(
        side_kernel,
        [(rows, species, four), (2 * species + 8, four), (2 * species, four), (6, rows, four), jax.ShapeDtypeStruct((rows, four), jnp.int32)],
        [FAR] + [WHOLE] * 5,
        done,
        west,
        east,
        halo_west,
        halo_east,
        coef,
        cost=3,
    )
    side_from_south = ring(side_north, "lat", 1)
    side_from_north = ring(side_south, "lat", -1)
    edge_done, main_south, main_north = call(
        edge_kernel,
        [(4, species, inner), (2, species, inner - two), (2, species, inner - two)],
        [FAR] + [WHOLE] * 9 + [SCALARS],
        side,
        mid,
        own_south,
        own_north,
        south,
        north,
        coef,
        row,
        chem,
        table,
        diffusion_counts,
        cost=9,
    )
    main_from_south = ring(main_north, "lat", 1)
    main_from_north = ring(main_south, "lat", -1)
    corner, corner_south, corner_north = call(
        corner_kernel,
        [(rows, species, four), (2, species, four), (2, species, four)],
        [WHOLE] * 8 + [SCALARS],
        mid_side,
        side_from_south,
        side_from_north,
        edge_done,
        coef,
        side,
        chem,
        table,
        counts,
        cost=5,
    )
    corner_from_south = ring(corner_north, "lat", 1)
    corner_from_north = ring(corner_south, "lat", -1)
    swept_main, main_out = call(
        rest_kernel,
        [(rows - 4, species, inner - two)] * 2,
        [FAR] + [WHOLE] * 4,
        corner_south,
        done,
        main_south,
        main_north,
        coef,
        cost=0.1,
    )
    swept_corner, corner_out = call(
        rest_corner_kernel,
        [(rows - 4, species, four)] * 2,
        [WHOLE] * 6,
        done,
        corner,
        corner_south,
        corner_north,
        coef,
        side,
        cost=0.1,
    )
    (edge_out,) = call(
        edge_last_kernel,
        [(4, species, inner - two)],
        [FAR] + [WHOLE] * 8,
        corner_out,
        swept_main,
        main_south,
        main_north,
        main_from_south,
        main_from_north,
        coef,
        row,
        chem,
        cost=0.5,
    )
    (out,) = call(
        last_kernel,
        [(species, rows, width)],
        [WHOLE] * 11,
        main_out,
        corner_out,
        edge_out,
        swept_corner,
        corner_south,
        corner_north,
        corner_from_south,
        corner_from_north,
        coef,
        row,
        chem,
        scratch=[pltpu.VMEM((4, species, four), F32), pltpu.SemaphoreType.DMA((3 * rows,))],
        out_specs=[FAR],
        cost=3,
    )
    return out


def solution(mesh):
    in_specs = (
        P(None, "lat", "lon"),
        P(None, "lat", "lon"),
        P(None, "lat", "lon"),
        P("lat", "lon"),
        P("lat", "lon"),
        P(),
        P(),
        P(),
        P(),
        P(),
    )
    out_specs = P(None, "lat", "lon")
    return jax.shard_map(shards, mesh=mesh, in_specs=in_specs, out_specs=out_specs, check_vma=False)
```

```python
import jax
import jax.numpy as jnp
from jax import lax
from jax.experimental import pallas as pl
from jax.experimental.pallas import tpu as pltpu
from jax.sharding import PartitionSpec as P

CHEM = 6
KMAX = 8
PIECE = 128
HALF = 64
LEVELS = 64
VMEM_LIMIT = 24 * 1024 * 1024
VMEM_ALL = 60 * 1024 * 1024
F32 = jnp.float32
BF16 = jnp.bfloat16
LON_C, LON_G, LAT_C, LAT_G, DAY, COUNT = range(6)


def ring(value, axis, steps):
    count = lax.axis_size(axis)
    return lax.ppermute(value, axis, [(i, (i + steps) % count) for i in range(count)])


def half_roll(value):
    return pltpu.roll(value, HALF, 1)


def minmod(x, y):
    return jnp.minimum(jnp.maximum(x, jnp.minimum(y, 0.0)), jnp.maximum(y, 0.0))


def gain(cour, switch):
    return 0.5 * cour * switch * jnp.where(cour >= 0.0, 1.0 - cour, -1.0 - cour)


def lon_sweep(cells, cours, gains):
    n = len(cells)
    low = lax.broadcasted_iota(jnp.int32, cells[0].shape, 1) < HALF
    turned = [half_roll(q) for q in cells]
    flux = [None]
    for i in range(1, n):
        west = jnp.where(low, turned[i - 1], turned[i])
        east = jnp.where(low, turned[i], turned[i + 1]) if i < n - 1 else turned[i]
        step = cells[i] - west
        slope = minmod(step, east - cells[i])
        behind = minmod(west - cells[i - 1], step)
        forward = cours[i - 1] >= 0.0
        flux.append(
            cours[i - 1] * jnp.where(forward, west, cells[i])
            + gains[i - 1] * jnp.where(forward, behind, slope)
        )
    turned = [None] + [half_roll(f) for f in flux[1:]]
    return [
        cells[i] - (jnp.where(low, turned[i], turned[i + 1]) - flux[i]) for i in range(1, n - 1)
    ]


def lat_sweep(rows, cours, gains):
    n = len(rows) - 4
    step = [rows[i + 1] - rows[i] for i in range(n + 3)]
    slope = [minmod(step[i], step[i + 1]) for i in range(n + 2)]
    flux = []
    for i in range(n + 1):
        forward = cours[i] >= 0.0
        flux.append(
            cours[i] * jnp.where(forward, rows[i + 1], rows[i + 2])
            + gains[i] * jnp.where(forward, slope[i], slope[i + 1])
        )
    return [rows[i + 2] - (flux[i + 1] - flux[i]) for i in range(n)]


def expand(compact, first):
    rows = compact.shape[0]
    low = lax.broadcasted_iota(jnp.int32, (rows, PIECE), 1) < HALF
    left = jnp.broadcast_to(compact[:, first : first + 1], (rows, PIECE))
    right = jnp.broadcast_to(compact[:, first + 1 : first + 2], (rows, PIECE))
    return jnp.where(low, left, right)


def rate_pieces(chem_ref, species):
    square = (2 * species, species)
    own = lax.broadcasted_iota(jnp.int32, square, 0) == lax.broadcasted_iota(jnp.int32, square, 1)
    rates = chem_ref[0 : 2 * species, 0:species] + jnp.where(own, 1.0, 0.0)
    high = rates.astype(BF16)
    low = (rates - high.astype(F32)).astype(BF16)
    return jnp.concatenate([high, high, low], 1)


def react(rows, suns, rates, loss):
    species = rows[0].shape[0]
    for _ in range(CHEM):
        nexts = []
        for q, sun in zip(rows, suns):
            high = q.astype(BF16)
            low = (q - high.astype(F32)).astype(BF16)
            both = jnp.dot(
                rates, jnp.concatenate([high, low, high], 0), preferred_element_type=F32
            )
            top = both[:species] + sun * both[species:]
            nexts.append(top * pl.reciprocal(1.0 + loss * q * q, approx=True))
        rows = nexts
    return rows


def fill_table(mixing, table_ref):
    shape = (HALF, PIECE)
    lane = lax.broadcasted_iota(jnp.int32, shape, 1)
    low = lane < HALF
    q = jnp.where((lane & (HALF - 1)) == lax.broadcasted_iota(jnp.int32, shape, 0), 1.0, 0.0)
    for n in range(KMAX):
        flux = mixing * (pltpu.roll(q, PIECE - 1, 1) - q)
        q = q + flux - pltpu.roll(flux, 1, 1)
        high = q.astype(BF16).astype(F32)
        for i, term in enumerate((high, q - high)):
            table_ref[0, n, i] = jnp.where(low, term, 0.0).astype(BF16)
            table_ref[1, n, i] = jnp.where(low, 0.0, term).astype(BF16)


def diffuse(q, first, second, table_ref):
    species = q.shape[0]
    high = q.astype(BF16)
    low = (q - high.astype(F32)).astype(BF16)
    state = jnp.concatenate(
        [jnp.concatenate([high, high], 1), jnp.concatenate([low, low], 1)], 0
    )
    powers = jnp.concatenate(
        [table_ref[0, first - 1, i] if side == 0 else table_ref[1, second - 1, i] for i in (0, 1) for side in (0, 1)], 0
    )
    both = jnp.dot(state, powers, preferred_element_type=F32)
    return both[:species] + both[species:]


def column_block(rows, days, counts, rates, loss, level, table_ref):
    pieces = rows[0].shape[1] // PIECE
    level = jnp.concatenate([level] * pieces, 1)
    loss = jnp.concatenate([loss] * pieces, 1)
    rows = react(rows, [day * level for day in days], rates, loss)
    return [
        [
            diffuse(q[:, j * PIECE : (j + 1) * PIECE], counts(i, 2 * j), counts(i, 2 * j + 1), table_ref)
            for j in range(pieces)
        ]
        for i, q in enumerate(rows)
    ]


WHOLE = pl.BlockSpec(memory_space=pltpu.VMEM)
SCALARS = pl.BlockSpec(memory_space=pltpu.SMEM)
FAR = pl.BlockSpec(memory_space=pl.ANY)
BLOCK = 4 * PIECE


def call(kernel, outs, ins, *args, scratch=(), out_specs=None, cost=10.0, limit=VMEM_LIMIT):
    return pl.pallas_call(
        kernel,
        out_shape=[s if isinstance(s, jax.ShapeDtypeStruct) else jax.ShapeDtypeStruct(s, F32) for s in outs],
        in_specs=ins,
        out_specs=out_specs or [WHOLE] * len(outs),
        scratch_shapes=list(scratch),
        compiler_params=pltpu.CompilerParams(vmem_limit_bytes=limit),
        cost_estimate=pl.CostEstimate(flops=int(cost * 1.0e9), bytes_accessed=int(cost * 3.0e6), transcendentals=0),
    )(*args)


def lanes_of(j, count=1):
    return slice(j * PIECE, (j + count) * PIECE)


def blocks(width, body):
    full = width // BLOCK

    def step(b, carry):
        body(pl.multiple_of(b * BLOCK, BLOCK), BLOCK)
        return carry

    if full:
        lax.fori_loop(0, full, step, 0)
    if width % BLOCK:
        body(full * BLOCK, width % BLOCK)


def tiles(species, body):
    def step(s, carry):
        body(pl.ds(pl.multiple_of(s * 8, 8), 8))
        return carry

    lax.fori_loop(0, species // 8, step, 0)


def wide(row, lanes):
    return jnp.concatenate([row] * (lanes // PIECE), 1)


def fill_chem(night_ref, photo_ref, level_ref, loss_ref, mixing_ref, chem_ref):
    species = night_ref.shape[0]
    chem_ref[0:species, 0:species] = night_ref[...]
    chem_ref[species : 2 * species, 0:species] = photo_ref[...]
    square = (species, species)
    own = lax.broadcasted_iota(jnp.int32, square, 0) == lax.broadcasted_iota(jnp.int32, square, 1)
    loss = jnp.sum(jnp.where(own, loss_ref[...], 0.0), axis=1, keepdims=True)
    chem_ref[2 * species : 3 * species] = jnp.broadcast_to(loss, (species, PIECE))
    at = 3 * species
    chem_ref[at : at + 8] = jnp.zeros((8, PIECE), F32)
    for i, ref in enumerate((level_ref, mixing_ref)):
        row = slice(at + i, at + i + 1)
        chem_ref[row, 0 : ref.shape[1]] = ref[...]
        low = lax.broadcasted_iota(jnp.int32, (1, PIECE), 1) < HALF
        value = chem_ref[row]
        chem_ref[row] = jnp.where(low, value, half_roll(value))
    lat = lax.axis_index("lat")
    for i, there in ((2, lat > 0), (3, lat < lax.axis_size("lat") - 1)):
        chem_ref[at + i : at + i + 1] = jnp.where(there, 1.0, 0.0) * jnp.ones((1, PIECE), F32)


def face_fields(cour_ref, sw_ref, day_ref, cnt_ref):
    cour = [cour_ref[0], cour_ref[1]]
    switch = [sw_ref[0].astype(F32), sw_ref[1].astype(F32)]
    return [
        cour[0],
        gain(cour[0], switch[0]),
        cour[1],
        gain(cour[1], switch[1]),
        day_ref[...].astype(F32),
        cnt_ref[...].astype(F32),
    ]


def start_kernel(
    x_ref, cour_in, sw_in, day_in, cnt_in, west_ref, east_ref, sides_ref, cour_ref, sw_ref, day_ref, cnt_ref, sems
):
    species, rows, width = x_ref.shape
    two = 2 * PIECE
    copies = [
        pltpu.make_async_copy(a, b, sems.at[i])
        for i, (a, b) in enumerate(
            (
                (cour_in, cour_ref),
                (sw_in, sw_ref),
                (day_in, day_ref),
                (cnt_in, cnt_ref),
                (x_ref.at[:, :, 0:two], sides_ref.at[:, :, 0:two]),
                (x_ref.at[:, :, width - two : width], sides_ref.at[:, :, two : 2 * two]),
            )
        )
    ]
    for copy in copies:
        copy.start()
    for copy in copies[:4]:
        copy.wait()
    fields = face_fields(cour_ref, sw_ref, day_ref, cnt_ref)
    columns = cour_ref.shape[2]
    for ref, first in ((west_ref, 0), (east_ref, columns - 4)):
        for i, field in enumerate(fields):
            at = rows * species + i * rows
            for half in (0, 1):
                ref[at : at + rows, lanes_of(half)] = expand(field, first + 2 * half)
    for copy in copies[4:]:
        copy.wait()
    for j, ref in enumerate((west_ref, east_ref)):
        for r in range(rows):
            ref[r * species : (r + 1) * species] = sides_ref[:, r, lanes_of(2 * j, 2)]


def first_kernel(
    west_ref, x_ref, cour_in, sw_in, day_in, cnt_in, night_in, photo_in, level_in, loss_in, mixing_in,
    south_ref, north_ref, coef_ref, row_ref, chem_ref,
    xt_ref, cour_ref, sw_ref, day_ref, cnt_ref, night_ref, photo_ref, level_ref, loss_ref, mixing_ref,
    row_sems, sems,
):
    rows, species, width = xt_ref.shape
    pieces = width // PIECE
    edge = (0, 1, rows - 2, rows - 1)
    small = [
        pltpu.make_async_copy(a, b, sems.at[i])
        for i, (a, b) in enumerate(
            (
                (cour_in, cour_ref),
                (sw_in, sw_ref),
                (day_in, day_ref),
                (cnt_in, cnt_ref),
                (night_in, night_ref),
                (photo_in, photo_ref),
                (level_in, level_ref),
                (loss_in, loss_ref),
                (mixing_in, mixing_ref),
            )
        )
    ]
    big = {r: pltpu.make_async_copy(x_ref.at[:, r, :], xt_ref.at[r], row_sems.at[r]) for r in edge}
    for copy in small:
        copy.start()
    for copy in big.values():
        copy.start()
    for copy in small:
        copy.wait()
    fields = face_fields(cour_ref, sw_ref, day_ref, cnt_ref)
    for i, field in enumerate(fields):
        for j in range(pieces):
            coef_ref[i, :, lanes_of(j)] = expand(field, 2 * j)
    fill_chem(night_ref, photo_ref, level_ref, loss_ref, mixing_ref, chem_ref)
    row_ref[0:8] = coef_ref[LAT_C]
    row_ref[8:16] = coef_ref[LAT_G]
    for r in edge:
        big[r].wait()

    def tile(block):
        for r in edge:
            cells = [xt_ref[r, block, lanes_of(j)] for j in range(pieces)]
            faces = [
                [coef_ref[i, r : r + 1, lanes_of(j)] for j in range(1, pieces)] for i in (LON_C, LON_G)
            ]
            ref, row = (south_ref, r) if r < 2 else (north_ref, r - rows + 2)
            for j, value in enumerate(lon_sweep(cells, *faces)):
                ref[row, block, lanes_of(j)] = value

    tiles(species, tile)


def inner_kernel(
    x_ref, south_ref, north_ref, coef_ref, chem_ref, cnt_ref,
    mid_ref, done_ref, table_ref, xt_ref, sems,
):
    species, rows, width = x_ref.shape
    pieces = width // PIECE
    inner = range(2, rows - 2)
    copies = [pltpu.make_async_copy(x_ref.at[:, r, :], xt_ref.at[r - 2], sems.at[r - 2]) for r in inner]
    for copy in copies:
        copy.start()
    fill_table(chem_ref[3 * species + 1 : 3 * species + 2], table_ref)
    for copy in copies:
        copy.wait()

    def tile(block):
        for r in inner:
            cells = [xt_ref[r - 2, block, lanes_of(j)] for j in range(pieces)]
            faces = [
                [coef_ref[i, r : r + 1, lanes_of(j)] for j in range(1, pieces)] for i in (LON_C, LON_G)
            ]
            for j, value in enumerate(lon_sweep(cells, *faces)):
                mid_ref[r - 2, block, lanes_of(j)] = value

    tiles(species, tile)
    rates = rate_pieces(chem_ref, species)

    def block(at, lanes):
        here = pl.ds(at, lanes)
        own = pl.ds(at + PIECE if isinstance(at, int) else pl.multiple_of(at + PIECE, PIECE), lanes)
        column = 2 + at // LEVELS
        cells = (
            [south_ref[i, :, here] for i in (0, 1)]
            + [mid_ref[i, :, here] for i in range(rows - 4)]
            + [north_ref[i, :, here] for i in (0, 1)]
        )
        faces = [[coef_ref[i, f : f + 1, own] for f in range(2, rows - 1)] for i in (LAT_C, LAT_G)]
        done = column_block(
            lat_sweep(cells, *faces),
            [coef_ref[DAY, r : r + 1, own] for r in inner],
            lambda i, j: cnt_ref[2 + i, column + j],
            rates,
            chem_ref[2 * species : 3 * species],
            chem_ref[3 * species + 0 : 3 * species + 1],
            table_ref,
        )
        for i, row in enumerate(done):
            done_ref[i, :, here] = jnp.concatenate(row, 1)

    blocks(width - 2 * PIECE, block)


def side_kernel(
    xw_ref, xe_ref, hw_ref, he_ref, coef_ref, mid_ref, south_ref, north_ref, side_ref, cnt_ref
):
    rows, species = mid_ref.shape[:2]
    width = coef_ref.shape[2]
    base = rows * species
    for i in range(6):
        here = slice(base + i * rows, base + (i + 1) * rows)
        side_ref[i, :, lanes_of(0)] = hw_ref[here, lanes_of(1)]
        side_ref[i, :, lanes_of(1)] = coef_ref[i, :, 0:PIECE]
        side_ref[i, :, lanes_of(2)] = coef_ref[i, :, width - PIECE : width]
        side_ref[i, :, lanes_of(3)] = he_ref[here, lanes_of(0)]

    cnt_ref[...] = side_ref[COUNT].astype(jnp.int32)

    def tile(s, carry):
        for r in range(rows):
            row = slice(r, r + 1)
            from_row = pl.ds(pl.multiple_of(r * species + s * 8, 8), 8)
            block = pl.ds(pl.multiple_of(s * 8, 8), 8)
            faces = [
                [side_ref[i, row, lanes_of(0)], side_ref[i, row, lanes_of(1)], coef_ref[i, row, lanes_of(1)]]
                for i in (LON_C, LON_G)
            ]
            out = lon_sweep([ref[from_row, lanes_of(h)] for ref in (hw_ref, xw_ref) for h in (0, 1)], *faces)
            faces = [
                [
                    side_ref[i, row, lanes_of(2)],
                    side_ref[i, row, lanes_of(3)],
                    he_ref[base + i * rows + r : base + i * rows + r + 1, lanes_of(1)],
                ]
                for i in (LON_C, LON_G)
            ]
            out = out + lon_sweep([ref[from_row, lanes_of(h)] for ref in (xe_ref, he_ref) for h in (0, 1)], *faces)
            for j, value in enumerate(out):
                mid_ref[r, block, lanes_of(j)] = value
                if r < 2:
                    south_ref[pl.ds(pl.multiple_of(r * species + s * 8, 8), 8), lanes_of(j)] = value
                if r >= rows - 2:
                    north_ref[pl.ds(pl.multiple_of((r - rows + 2) * species + s * 8, 8), 8), lanes_of(j)] = value
        return carry

    lax.fori_loop(0, species // 8, tile, 0)
    for j in range(4):
        two = [side_ref[i, 0:1, lanes_of(j)] for i in (LAT_C, LAT_G)]
        south_ref[2 * species : 2 * species + 8, lanes_of(j)] = jnp.concatenate([two[0]] * 4 + [two[1]] * 4, 0)


def edge_kernel(
    side_ref, mid_ref, own_south_ref, own_north_ref, south_ref, north_ref, coef_ref, row_ref,
    chem_ref, table_ref, cnt_ref,
    done_ref, sent_south_ref, sent_north_ref,
):
    species, inner_width = mid_ref.shape[1:]
    rows = coef_ref.shape[1]
    rates = rate_pieces(chem_ref, species)
    edge = (0, 1, rows - 2, rows - 1)

    def block(at, lanes):
        here = pl.ds(at, lanes)
        own = pl.ds(at + PIECE if isinstance(at, int) else pl.multiple_of(at + PIECE, PIECE), lanes)
        column = 2 + at // LEVELS
        valid_south, valid_north = wide(chem_ref[3 * species + 2 : 3 * species + 3], lanes), wide(chem_ref[3 * species + 3 : 3 * species + 4], lanes)
        lower = (
            [south_ref[i, :, here] * valid_south for i in (0, 1)]
            + [own_south_ref[i, :, here] for i in (0, 1)]
            + [mid_ref[i, :, here] for i in (0, 1)]
        )
        upper = (
            [mid_ref[i, :, here] for i in (2, 3)]
            + [own_north_ref[i, :, here] for i in (0, 1)]
            + [north_ref[i, :, here] * valid_north for i in (0, 1)]
        )
        lower_faces = [
            [coef_ref[i, 0:1, own] * valid_south, coef_ref[i, 1:2, own], coef_ref[i, 2:3, own]]
            for i in (LAT_C, LAT_G)
        ]
        upper_faces = [
            [
                coef_ref[i, rows - 2 : rows - 1, own],
                coef_ref[i, rows - 1 : rows, own],
                row_ref[8 * (i - LAT_C) : 8 * (i - LAT_C) + 1, own] * valid_north,
            ]
            for i in (LAT_C, LAT_G)
        ]
        done = column_block(
            lat_sweep(lower, *lower_faces) + lat_sweep(upper, *upper_faces),
            [coef_ref[DAY, r : r + 1, own] for r in edge],
            lambda i, j: cnt_ref[edge[i], column + j],
            rates,
            chem_ref[2 * species : 3 * species],
            chem_ref[3 * species + 0 : 3 * species + 1],
            table_ref,
        )
        for i, row in enumerate(done):
            done_ref[i, :, here] = jnp.concatenate(row, 1)

    blocks(inner_width, block)
    pieces = inner_width // PIECE

    def tile(block):
        for k, r in enumerate(edge):
            cells = [done_ref[k, block, lanes_of(j)] for j in range(pieces)]
            faces = [
                [coef_ref[i, r : r + 1, lanes_of(j + 1)] for j in range(1, pieces)] for i in (LON_C, LON_G)
            ]
            ref = sent_south_ref if k < 2 else sent_north_ref
            for j, value in enumerate(lon_sweep(cells, *faces)):
                ref[k % 2, block, lanes_of(j)] = value

    tiles(species, tile)


def corner_kernel(
    mid_ref, south_ref, north_ref, edge_ref, coef_ref, side_ref,
    chem_ref, table_ref, cnt_ref,
    done_ref, sent_south_ref, sent_north_ref,
):
    rows, species, width = mid_ref.shape
    rates = rate_pieces(chem_ref, species)
    valid_south, valid_north = wide(chem_ref[3 * species + 2 : 3 * species + 3], width), wide(chem_ref[3 * species + 3 : 3 * species + 4], width)
    cells = (
        [south_ref[i * species : (i + 1) * species] * valid_south for i in (0, 1)]
        + [mid_ref[r] for r in range(rows)]
        + [north_ref[i * species : (i + 1) * species] * valid_north for i in (0, 1)]
    )
    faces = [
        [side_ref[i, 0:1] * valid_south]
        + [side_ref[i, r : r + 1] for r in range(1, rows)]
        + [north_ref[2 * species + 4 * (i - LAT_C) : 2 * species + 4 * (i - LAT_C) + 1] * valid_north]
        for i in (LAT_C, LAT_G)
    ]
    for r, q in enumerate(lat_sweep(cells, *faces)):
        done_ref[r] = q
    for part in (0, rows // 2):
        done = column_block(
            [done_ref[part + i] for i in range(rows // 2)],
            [side_ref[DAY, part + i : part + i + 1] for i in range(rows // 2)],
            lambda i, j: cnt_ref[part + i, LEVELS * j],
            rates,
            chem_ref[2 * species : 3 * species],
            chem_ref[3 * species + 0 : 3 * species + 1],
            table_ref,
        )
        for i, row in enumerate(done):
            done_ref[part + i] = jnp.concatenate(row, 1)
    last = edge_ref.shape[2] // PIECE

    def tile(block):
        for k, r in enumerate((0, 1, rows - 2, rows - 1)):
            row = slice(r, r + 1)
            ref = sent_south_ref if k < 2 else sent_north_ref
            out = corner_sweep(
                [done_ref[r, block, lanes_of(j)] for j in range(4)],
                [edge_ref[k, block, lanes_of(j)] for j in (0, 1, last - 2, last - 1)],
                row,
                coef_ref,
                side_ref,
            )
            for j, value in enumerate(out):
                ref[k % 2, block, lanes_of(j)] = value

    tiles(species, tile)


def rest_kernel(corner_ref, done_ref, south_ref, north_ref, coef_ref, swept_ref, out_ref):
    count, species, width = done_ref.shape
    pieces = width // PIECE

    def tile(block):
        for k in range(count):
            row = slice(k + 2, k + 3)
            cells = [done_ref[k, block, lanes_of(j)] for j in range(pieces)]
            faces = [[coef_ref[i, row, lanes_of(j + 1)] for j in range(1, pieces)] for i in (LON_C, LON_G)]
            for j, value in enumerate(lon_sweep(cells, *faces)):
                swept_ref[k, block, lanes_of(j)] = value

    tiles(species, tile)
    for j in range(pieces - 2):
        inner_lat(swept_ref, south_ref, north_ref, coef_ref, out_ref, j, j + 2)


def inner_lat(swept_ref, south_ref, north_ref, coef_ref, out_ref, j, own):
    count = swept_ref.shape[0]
    at = lanes_of(j)
    cells = (
        [south_ref[i, :, at] for i in (0, 1)]
        + [swept_ref[i, :, at] for i in range(count)]
        + [north_ref[i, :, at] for i in (0, 1)]
    )
    faces = [[coef_ref[i, f : f + 1, lanes_of(own)] for f in range(2, count + 3)] for i in (LAT_C, LAT_G)]
    for i, q in enumerate(lat_sweep(cells, *faces)):
        out_ref[i, :, at] = q


def rest_corner_kernel(done_ref, corner_ref, south_ref, north_ref, coef_ref, side_ref, swept_ref, out_ref):
    count, species, width = done_ref.shape
    last = width // PIECE
    total = coef_ref.shape[2] // PIECE

    def tile(block):
        for k in range(count):
            row = slice(k + 2, k + 3)
            out = corner_sweep(
                [corner_ref[k + 2, block, lanes_of(j)] for j in range(4)],
                [done_ref[k, block, lanes_of(j)] for j in (0, 1, last - 2, last - 1)],
                row,
                coef_ref,
                side_ref,
            )
            for j, value in enumerate(out):
                swept_ref[k, block, lanes_of(j)] = value

    tiles(species, tile)
    for j, own in enumerate((0, 1, total - 2, total - 1)):
        inner_lat(swept_ref, south_ref, north_ref, coef_ref, out_ref, j, own)


def corner_sweep(corner, inner, row, coef_ref, side_ref):
    total = coef_ref.shape[2] // PIECE
    faces = [[coef_ref[i, row, lanes_of(j)] for j in range(3)] for i in (LON_C, LON_G)]
    out = lon_sweep(corner[:2] + inner[:2], *faces)
    faces = [
        [coef_ref[i, row, lanes_of(j)] for j in (total - 2, total - 1)] + [side_ref[i, row, lanes_of(3)]]
        for i in (LON_C, LON_G)
    ]
    return out + lon_sweep(inner[2:] + corner[2:], *faces)


def edge_lat(swept, own_south, own_north, south, north, coef_ref, row_ref, chem_ref, out_ref, j, own):
    count, species = swept.shape[:2]
    rows = count + 4
    at, lanes = lanes_of(j), lanes_of(own)
    valid_south = chem_ref[3 * species + 2 : 3 * species + 3]
    valid_north = chem_ref[3 * species + 3 : 3 * species + 4]
    lower = (
        [south[i, :, at] * valid_south for i in (0, 1)]
        + [own_south[i, :, at] for i in (0, 1)]
        + [swept[i, :, at] for i in (0, 1)]
    )
    upper = (
        [swept[i, :, at] for i in (2, 3)]
        + [own_north[i, :, at] for i in (0, 1)]
        + [north[i, :, at] * valid_north for i in (0, 1)]
    )
    lower_faces = [
        [coef_ref[i, 0:1, lanes] * valid_south, coef_ref[i, 1:2, lanes], coef_ref[i, 2:3, lanes]]
        for i in (LAT_C, LAT_G)
    ]
    upper_faces = [
        [
            coef_ref[i, rows - 2 : rows - 1, lanes],
            coef_ref[i, rows - 1 : rows, lanes],
            row_ref[8 * (i - LAT_C) : 8 * (i - LAT_C) + 1, lanes] * valid_north,
        ]
        for i in (LAT_C, LAT_G)
    ]
    for k, q in enumerate(lat_sweep(lower, *lower_faces) + lat_sweep(upper, *upper_faces)):
        out_ref[k, :, at] = q


def edge_last_kernel(
    inner_c, swept, own_south, own_north, south, north, coef_ref, row_ref, chem_ref, out_ref
):
    for j in range(swept.shape[2] // PIECE):
        edge_lat(swept, own_south, own_north, south, north, coef_ref, row_ref, chem_ref, out_ref, j, j + 2)


def last_kernel(
    inner_a, inner_c, edge_a, swept, own_south, own_north, south, north, coef_ref, row_ref, chem_ref,
    out_ref, edge_c, sems,
):
    count, species, main = inner_a.shape
    width = coef_ref.shape[2]
    rows = count + 4
    pieces = width // PIECE
    two = 2 * PIECE

    def copies(array, row, source, first):
        return [
            pltpu.make_async_copy(array.at[source, :, 0:two], out_ref.at[:, row, 0:two], sems.at[first]),
            pltpu.make_async_copy(
                array.at[source, :, two : 2 * two], out_ref.at[:, row, width - two : width], sems.at[first + 1]
            ),
        ]

    started = []
    edge = (0, 1, rows - 2, rows - 1)
    for i in range(count):
        started.append(pltpu.make_async_copy(inner_a.at[i], out_ref.at[:, i + 2, two : two + main], sems.at[i]))
        started.append(
            pltpu.make_async_copy(edge_a.at[i], out_ref.at[:, edge[i], two : two + main], sems.at[count + i])
        )
        started += copies(inner_c, i + 2, i, 2 * count + 2 * i)
    for copy in started:
        copy.start()
    for j, own in enumerate((0, 1, pieces - 2, pieces - 1)):
        edge_lat(swept, own_south, own_north, south, north, coef_ref, row_ref, chem_ref, edge_c, j, own)
    more = []
    for k, r in enumerate(edge):
        more += copies(edge_c, r, k, 4 * count + 2 * k)
    for copy in more:
        copy.start()
    for copy in started + more:
        copy.wait()


def shards(
    tracers,
    courant,
    switches,
    day_flags,
    diffusion_counts,
    night_rates,
    photo_rates,
    level_light,
    self_loss,
    vertical_mixing,
):
    species, rows, width = tracers.shape
    inner = width - 2 * PIECE
    two = 2 * PIECE
    four = 4 * PIECE
    message = (rows * species + 6 * rows, two)

    columns = [
        pltpu.VMEM(courant.shape, F32),
        pltpu.VMEM(switches.shape, jnp.int32),
        pltpu.VMEM(day_flags.shape, jnp.int32),
        pltpu.VMEM(diffusion_counts.shape, jnp.int32),
    ]
    west, east = call(
        start_kernel,
        [message, message],
        [FAR] * 5,
        tracers,
        courant,
        switches,
        day_flags,
        diffusion_counts,
        scratch=[pltpu.VMEM((species, rows, four), F32)] + columns + [pltpu.SemaphoreType.DMA((6,))],
        cost=2,
        limit=VMEM_ALL,
    )
    halo_west = ring(east, "lon", 1)
    halo_east = ring(west, "lon", -1)
    own_south, own_north, coef, own_row, chem = call(
        first_kernel,
        [(2, species, inner), (2, species, inner), (6, rows, width), (16, width), (3 * species + 8, PIECE)],
        [FAR] * 11,
        west,
        tracers,
        courant,
        switches,
        day_flags,
        diffusion_counts,
        night_rates,
        photo_rates,
        level_light[None],
        self_loss[None],
        vertical_mixing[None],
        scratch=[
            pltpu.VMEM((rows, species, width), F32),
            *columns,
            pltpu.VMEM(night_rates.shape, F32),
            pltpu.VMEM(photo_rates.shape, F32),
            pltpu.VMEM((1,) + level_light.shape, F32),
            pltpu.VMEM((1,) + self_loss.shape, F32),
            pltpu.VMEM((1,) + vertical_mixing.shape, F32),
            pltpu.SemaphoreType.DMA((rows,)),
            pltpu.SemaphoreType.DMA((9,)),
        ],
        cost=3,
        limit=VMEM_ALL,
    )
    south = ring(own_north, "lat", 1)
    north = ring(own_south, "lat", -1)
    row = ring(own_row, "lat", -1)

    mid, done, table = call(
        inner_kernel,
        [
            (rows - 4, species, inner),
            (rows - 4, species, inner),
            jax.ShapeDtypeStruct((2, KMAX, 2, HALF, PIECE), BF16),
        ],
        [FAR] + [WHOLE] * 4 + [SCALARS],
        tracers,
        own_south,
        own_north,
        coef,
        chem,
        diffusion_counts,
        scratch=[pltpu.VMEM((rows - 4, species, width), F32), pltpu.SemaphoreType.DMA((rows - 4,))],
        cost=9,
        limit=VMEM_ALL,
    )
    mid_side, side_south, side_north, side, counts = call(
        side_kernel,
        [(rows, species, four), (2 * species + 8, four), (2 * species, four), (6, rows, four), jax.ShapeDtypeStruct((rows, four), jnp.int32)],
        [WHOLE] * 5,
        west,
        east,
        halo_west,
        halo_east,
        coef,
        cost=3,
    )
    side_from_south = ring(side_north, "lat", 1)
    side_from_north = ring(side_south, "lat", -1)
    edge_done, main_south, main_north = call(
        edge_kernel,
        [(4, species, inner), (2, species, inner - two), (2, species, inner - two)],
        [FAR] + [WHOLE] * 9 + [SCALARS],
        side,
        mid,
        own_south,
        own_north,
        south,
        north,
        coef,
        row,
        chem,
        table,
        diffusion_counts,
        cost=9,
    )
    main_from_south = ring(main_north, "lat", 1)
    main_from_north = ring(main_south, "lat", -1)
    corner, corner_south, corner_north = call(
        corner_kernel,
        [(rows, species, four), (2, species, four), (2, species, four)],
        [WHOLE] * 8 + [SCALARS],
        mid_side,
        side_from_south,
        side_from_north,
        edge_done,
        coef,
        side,
        chem,
        table,
        counts,
        cost=5,
    )
    corner_from_south = ring(corner_north, "lat", 1)
    corner_from_north = ring(corner_south, "lat", -1)
    swept_main, main_out = call(
        rest_kernel,
        [(rows - 4, species, inner - two)] * 2,
        [FAR] + [WHOLE] * 4,
        corner_south,
        done,
        main_south,
        main_north,
        coef,
        cost=0.1,
    )
    swept_corner, corner_out = call(
        rest_corner_kernel,
        [(rows - 4, species, four)] * 2,
        [WHOLE] * 6,
        done,
        corner,
        corner_south,
        corner_north,
        coef,
        side,
        cost=0.1,
    )
    (edge_out,) = call(
        edge_last_kernel,
        [(4, species, inner - two)],
        [FAR] + [WHOLE] * 8,
        corner_out,
        swept_main,
        main_south,
        main_north,
        main_from_south,
        main_from_north,
        coef,
        row,
        chem,
        cost=0.5,
    )
    (out,) = call(
        last_kernel,
        [(species, rows, width)],
        [WHOLE] * 11,
        main_out,
        corner_out,
        edge_out,
        swept_corner,
        corner_south,
        corner_north,
        corner_from_south,
        corner_from_north,
        coef,
        row,
        chem,
        scratch=[pltpu.VMEM((4, species, four), F32), pltpu.SemaphoreType.DMA((3 * rows,))],
        out_specs=[FAR],
        cost=3,
    )
    return out


def solution(mesh):
    in_specs = (
        P(None, "lat", "lon"),
        P(None, "lat", "lon"),
        P(None, "lat", "lon"),
        P("lat", "lon"),
        P("lat", "lon"),
        P(),
        P(),
        P(),
        P(),
        P(),
    )
    out_specs = P(None, "lat", "lon")
    return jax.shard_map(shards, mesh=mesh, in_specs=in_specs, out_specs=out_specs, check_vma=False)
```

```python
import jax
import jax.numpy as jnp
from jax import lax
from jax.experimental import pallas as pl
from jax.experimental.pallas import tpu as pltpu
from jax.sharding import PartitionSpec as P

CHEM = 6
KMAX = 8
PIECE = 128
HALF = 64
LEVELS = 64
VMEM_LIMIT = 24 * 1024 * 1024
VMEM_ALL = 60 * 1024 * 1024
F32 = jnp.float32
BF16 = jnp.bfloat16
LON_C, LON_G, LAT_C, LAT_G, DAY, COUNT = range(6)


def ring(value, axis, steps):
    count = lax.axis_size(axis)
    return lax.ppermute(value, axis, [(i, (i + steps) % count) for i in range(count)])


def half_roll(value):
    return pltpu.roll(value, HALF, 1)


def minmod(x, y):
    return jnp.minimum(jnp.maximum(x, jnp.minimum(y, 0.0)), jnp.maximum(y, 0.0))


def gain(cour, switch):
    return 0.5 * cour * switch * jnp.where(cour >= 0.0, 1.0 - cour, -1.0 - cour)


def lon_sweep(cells, cours, gains):
    n = len(cells)
    low = lax.broadcasted_iota(jnp.int32, cells[0].shape, 1) < HALF
    turned = [half_roll(q) for q in cells]
    flux = [None]
    for i in range(1, n):
        west = jnp.where(low, turned[i - 1], turned[i])
        east = jnp.where(low, turned[i], turned[i + 1]) if i < n - 1 else turned[i]
        step = cells[i] - west
        slope = minmod(step, east - cells[i])
        behind = minmod(west - cells[i - 1], step)
        forward = cours[i - 1] >= 0.0
        flux.append(
            cours[i - 1] * jnp.where(forward, west, cells[i])
            + gains[i - 1] * jnp.where(forward, behind, slope)
        )
    turned = [None] + [half_roll(f) for f in flux[1:]]
    return [
        cells[i] - (jnp.where(low, turned[i], turned[i + 1]) - flux[i]) for i in range(1, n - 1)
    ]


def lat_sweep(rows, cours, gains):
    n = len(rows) - 4
    step = [rows[i + 1] - rows[i] for i in range(n + 3)]
    slope = [minmod(step[i], step[i + 1]) for i in range(n + 2)]
    flux = []
    for i in range(n + 1):
        forward = cours[i] >= 0.0
        flux.append(
            cours[i] * jnp.where(forward, rows[i + 1], rows[i + 2])
            + gains[i] * jnp.where(forward, slope[i], slope[i + 1])
        )
    return [rows[i + 2] - (flux[i + 1] - flux[i]) for i in range(n)]


def expand(compact, first):
    rows = compact.shape[0]
    low = lax.broadcasted_iota(jnp.int32, (rows, PIECE), 1) < HALF
    left = jnp.broadcast_to(compact[:, first : first + 1], (rows, PIECE))
    right = jnp.broadcast_to(compact[:, first + 1 : first + 2], (rows, PIECE))
    return jnp.where(low, left, right)


def rate_pieces(chem_ref, species):
    square = (2 * species, species)
    own = lax.broadcasted_iota(jnp.int32, square, 0) == lax.broadcasted_iota(jnp.int32, square, 1)
    rates = chem_ref[0 : 2 * species, 0:species] + jnp.where(own, 1.0, 0.0)
    high = rates.astype(BF16)
    low = (rates - high.astype(F32)).astype(BF16)
    return jnp.concatenate([high, high, low], 1)


def react(rows, suns, rates, loss):
    species = rows[0].shape[0]
    for _ in range(CHEM):
        nexts = []
        for q, sun in zip(rows, suns):
            high = q.astype(BF16)
            low = (q - high.astype(F32)).astype(BF16)
            both = jnp.dot(
                rates, jnp.concatenate([high, low, high], 0), preferred_element_type=F32
            )
            top = both[:species] + sun * both[species:]
            nexts.append(top * pl.reciprocal(1.0 + loss * q * q, approx=True))
        rows = nexts
    return rows


def fill_table(mixing, table_ref):
    shape = (HALF, PIECE)
    lane = lax.broadcasted_iota(jnp.int32, shape, 1)
    low = lane < HALF
    q = jnp.where((lane & (HALF - 1)) == lax.broadcasted_iota(jnp.int32, shape, 0), 1.0, 0.0)
    for n in range(KMAX):
        flux = mixing * (pltpu.roll(q, PIECE - 1, 1) - q)
        q = q + flux - pltpu.roll(flux, 1, 1)
        high = q.astype(BF16).astype(F32)
        for i, term in enumerate((high, q - high)):
            table_ref[0, n, i] = jnp.where(low, term, 0.0).astype(BF16)
            table_ref[1, n, i] = jnp.where(low, 0.0, term).astype(BF16)


def diffuse(q, first, second, table_ref):
    species = q.shape[0]
    high = q.astype(BF16)
    low = (q - high.astype(F32)).astype(BF16)
    state = jnp.concatenate(
        [jnp.concatenate([high, high], 1), jnp.concatenate([low, low], 1)], 0
    )
    powers = jnp.concatenate(
        [table_ref[0, first - 1, i] if side == 0 else table_ref[1, second - 1, i] for i in (0, 1) for side in (0, 1)], 0
    )
    both = jnp.dot(state, powers, preferred_element_type=F32)
    return both[:species] + both[species:]


def column_block(rows, days, counts, rates, loss, level, table_ref):
    pieces = rows[0].shape[1] // PIECE
    level = jnp.concatenate([level] * pieces, 1)
    loss = jnp.concatenate([loss] * pieces, 1)
    rows = react(rows, [day * level for day in days], rates, loss)
    return [
        [
            diffuse(q[:, j * PIECE : (j + 1) * PIECE], counts(i, 2 * j), counts(i, 2 * j + 1), table_ref)
            for j in range(pieces)
        ]
        for i, q in enumerate(rows)
    ]


WHOLE = pl.BlockSpec(memory_space=pltpu.VMEM)
SCALARS = pl.BlockSpec(memory_space=pltpu.SMEM)
FAR = pl.BlockSpec(memory_space=pl.ANY)
BLOCK = 7 * PIECE


def call(kernel, outs, ins, *args, scratch=(), out_specs=None, cost=10.0, limit=VMEM_LIMIT):
    return pl.pallas_call(
        kernel,
        out_shape=[s if isinstance(s, jax.ShapeDtypeStruct) else jax.ShapeDtypeStruct(s, F32) for s in outs],
        in_specs=ins,
        out_specs=out_specs or [WHOLE] * len(outs),
        scratch_shapes=list(scratch),
        compiler_params=pltpu.CompilerParams(vmem_limit_bytes=limit),
        cost_estimate=pl.CostEstimate(flops=int(cost * 1.0e9), bytes_accessed=int(cost * 3.0e6), transcendentals=0),
    )(*args)


def lanes_of(j, count=1):
    return slice(j * PIECE, (j + count) * PIECE)


def blocks(width, body):
    full = width // BLOCK

    def step(b, carry):
        body(pl.multiple_of(b * BLOCK, BLOCK), BLOCK)
        return carry

    if full:
        lax.fori_loop(0, full, step, 0)
    if width % BLOCK:
        body(full * BLOCK, width % BLOCK)


def tiles(species, body):
    def step(s, carry):
        body(pl.ds(pl.multiple_of(s * 8, 8), 8))
        return carry

    lax.fori_loop(0, species // 8, step, 0)


def wide(row, lanes):
    return jnp.concatenate([row] * (lanes // PIECE), 1)


def fill_chem(night_ref, photo_ref, level_ref, loss_ref, mixing_ref, chem_ref):
    species = night_ref.shape[0]
    chem_ref[0:species, 0:species] = night_ref[...]
    chem_ref[species : 2 * species, 0:species] = photo_ref[...]
    square = (species, species)
    own = lax.broadcasted_iota(jnp.int32, square, 0) == lax.broadcasted_iota(jnp.int32, square, 1)
    loss = jnp.sum(jnp.where(own, loss_ref[...], 0.0), axis=1, keepdims=True)
    chem_ref[2 * species : 3 * species] = jnp.broadcast_to(loss, (species, PIECE))
    at = 3 * species
    chem_ref[at : at + 8] = jnp.zeros((8, PIECE), F32)
    for i, ref in enumerate((level_ref, mixing_ref)):
        row = slice(at + i, at + i + 1)
        chem_ref[row, 0 : ref.shape[1]] = ref[...]
        low = lax.broadcasted_iota(jnp.int32, (1, PIECE), 1) < HALF
        value = chem_ref[row]
        chem_ref[row] = jnp.where(low, value, half_roll(value))
    lat = lax.axis_index("lat")
    for i, there in ((2, lat > 0), (3, lat < lax.axis_size("lat") - 1)):
        chem_ref[at + i : at + i + 1] = jnp.where(there, 1.0, 0.0) * jnp.ones((1, PIECE), F32)


def face_fields(cour_ref, sw_ref, day_ref, cnt_ref):
    cour = [cour_ref[0], cour_ref[1]]
    switch = [sw_ref[0].astype(F32), sw_ref[1].astype(F32)]
    return [
        cour[0],
        gain(cour[0], switch[0]),
        cour[1],
        gain(cour[1], switch[1]),
        day_ref[...].astype(F32),
        cnt_ref[...].astype(F32),
    ]


def start_kernel(
    x_ref, cour_in, sw_in, day_in, cnt_in, west_ref, east_ref, sides_ref, cour_ref, sw_ref, day_ref, cnt_ref, sems
):
    species, rows, width = x_ref.shape
    two = 2 * PIECE
    copies = [
        pltpu.make_async_copy(a, b, sems.at[i])
        for i, (a, b) in enumerate(
            (
                (cour_in, cour_ref),
                (sw_in, sw_ref),
                (day_in, day_ref),
                (cnt_in, cnt_ref),
                (x_ref.at[:, :, 0:two], sides_ref.at[:, :, 0:two]),
                (x_ref.at[:, :, width - two : width], sides_ref.at[:, :, two : 2 * two]),
            )
        )
    ]
    for copy in copies:
        copy.start()
    for copy in copies[:4]:
        copy.wait()
    fields = face_fields(cour_ref, sw_ref, day_ref, cnt_ref)
    columns = cour_ref.shape[2]
    for ref, first in ((west_ref, 0), (east_ref, columns - 4)):
        for i, field in enumerate(fields):
            at = rows * species + i * rows
            for half in (0, 1):
                ref[at : at + rows, lanes_of(half)] = expand(field, first + 2 * half)
    for copy in copies[4:]:
        copy.wait()
    for j, ref in enumerate((west_ref, east_ref)):
        for r in range(rows):
            ref[r * species : (r + 1) * species] = sides_ref[:, r, lanes_of(2 * j, 2)]


def first_kernel(
    west_ref, x_ref, cour_in, sw_in, day_in, cnt_in, night_in, photo_in, level_in, loss_in, mixing_in,
    south_ref, north_ref, coef_ref, row_ref, chem_ref,
    xt_ref, cour_ref, sw_ref, day_ref, cnt_ref, night_ref, photo_ref, level_ref, loss_ref, mixing_ref,
    row_sems, sems,
):
    rows, species, width = xt_ref.shape
    pieces = width // PIECE
    edge = (0, 1, rows - 2, rows - 1)
    small = [
        pltpu.make_async_copy(a, b, sems.at[i])
        for i, (a, b) in enumerate(
            (
                (cour_in, cour_ref),
                (sw_in, sw_ref),
                (day_in, day_ref),
                (cnt_in, cnt_ref),
                (night_in, night_ref),
                (photo_in, photo_ref),
                (level_in, level_ref),
                (loss_in, loss_ref),
                (mixing_in, mixing_ref),
            )
        )
    ]
    big = {r: pltpu.make_async_copy(x_ref.at[:, r, :], xt_ref.at[r], row_sems.at[r]) for r in edge}
    for copy in small:
        copy.start()
    for copy in big.values():
        copy.start()
    for copy in small:
        copy.wait()
    fields = face_fields(cour_ref, sw_ref, day_ref, cnt_ref)
    for i, field in enumerate(fields):
        for j in range(pieces):
            coef_ref[i, :, lanes_of(j)] = expand(field, 2 * j)
    fill_chem(night_ref, photo_ref, level_ref, loss_ref, mixing_ref, chem_ref)
    row_ref[0:8] = coef_ref[LAT_C]
    row_ref[8:16] = coef_ref[LAT_G]
    for r in edge:
        big[r].wait()

    def tile(block):
        for r in edge:
            cells = [xt_ref[r, block, lanes_of(j)] for j in range(pieces)]
            faces = [
                [coef_ref[i, r : r + 1, lanes_of(j)] for j in range(1, pieces)] for i in (LON_C, LON_G)
            ]
            ref, row = (south_ref, r) if r < 2 else (north_ref, r - rows + 2)
            for j, value in enumerate(lon_sweep(cells, *faces)):
                ref[row, block, lanes_of(j)] = value

    tiles(species, tile)


def inner_kernel(
    x_ref, south_ref, north_ref, coef_ref, chem_ref, cnt_ref,
    mid_ref, done_ref, table_ref, xt_ref, sems,
):
    species, rows, width = x_ref.shape
    pieces = width // PIECE
    inner = range(2, rows - 2)
    copies = [pltpu.make_async_copy(x_ref.at[:, r, :], xt_ref.at[r - 2], sems.at[r - 2]) for r in inner]
    for copy in copies:
        copy.start()
    fill_table(chem_ref[3 * species + 1 : 3 * species + 2], table_ref)
    for copy in copies:
        copy.wait()

    def tile(block):
        for r in inner:
            cells = [xt_ref[r - 2, block, lanes_of(j)] for j in range(pieces)]
            faces = [
                [coef_ref[i, r : r + 1, lanes_of(j)] for j in range(1, pieces)] for i in (LON_C, LON_G)
            ]
            for j, value in enumerate(lon_sweep(cells, *faces)):
                mid_ref[r - 2, block, lanes_of(j)] = value

    tiles(species, tile)
    rates = rate_pieces(chem_ref, species)

    def block(at, lanes):
        here = pl.ds(at, lanes)
        own = pl.ds(at + PIECE if isinstance(at, int) else pl.multiple_of(at + PIECE, PIECE), lanes)
        column = 2 + at // LEVELS
        cells = (
            [south_ref[i, :, here] for i in (0, 1)]
            + [mid_ref[i, :, here] for i in range(rows - 4)]
            + [north_ref[i, :, here] for i in (0, 1)]
        )
        faces = [[coef_ref[i, f : f + 1, own] for f in range(2, rows - 1)] for i in (LAT_C, LAT_G)]
        done = column_block(
            lat_sweep(cells, *faces),
            [coef_ref[DAY, r : r + 1, own] for r in inner],
            lambda i, j: cnt_ref[2 + i, column + j],
            rates,
            chem_ref[2 * species : 3 * species],
            chem_ref[3 * species + 0 : 3 * species + 1],
            table_ref,
        )
        for i, row in enumerate(done):
            done_ref[i, :, here] = jnp.concatenate(row, 1)

    blocks(width - 2 * PIECE, block)


def side_kernel(
    xw_ref, xe_ref, hw_ref, he_ref, coef_ref, mid_ref, south_ref, north_ref, side_ref, cnt_ref
):
    rows, species = mid_ref.shape[:2]
    width = coef_ref.shape[2]
    base = rows * species
    for i in range(6):
        here = slice(base + i * rows, base + (i + 1) * rows)
        side_ref[i, :, lanes_of(0)] = hw_ref[here, lanes_of(1)]
        side_ref[i, :, lanes_of(1)] = coef_ref[i, :, 0:PIECE]
        side_ref[i, :, lanes_of(2)] = coef_ref[i, :, width - PIECE : width]
        side_ref[i, :, lanes_of(3)] = he_ref[here, lanes_of(0)]

    cnt_ref[...] = side_ref[COUNT].astype(jnp.int32)

    def tile(s, carry):
        for r in range(rows):
            row = slice(r, r + 1)
            from_row = pl.ds(pl.multiple_of(r * species + s * 8, 8), 8)
            block = pl.ds(pl.multiple_of(s * 8, 8), 8)
            faces = [
                [side_ref[i, row, lanes_of(0)], side_ref[i, row, lanes_of(1)], coef_ref[i, row, lanes_of(1)]]
                for i in (LON_C, LON_G)
            ]
            out = lon_sweep([ref[from_row, lanes_of(h)] for ref in (hw_ref, xw_ref) for h in (0, 1)], *faces)
            faces = [
                [
                    side_ref[i, row, lanes_of(2)],
                    side_ref[i, row, lanes_of(3)],
                    he_ref[base + i * rows + r : base + i * rows + r + 1, lanes_of(1)],
                ]
                for i in (LON_C, LON_G)
            ]
            out = out + lon_sweep([ref[from_row, lanes_of(h)] for ref in (xe_ref, he_ref) for h in (0, 1)], *faces)
            for j, value in enumerate(out):
                mid_ref[r, block, lanes_of(j)] = value
                if r < 2:
                    south_ref[pl.ds(pl.multiple_of(r * species + s * 8, 8), 8), lanes_of(j)] = value
                if r >= rows - 2:
                    north_ref[pl.ds(pl.multiple_of((r - rows + 2) * species + s * 8, 8), 8), lanes_of(j)] = value
        return carry

    lax.fori_loop(0, species // 8, tile, 0)
    for j in range(4):
        two = [side_ref[i, 0:1, lanes_of(j)] for i in (LAT_C, LAT_G)]
        south_ref[2 * species : 2 * species + 8, lanes_of(j)] = jnp.concatenate([two[0]] * 4 + [two[1]] * 4, 0)


def edge_kernel(
    side_ref, mid_ref, own_south_ref, own_north_ref, south_ref, north_ref, coef_ref, row_ref,
    chem_ref, table_ref, cnt_ref,
    done_ref, sent_south_ref, sent_north_ref,
):
    species, inner_width = mid_ref.shape[1:]
    rows = coef_ref.shape[1]
    rates = rate_pieces(chem_ref, species)
    edge = (0, 1, rows - 2, rows - 1)

    def block(at, lanes):
        here = pl.ds(at, lanes)
        own = pl.ds(at + PIECE if isinstance(at, int) else pl.multiple_of(at + PIECE, PIECE), lanes)
        column = 2 + at // LEVELS
        valid_south, valid_north = wide(chem_ref[3 * species + 2 : 3 * species + 3], lanes), wide(chem_ref[3 * species + 3 : 3 * species + 4], lanes)
        lower = (
            [south_ref[i, :, here] * valid_south for i in (0, 1)]
            + [own_south_ref[i, :, here] for i in (0, 1)]
            + [mid_ref[i, :, here] for i in (0, 1)]
        )
        upper = (
            [mid_ref[i, :, here] for i in (2, 3)]
            + [own_north_ref[i, :, here] for i in (0, 1)]
            + [north_ref[i, :, here] * valid_north for i in (0, 1)]
        )
        lower_faces = [
            [coef_ref[i, 0:1, own] * valid_south, coef_ref[i, 1:2, own], coef_ref[i, 2:3, own]]
            for i in (LAT_C, LAT_G)
        ]
        upper_faces = [
            [
                coef_ref[i, rows - 2 : rows - 1, own],
                coef_ref[i, rows - 1 : rows, own],
                row_ref[8 * (i - LAT_C) : 8 * (i - LAT_C) + 1, own] * valid_north,
            ]
            for i in (LAT_C, LAT_G)
        ]
        done = column_block(
            lat_sweep(lower, *lower_faces) + lat_sweep(upper, *upper_faces),
            [coef_ref[DAY, r : r + 1, own] for r in edge],
            lambda i, j: cnt_ref[edge[i], column + j],
            rates,
            chem_ref[2 * species : 3 * species],
            chem_ref[3 * species + 0 : 3 * species + 1],
            table_ref,
        )
        for i, row in enumerate(done):
            done_ref[i, :, here] = jnp.concatenate(row, 1)

    blocks(inner_width, block)
    pieces = inner_width // PIECE

    def tile(block):
        for k, r in enumerate(edge):
            cells = [done_ref[k, block, lanes_of(j)] for j in range(pieces)]
            faces = [
                [coef_ref[i, r : r + 1, lanes_of(j + 1)] for j in range(1, pieces)] for i in (LON_C, LON_G)
            ]
            ref = sent_south_ref if k < 2 else sent_north_ref
            for j, value in enumerate(lon_sweep(cells, *faces)):
                ref[k % 2, block, lanes_of(j)] = value

    tiles(species, tile)


def corner_kernel(
    mid_ref, south_ref, north_ref, edge_ref, coef_ref, side_ref,
    chem_ref, table_ref, cnt_ref,
    done_ref, sent_south_ref, sent_north_ref,
):
    rows, species, width = mid_ref.shape
    rates = rate_pieces(chem_ref, species)
    valid_south, valid_north = wide(chem_ref[3 * species + 2 : 3 * species + 3], width), wide(chem_ref[3 * species + 3 : 3 * species + 4], width)
    cells = (
        [south_ref[i * species : (i + 1) * species] * valid_south for i in (0, 1)]
        + [mid_ref[r] for r in range(rows)]
        + [north_ref[i * species : (i + 1) * species] * valid_north for i in (0, 1)]
    )
    faces = [
        [side_ref[i, 0:1] * valid_south]
        + [side_ref[i, r : r + 1] for r in range(1, rows)]
        + [north_ref[2 * species + 4 * (i - LAT_C) : 2 * species + 4 * (i - LAT_C) + 1] * valid_north]
        for i in (LAT_C, LAT_G)
    ]
    for r, q in enumerate(lat_sweep(cells, *faces)):
        done_ref[r] = q
    for part in (0, rows // 2):
        done = column_block(
            [done_ref[part + i] for i in range(rows // 2)],
            [side_ref[DAY, part + i : part + i + 1] for i in range(rows // 2)],
            lambda i, j: cnt_ref[part + i, LEVELS * j],
            rates,
            chem_ref[2 * species : 3 * species],
            chem_ref[3 * species + 0 : 3 * species + 1],
            table_ref,
        )
        for i, row in enumerate(done):
            done_ref[part + i] = jnp.concatenate(row, 1)
    last = edge_ref.shape[2] // PIECE

    def tile(block):
        for k, r in enumerate((0, 1, rows - 2, rows - 1)):
            row = slice(r, r + 1)
            ref = sent_south_ref if k < 2 else sent_north_ref
            out = corner_sweep(
                [done_ref[r, block, lanes_of(j)] for j in range(4)],
                [edge_ref[k, block, lanes_of(j)] for j in (0, 1, last - 2, last - 1)],
                row,
                coef_ref,
                side_ref,
            )
            for j, value in enumerate(out):
                ref[k % 2, block, lanes_of(j)] = value

    tiles(species, tile)


def rest_kernel(corner_ref, done_ref, south_ref, north_ref, coef_ref, swept_ref, out_ref):
    count, species, width = done_ref.shape
    pieces = width // PIECE

    def tile(block):
        for k in range(count):
            row = slice(k + 2, k + 3)
            cells = [done_ref[k, block, lanes_of(j)] for j in range(pieces)]
            faces = [[coef_ref[i, row, lanes_of(j + 1)] for j in range(1, pieces)] for i in (LON_C, LON_G)]
            for j, value in enumerate(lon_sweep(cells, *faces)):
                swept_ref[k, block, lanes_of(j)] = value

    tiles(species, tile)
    for j in range(pieces - 2):
        inner_lat(swept_ref, south_ref, north_ref, coef_ref, out_ref, j, j + 2)


def inner_lat(swept_ref, south_ref, north_ref, coef_ref, out_ref, j, own):
    count = swept_ref.shape[0]
    at = lanes_of(j)
    cells = (
        [south_ref[i, :, at] for i in (0, 1)]
        + [swept_ref[i, :, at] for i in range(count)]
        + [north_ref[i, :, at] for i in (0, 1)]
    )
    faces = [[coef_ref[i, f : f + 1, lanes_of(own)] for f in range(2, count + 3)] for i in (LAT_C, LAT_G)]
    for i, q in enumerate(lat_sweep(cells, *faces)):
        out_ref[i, :, at] = q


def rest_corner_kernel(done_ref, corner_ref, south_ref, north_ref, coef_ref, side_ref, swept_ref, out_ref):
    count, species, width = done_ref.shape
    last = width // PIECE
    total = coef_ref.shape[2] // PIECE

    def tile(block):
        for k in range(count):
            row = slice(k + 2, k + 3)
            out = corner_sweep(
                [corner_ref[k + 2, block, lanes_of(j)] for j in range(4)],
                [done_ref[k, block, lanes_of(j)] for j in (0, 1, last - 2, last - 1)],
                row,
                coef_ref,
                side_ref,
            )
            for j, value in enumerate(out):
                swept_ref[k, block, lanes_of(j)] = value

    tiles(species, tile)
    for j, own in enumerate((0, 1, total - 2, total - 1)):
        inner_lat(swept_ref, south_ref, north_ref, coef_ref, out_ref, j, own)


def corner_sweep(corner, inner, row, coef_ref, side_ref):
    total = coef_ref.shape[2] // PIECE
    faces = [[coef_ref[i, row, lanes_of(j)] for j in range(3)] for i in (LON_C, LON_G)]
    out = lon_sweep(corner[:2] + inner[:2], *faces)
    faces = [
        [coef_ref[i, row, lanes_of(j)] for j in (total - 2, total - 1)] + [side_ref[i, row, lanes_of(3)]]
        for i in (LON_C, LON_G)
    ]
    return out + lon_sweep(inner[2:] + corner[2:], *faces)


def edge_lat(swept, own_south, own_north, south, north, coef_ref, row_ref, chem_ref, out_ref, j, own):
    count, species = swept.shape[:2]
    rows = count + 4
    at, lanes = lanes_of(j), lanes_of(own)
    valid_south = chem_ref[3 * species + 2 : 3 * species + 3]
    valid_north = chem_ref[3 * species + 3 : 3 * species + 4]
    lower = (
        [south[i, :, at] * valid_south for i in (0, 1)]
        + [own_south[i, :, at] for i in (0, 1)]
        + [swept[i, :, at] for i in (0, 1)]
    )
    upper = (
        [swept[i, :, at] for i in (2, 3)]
        + [own_north[i, :, at] for i in (0, 1)]
        + [north[i, :, at] * valid_north for i in (0, 1)]
    )
    lower_faces = [
        [coef_ref[i, 0:1, lanes] * valid_south, coef_ref[i, 1:2, lanes], coef_ref[i, 2:3, lanes]]
        for i in (LAT_C, LAT_G)
    ]
    upper_faces = [
        [
            coef_ref[i, rows - 2 : rows - 1, lanes],
            coef_ref[i, rows - 1 : rows, lanes],
            row_ref[8 * (i - LAT_C) : 8 * (i - LAT_C) + 1, lanes] * valid_north,
        ]
        for i in (LAT_C, LAT_G)
    ]
    for k, q in enumerate(lat_sweep(lower, *lower_faces) + lat_sweep(upper, *upper_faces)):
        out_ref[k, :, at] = q


def edge_last_kernel(
    inner_c, swept, own_south, own_north, south, north, coef_ref, row_ref, chem_ref, out_ref
):
    for j in range(swept.shape[2] // PIECE):
        edge_lat(swept, own_south, own_north, south, north, coef_ref, row_ref, chem_ref, out_ref, j, j + 2)


def last_kernel(
    inner_a, inner_c, edge_a, swept, own_south, own_north, south, north, coef_ref, row_ref, chem_ref,
    out_ref, edge_c, sems,
):
    count, species, main = inner_a.shape
    width = coef_ref.shape[2]
    rows = count + 4
    pieces = width // PIECE
    two = 2 * PIECE

    def copies(array, row, source, first):
        return [
            pltpu.make_async_copy(array.at[source, :, 0:two], out_ref.at[:, row, 0:two], sems.at[first]),
            pltpu.make_async_copy(
                array.at[source, :, two : 2 * two], out_ref.at[:, row, width - two : width], sems.at[first + 1]
            ),
        ]

    started = []
    edge = (0, 1, rows - 2, rows - 1)
    for i in range(count):
        started.append(pltpu.make_async_copy(inner_a.at[i], out_ref.at[:, i + 2, two : two + main], sems.at[i]))
        started.append(
            pltpu.make_async_copy(edge_a.at[i], out_ref.at[:, edge[i], two : two + main], sems.at[count + i])
        )
        started += copies(inner_c, i + 2, i, 2 * count + 2 * i)
    for copy in started:
        copy.start()
    for j, own in enumerate((0, 1, pieces - 2, pieces - 1)):
        edge_lat(swept, own_south, own_north, south, north, coef_ref, row_ref, chem_ref, edge_c, j, own)
    more = []
    for k, r in enumerate(edge):
        more += copies(edge_c, r, k, 4 * count + 2 * k)
    for copy in more:
        copy.start()
    for copy in started + more:
        copy.wait()


def shards(
    tracers,
    courant,
    switches,
    day_flags,
    diffusion_counts,
    night_rates,
    photo_rates,
    level_light,
    self_loss,
    vertical_mixing,
):
    species, rows, width = tracers.shape
    inner = width - 2 * PIECE
    two = 2 * PIECE
    four = 4 * PIECE
    message = (rows * species + 6 * rows, two)

    columns = [
        pltpu.VMEM(courant.shape, F32),
        pltpu.VMEM(switches.shape, jnp.int32),
        pltpu.VMEM(day_flags.shape, jnp.int32),
        pltpu.VMEM(diffusion_counts.shape, jnp.int32),
    ]
    west, east = call(
        start_kernel,
        [message, message],
        [FAR] * 5,
        tracers,
        courant,
        switches,
        day_flags,
        diffusion_counts,
        scratch=[pltpu.VMEM((species, rows, four), F32)] + columns + [pltpu.SemaphoreType.DMA((6,))],
        cost=2,
        limit=VMEM_ALL,
    )
    halo_west = ring(east, "lon", 1)
    halo_east = ring(west, "lon", -1)
    own_south, own_north, coef, own_row, chem = call(
        first_kernel,
        [(2, species, inner), (2, species, inner), (6, rows, width), (16, width), (3 * species + 8, PIECE)],
        [FAR] * 11,
        west,
        tracers,
        courant,
        switches,
        day_flags,
        diffusion_counts,
        night_rates,
        photo_rates,
        level_light[None],
        self_loss[None],
        vertical_mixing[None],
        scratch=[
            pltpu.VMEM((rows, species, width), F32),
            *columns,
            pltpu.VMEM(night_rates.shape, F32),
            pltpu.VMEM(photo_rates.shape, F32),
            pltpu.VMEM((1,) + level_light.shape, F32),
            pltpu.VMEM((1,) + self_loss.shape, F32),
            pltpu.VMEM((1,) + vertical_mixing.shape, F32),
            pltpu.SemaphoreType.DMA((rows,)),
            pltpu.SemaphoreType.DMA((9,)),
        ],
        cost=3,
        limit=VMEM_ALL,
    )
    south = ring(own_north, "lat", 1)
    north = ring(own_south, "lat", -1)
    row = ring(own_row, "lat", -1)

    mid, done, table = call(
        inner_kernel,
        [
            (rows - 4, species, inner),
            (rows - 4, species, inner),
            jax.ShapeDtypeStruct((2, KMAX, 2, HALF, PIECE), BF16),
        ],
        [FAR] + [WHOLE] * 4 + [SCALARS],
        tracers,
        own_south,
        own_north,
        coef,
        chem,
        diffusion_counts,
        scratch=[pltpu.VMEM((rows - 4, species, width), F32), pltpu.SemaphoreType.DMA((rows - 4,))],
        cost=9,
        limit=VMEM_ALL,
    )
    mid_side, side_south, side_north, side, counts = call(
        side_kernel,
        [(rows, species, four), (2 * species + 8, four), (2 * species, four), (6, rows, four), jax.ShapeDtypeStruct((rows, four), jnp.int32)],
        [WHOLE] * 5,
        west,
        east,
        halo_west,
        halo_east,
        coef,
        cost=3,
    )
    side_from_south = ring(side_north, "lat", 1)
    side_from_north = ring(side_south, "lat", -1)
    edge_done, main_south, main_north = call(
        edge_kernel,
        [(4, species, inner), (2, species, inner - two), (2, species, inner - two)],
        [FAR] + [WHOLE] * 9 + [SCALARS],
        side,
        mid,
        own_south,
        own_north,
        south,
        north,
        coef,
        row,
        chem,
        table,
        diffusion_counts,
        cost=9,
    )
    main_from_south = ring(main_north, "lat", 1)
    main_from_north = ring(main_south, "lat", -1)
    corner, corner_south, corner_north = call(
        corner_kernel,
        [(rows, species, four), (2, species, four), (2, species, four)],
        [WHOLE] * 8 + [SCALARS],
        mid_side,
        side_from_south,
        side_from_north,
        edge_done,
        coef,
        side,
        chem,
        table,
        counts,
        cost=5,
    )
    corner_from_south = ring(corner_north, "lat", 1)
    corner_from_north = ring(corner_south, "lat", -1)
    swept_main, main_out = call(
        rest_kernel,
        [(rows - 4, species, inner - two)] * 2,
        [FAR] + [WHOLE] * 4,
        corner_south,
        done,
        main_south,
        main_north,
        coef,
        cost=0.1,
    )
    swept_corner, corner_out = call(
        rest_corner_kernel,
        [(rows - 4, species, four)] * 2,
        [WHOLE] * 6,
        done,
        corner,
        corner_south,
        corner_north,
        coef,
        side,
        cost=0.1,
    )
    (edge_out,) = call(
        edge_last_kernel,
        [(4, species, inner - two)],
        [FAR] + [WHOLE] * 8,
        corner_out,
        swept_main,
        main_south,
        main_north,
        main_from_south,
        main_from_north,
        coef,
        row,
        chem,
        cost=0.5,
    )
    (out,) = call(
        last_kernel,
        [(species, rows, width)],
        [WHOLE] * 11,
        main_out,
        corner_out,
        edge_out,
        swept_corner,
        corner_south,
        corner_north,
        corner_from_south,
        corner_from_north,
        coef,
        row,
        chem,
        scratch=[pltpu.VMEM((4, species, four), F32), pltpu.SemaphoreType.DMA((3 * rows,))],
        out_specs=[FAR],
        cost=3,
    )
    return out


def solution(mesh):
    in_specs = (
        P(None, "lat", "lon"),
        P(None, "lat", "lon"),
        P(None, "lat", "lon"),
        P("lat", "lon"),
        P("lat", "lon"),
        P(),
        P(),
        P(),
        P(),
        P(),
    )
    out_specs = P(None, "lat", "lon")
    return jax.shard_map(shards, mesh=mesh, in_specs=in_specs, out_specs=out_specs, check_vma=False)
```

```python
import jax
import jax.numpy as jnp
from jax import lax
from jax.experimental import pallas as pl
from jax.experimental.pallas import tpu as pltpu
from jax.sharding import PartitionSpec as P

CHEM = 6
KMAX = 8
PIECE = 128
HALF = 64
LEVELS = 64
VMEM_LIMIT = 24 * 1024 * 1024
VMEM_ALL = 60 * 1024 * 1024
F32 = jnp.float32
BF16 = jnp.bfloat16
LON_C, LON_G, LAT_C, LAT_G, DAY, COUNT = range(6)


def ring(value, axis, steps):
    count = lax.axis_size(axis)
    return lax.ppermute(value, axis, [(i, (i + steps) % count) for i in range(count)])


def half_roll(value):
    return pltpu.roll(value, HALF, 1)


def minmod(x, y):
    return jnp.minimum(jnp.maximum(x, jnp.minimum(y, 0.0)), jnp.maximum(y, 0.0))


def gain(cour, switch):
    return 0.5 * cour * switch * jnp.where(cour >= 0.0, 1.0 - cour, -1.0 - cour)


def lon_sweep(cells, cours, gains):
    n = len(cells)
    low = lax.broadcasted_iota(jnp.int32, cells[0].shape, 1) < HALF
    turned = [half_roll(q) for q in cells]
    flux = [None]
    for i in range(1, n):
        west = jnp.where(low, turned[i - 1], turned[i])
        east = jnp.where(low, turned[i], turned[i + 1]) if i < n - 1 else turned[i]
        step = cells[i] - west
        slope = minmod(step, east - cells[i])
        behind = minmod(west - cells[i - 1], step)
        forward = cours[i - 1] >= 0.0
        flux.append(
            cours[i - 1] * jnp.where(forward, west, cells[i])
            + gains[i - 1] * jnp.where(forward, behind, slope)
        )
    turned = [None] + [half_roll(f) for f in flux[1:]]
    return [
        cells[i] - (jnp.where(low, turned[i], turned[i + 1]) - flux[i]) for i in range(1, n - 1)
    ]


def lat_sweep(rows, cours, gains):
    n = len(rows) - 4
    step = [rows[i + 1] - rows[i] for i in range(n + 3)]
    slope = [minmod(step[i], step[i + 1]) for i in range(n + 2)]
    flux = []
    for i in range(n + 1):
        forward = cours[i] >= 0.0
        flux.append(
            cours[i] * jnp.where(forward, rows[i + 1], rows[i + 2])
            + gains[i] * jnp.where(forward, slope[i], slope[i + 1])
        )
    return [rows[i + 2] - (flux[i + 1] - flux[i]) for i in range(n)]


def expand(compact, first):
    rows = compact.shape[0]
    low = lax.broadcasted_iota(jnp.int32, (rows, PIECE), 1) < HALF
    left = jnp.broadcast_to(compact[:, first : first + 1], (rows, PIECE))
    right = jnp.broadcast_to(compact[:, first + 1 : first + 2], (rows, PIECE))
    return jnp.where(low, left, right)


def rate_pieces(chem_ref, species):
    square = (2 * species, species)
    own = lax.broadcasted_iota(jnp.int32, square, 0) == lax.broadcasted_iota(jnp.int32, square, 1)
    rates = chem_ref[0 : 2 * species, 0:species] + jnp.where(own, 1.0, 0.0)
    high = rates.astype(BF16)
    low = (rates - high.astype(F32)).astype(BF16)
    return jnp.concatenate([high, high, low], 1)


def react(rows, suns, rates, loss):
    species = rows[0].shape[0]
    for _ in range(CHEM):
        nexts = []
        for q, sun in zip(rows, suns):
            high = q.astype(BF16)
            low = (q - high.astype(F32)).astype(BF16)
            both = jnp.dot(
                rates, jnp.concatenate([high, low, high], 0), preferred_element_type=F32
            )
            top = both[:species] + sun * both[species:]
            nexts.append(top * pl.reciprocal(1.0 + loss * q * q, approx=True))
        rows = nexts
    return rows


def fill_table(mixing, table_ref):
    shape = (HALF, PIECE)
    lane = lax.broadcasted_iota(jnp.int32, shape, 1)
    low = lane < HALF
    q = jnp.where((lane & (HALF - 1)) == lax.broadcasted_iota(jnp.int32, shape, 0), 1.0, 0.0)
    for n in range(KMAX):
        flux = mixing * (pltpu.roll(q, PIECE - 1, 1) - q)
        q = q + flux - pltpu.roll(flux, 1, 1)
        high = q.astype(BF16).astype(F32)
        for i, term in enumerate((high, q - high)):
            table_ref[0, n, i] = jnp.where(low, term, 0.0).astype(BF16)
            table_ref[1, n, i] = jnp.where(low, 0.0, term).astype(BF16)


def diffuse(q, first, second, table_ref):
    species = q.shape[0]
    high = q.astype(BF16)
    low = (q - high.astype(F32)).astype(BF16)
    state = jnp.concatenate(
        [jnp.concatenate([high, high], 1), jnp.concatenate([low, low], 1)], 0
    )
    powers = jnp.concatenate(
        [table_ref[0, first - 1, i] if side == 0 else table_ref[1, second - 1, i] for i in (0, 1) for side in (0, 1)], 0
    )
    both = jnp.dot(state, powers, preferred_element_type=F32)
    return both[:species] + both[species:]


def column_block(rows, days, counts, rates, loss, level, table_ref):
    pieces = rows[0].shape[1] // PIECE
    level = jnp.concatenate([level] * pieces, 1)
    loss = jnp.concatenate([loss] * pieces, 1)
    rows = react(rows, [day * level for day in days], rates, loss)
    return [
        [
            diffuse(q[:, j * PIECE : (j + 1) * PIECE], counts(i, 2 * j), counts(i, 2 * j + 1), table_ref)
            for j in range(pieces)
        ]
        for i, q in enumerate(rows)
    ]


WHOLE = pl.BlockSpec(memory_space=pltpu.VMEM)
SCALARS = pl.BlockSpec(memory_space=pltpu.SMEM)
FAR = pl.BlockSpec(memory_space=pl.ANY)
BLOCK = 7 * PIECE


def call(kernel, outs, ins, *args, scratch=(), out_specs=None, cost=10.0, limit=VMEM_LIMIT):
    return pl.pallas_call(
        kernel,
        out_shape=[s if isinstance(s, jax.ShapeDtypeStruct) else jax.ShapeDtypeStruct(s, F32) for s in outs],
        in_specs=ins,
        out_specs=out_specs or [WHOLE] * len(outs),
        scratch_shapes=list(scratch),
        compiler_params=pltpu.CompilerParams(vmem_limit_bytes=limit),
        cost_estimate=pl.CostEstimate(flops=int(cost * 1.0e9), bytes_accessed=int(cost * 3.0e6), transcendentals=0),
    )(*args)


def lanes_of(j, count=1):
    return slice(j * PIECE, (j + count) * PIECE)


def blocks(width, body):
    full = width // BLOCK

    def step(b, carry):
        body(pl.multiple_of(b * BLOCK, BLOCK), BLOCK)
        return carry

    if full:
        lax.fori_loop(0, full, step, 0)
    if width % BLOCK:
        body(full * BLOCK, width % BLOCK)


def tiles(species, body):
    def step(s, carry):
        body(pl.ds(pl.multiple_of(s * 8, 8), 8))
        return carry

    lax.fori_loop(0, species // 8, step, 0)


def wide(row, lanes):
    return jnp.concatenate([row] * (lanes // PIECE), 1)


def fill_chem(night_ref, photo_ref, level_ref, loss_ref, mixing_ref, chem_ref):
    species = night_ref.shape[0]
    chem_ref[0:species, 0:species] = night_ref[...]
    chem_ref[species : 2 * species, 0:species] = photo_ref[...]
    square = (species, species)
    own = lax.broadcasted_iota(jnp.int32, square, 0) == lax.broadcasted_iota(jnp.int32, square, 1)
    loss = jnp.sum(jnp.where(own, loss_ref[...], 0.0), axis=1, keepdims=True)
    chem_ref[2 * species : 3 * species] = jnp.broadcast_to(loss, (species, PIECE))
    at = 3 * species
    chem_ref[at : at + 8] = jnp.zeros((8, PIECE), F32)
    for i, ref in enumerate((level_ref, mixing_ref)):
        row = slice(at + i, at + i + 1)
        chem_ref[row, 0 : ref.shape[1]] = ref[...]
        low = lax.broadcasted_iota(jnp.int32, (1, PIECE), 1) < HALF
        value = chem_ref[row]
        chem_ref[row] = jnp.where(low, value, half_roll(value))
    lat = lax.axis_index("lat")
    for i, there in ((2, lat > 0), (3, lat < lax.axis_size("lat") - 1)):
        chem_ref[at + i : at + i + 1] = jnp.where(there, 1.0, 0.0) * jnp.ones((1, PIECE), F32)


def face_fields(cour_ref, sw_ref, day_ref, cnt_ref):
    cour = [cour_ref[0], cour_ref[1]]
    switch = [sw_ref[0].astype(F32), sw_ref[1].astype(F32)]
    return [
        cour[0],
        gain(cour[0], switch[0]),
        cour[1],
        gain(cour[1], switch[1]),
        day_ref[...].astype(F32),
        cnt_ref[...].astype(F32),
    ]


def start_kernel(
    x_ref, cour_in, sw_in, day_in, cnt_in, west_ref, east_ref, sides_ref, cour_ref, sw_ref, day_ref, cnt_ref, sems
):
    species, rows, width = x_ref.shape
    two = 2 * PIECE
    copies = [
        pltpu.make_async_copy(a, b, sems.at[i])
        for i, (a, b) in enumerate(
            (
                (cour_in, cour_ref),
                (sw_in, sw_ref),
                (day_in, day_ref),
                (cnt_in, cnt_ref),
                (x_ref.at[:, :, 0:two], sides_ref.at[:, :, 0:two]),
                (x_ref.at[:, :, width - two : width], sides_ref.at[:, :, two : 2 * two]),
            )
        )
    ]
    for copy in copies:
        copy.start()
    for copy in copies[:4]:
        copy.wait()
    fields = face_fields(cour_ref, sw_ref, day_ref, cnt_ref)
    columns = cour_ref.shape[2]
    for ref, first in ((west_ref, 0), (east_ref, columns - 4)):
        for i, field in enumerate(fields):
            at = rows * species + i * rows
            for half in (0, 1):
                ref[at : at + rows, lanes_of(half)] = expand(field, first + 2 * half)
    for copy in copies[4:]:
        copy.wait()
    for j, ref in enumerate((west_ref, east_ref)):
        for r in range(rows):
            ref[r * species : (r + 1) * species] = sides_ref[:, r, lanes_of(2 * j, 2)]


def first_kernel(
    west_ref, x_ref, cour_in, sw_in, day_in, cnt_in, night_in, photo_in, level_in, loss_in, mixing_in,
    south_ref, north_ref, coef_ref, row_ref, chem_ref,
    xt_ref, cour_ref, sw_ref, day_ref, cnt_ref, night_ref, photo_ref, level_ref, loss_ref, mixing_ref,
    row_sems, sems,
):
    rows, species, width = xt_ref.shape
    pieces = width // PIECE
    edge = (0, 1, rows - 2, rows - 1)
    small = [
        pltpu.make_async_copy(a, b, sems.at[i])
        for i, (a, b) in enumerate(
            (
                (cour_in, cour_ref),
                (sw_in, sw_ref),
                (day_in, day_ref),
                (cnt_in, cnt_ref),
                (night_in, night_ref),
                (photo_in, photo_ref),
                (level_in, level_ref),
                (loss_in, loss_ref),
                (mixing_in, mixing_ref),
            )
        )
    ]
    big = {r: pltpu.make_async_copy(x_ref.at[:, r, :], xt_ref.at[r], row_sems.at[r]) for r in edge}
    for copy in small:
        copy.start()
    for copy in big.values():
        copy.start()
    for copy in small:
        copy.wait()
    fields = face_fields(cour_ref, sw_ref, day_ref, cnt_ref)
    for i, field in enumerate(fields):
        for j in range(pieces):
            coef_ref[i, :, lanes_of(j)] = expand(field, 2 * j)
    fill_chem(night_ref, photo_ref, level_ref, loss_ref, mixing_ref, chem_ref)
    row_ref[0:8] = coef_ref[LAT_C]
    row_ref[8:16] = coef_ref[LAT_G]
    for r in edge:
        big[r].wait()

    def tile(block):
        for r in edge:
            cells = [xt_ref[r, block, lanes_of(j)] for j in range(pieces)]
            faces = [
                [coef_ref[i, r : r + 1, lanes_of(j)] for j in range(1, pieces)] for i in (LON_C, LON_G)
            ]
            ref, row = (south_ref, r) if r < 2 else (north_ref, r - rows + 2)
            for j, value in enumerate(lon_sweep(cells, *faces)):
                ref[row, block, lanes_of(j)] = value

    tiles(species, tile)


def inner_kernel(
    x_ref, south_ref, north_ref, coef_ref, chem_ref, cnt_ref,
    mid_ref, done_ref, table_ref, xt_ref, sems,
):
    species, rows, width = x_ref.shape
    pieces = width // PIECE
    inner = range(2, rows - 2)
    copies = [pltpu.make_async_copy(x_ref.at[:, r, :], xt_ref.at[r - 2], sems.at[r - 2]) for r in inner]
    for copy in copies:
        copy.start()
    fill_table(chem_ref[3 * species + 1 : 3 * species + 2], table_ref)
    for copy in copies:
        copy.wait()

    def tile(block):
        for r in inner:
            cells = [xt_ref[r - 2, block, lanes_of(j)] for j in range(pieces)]
            faces = [
                [coef_ref[i, r : r + 1, lanes_of(j)] for j in range(1, pieces)] for i in (LON_C, LON_G)
            ]
            for j, value in enumerate(lon_sweep(cells, *faces)):
                mid_ref[r - 2, block, lanes_of(j)] = value

    tiles(species, tile)
    rates = rate_pieces(chem_ref, species)

    def block(at, lanes):
        here = pl.ds(at, lanes)
        own = pl.ds(at + PIECE if isinstance(at, int) else pl.multiple_of(at + PIECE, PIECE), lanes)
        column = 2 + at // LEVELS
        cells = (
            [south_ref[i, :, here] for i in (0, 1)]
            + [mid_ref[i, :, here] for i in range(rows - 4)]
            + [north_ref[i, :, here] for i in (0, 1)]
        )
        faces = [[coef_ref[i, f : f + 1, own] for f in range(2, rows - 1)] for i in (LAT_C, LAT_G)]
        done = column_block(
            lat_sweep(cells, *faces),
            [coef_ref[DAY, r : r + 1, own] for r in inner],
            lambda i, j: cnt_ref[2 + i, column + j],
            rates,
            chem_ref[2 * species : 3 * species],
            chem_ref[3 * species + 0 : 3 * species + 1],
            table_ref,
        )
        for i, row in enumerate(done):
            done_ref[i, :, here] = jnp.concatenate(row, 1)

    blocks(width - 2 * PIECE, block)


def side_kernel(
    xw_ref, xe_ref, hw_ref, he_ref, coef_ref, mid_ref, south_ref, north_ref, side_ref, cnt_ref
):
    rows, species = mid_ref.shape[:2]
    width = coef_ref.shape[2]
    base = rows * species
    for i in range(6):
        here = slice(base + i * rows, base + (i + 1) * rows)
        side_ref[i, :, lanes_of(0)] = hw_ref[here, lanes_of(1)]
        side_ref[i, :, lanes_of(1)] = coef_ref[i, :, 0:PIECE]
        side_ref[i, :, lanes_of(2)] = coef_ref[i, :, width - PIECE : width]
        side_ref[i, :, lanes_of(3)] = he_ref[here, lanes_of(0)]

    cnt_ref[...] = side_ref[COUNT].astype(jnp.int32)

    def tile(s, carry):
        for r in range(rows):
            row = slice(r, r + 1)
            from_row = pl.ds(pl.multiple_of(r * species + s * 8, 8), 8)
            block = pl.ds(pl.multiple_of(s * 8, 8), 8)
            faces = [
                [side_ref[i, row, lanes_of(0)], side_ref[i, row, lanes_of(1)], coef_ref[i, row, lanes_of(1)]]
                for i in (LON_C, LON_G)
            ]
            out = lon_sweep([ref[from_row, lanes_of(h)] for ref in (hw_ref, xw_ref) for h in (0, 1)], *faces)
            faces = [
                [
                    side_ref[i, row, lanes_of(2)],
                    side_ref[i, row, lanes_of(3)],
                    he_ref[base + i * rows + r : base + i * rows + r + 1, lanes_of(1)],
                ]
                for i in (LON_C, LON_G)
            ]
            out = out + lon_sweep([ref[from_row, lanes_of(h)] for ref in (xe_ref, he_ref) for h in (0, 1)], *faces)
            for j, value in enumerate(out):
                mid_ref[r, block, lanes_of(j)] = value
                if r < 2:
                    south_ref[pl.ds(pl.multiple_of(r * species + s * 8, 8), 8), lanes_of(j)] = value
                if r >= rows - 2:
                    north_ref[pl.ds(pl.multiple_of((r - rows + 2) * species + s * 8, 8), 8), lanes_of(j)] = value
        return carry

    lax.fori_loop(0, species // 8, tile, 0)
    for j in range(4):
        two = [side_ref[i, 0:1, lanes_of(j)] for i in (LAT_C, LAT_G)]
        south_ref[2 * species : 2 * species + 8, lanes_of(j)] = jnp.concatenate([two[0]] * 4 + [two[1]] * 4, 0)


def edge_kernel(
    side_ref, mid_ref, own_south_ref, own_north_ref, south_ref, north_ref, coef_ref, row_ref,
    chem_ref, table_ref, cnt_ref,
    done_ref, sent_south_ref, sent_north_ref,
):
    species, inner_width = mid_ref.shape[1:]
    rows = coef_ref.shape[1]
    rates = rate_pieces(chem_ref, species)
    edge = (0, 1, rows - 2, rows - 1)

    def block(at, lanes):
        here = pl.ds(at, lanes)
        own = pl.ds(at + PIECE if isinstance(at, int) else pl.multiple_of(at + PIECE, PIECE), lanes)
        column = 2 + at // LEVELS
        valid_south, valid_north = wide(chem_ref[3 * species + 2 : 3 * species + 3], lanes), wide(chem_ref[3 * species + 3 : 3 * species + 4], lanes)
        lower = (
            [south_ref[i, :, here] * valid_south for i in (0, 1)]
            + [own_south_ref[i, :, here] for i in (0, 1)]
            + [mid_ref[i, :, here] for i in (0, 1)]
        )
        upper = (
            [mid_ref[i, :, here] for i in (2, 3)]
            + [own_north_ref[i, :, here] for i in (0, 1)]
            + [north_ref[i, :, here] * valid_north for i in (0, 1)]
        )
        lower_faces = [
            [coef_ref[i, 0:1, own] * valid_south, coef_ref[i, 1:2, own], coef_ref[i, 2:3, own]]
            for i in (LAT_C, LAT_G)
        ]
        upper_faces = [
            [
                coef_ref[i, rows - 2 : rows - 1, own],
                coef_ref[i, rows - 1 : rows, own],
                row_ref[8 * (i - LAT_C) : 8 * (i - LAT_C) + 1, own] * valid_north,
            ]
            for i in (LAT_C, LAT_G)
        ]
        done = column_block(
            lat_sweep(lower, *lower_faces) + lat_sweep(upper, *upper_faces),
            [coef_ref[DAY, r : r + 1, own] for r in edge],
            lambda i, j: cnt_ref[edge[i], column + j],
            rates,
            chem_ref[2 * species : 3 * species],
            chem_ref[3 * species + 0 : 3 * species + 1],
            table_ref,
        )
        for i, row in enumerate(done):
            done_ref[i, :, here] = jnp.concatenate(row, 1)

    blocks(inner_width, block)
    pieces = inner_width // PIECE

    def tile(block):
        for k, r in enumerate(edge):
            cells = [done_ref[k, block, lanes_of(j)] for j in range(pieces)]
            faces = [
                [coef_ref[i, r : r + 1, lanes_of(j + 1)] for j in range(1, pieces)] for i in (LON_C, LON_G)
            ]
            ref = sent_south_ref if k < 2 else sent_north_ref
            for j, value in enumerate(lon_sweep(cells, *faces)):
                ref[k % 2, block, lanes_of(j)] = value

    tiles(species, tile)


def corner_kernel(
    mid_ref, south_ref, north_ref, edge_ref, coef_ref, side_ref,
    chem_ref, table_ref, cnt_ref,
    done_ref, sent_south_ref, sent_north_ref,
):
    rows, species, width = mid_ref.shape
    rates = rate_pieces(chem_ref, species)
    valid_south, valid_north = wide(chem_ref[3 * species + 2 : 3 * species + 3], width), wide(chem_ref[3 * species + 3 : 3 * species + 4], width)
    cells = (
        [south_ref[i * species : (i + 1) * species] * valid_south for i in (0, 1)]
        + [mid_ref[r] for r in range(rows)]
        + [north_ref[i * species : (i + 1) * species] * valid_north for i in (0, 1)]
    )
    faces = [
        [side_ref[i, 0:1] * valid_south]
        + [side_ref[i, r : r + 1] for r in range(1, rows)]
        + [north_ref[2 * species + 4 * (i - LAT_C) : 2 * species + 4 * (i - LAT_C) + 1] * valid_north]
        for i in (LAT_C, LAT_G)
    ]
    done = column_block(
        lat_sweep(cells, *faces),
        [side_ref[DAY, r : r + 1] for r in range(rows)],
        lambda i, j: cnt_ref[i, LEVELS * j],
        rates,
        chem_ref[2 * species : 3 * species],
        chem_ref[3 * species + 0 : 3 * species + 1],
        table_ref,
    )
    for r, row in enumerate(done):
        done_ref[r] = jnp.concatenate(row, 1)
    last = edge_ref.shape[2] // PIECE

    def tile(block):
        for k, r in enumerate((0, 1, rows - 2, rows - 1)):
            row = slice(r, r + 1)
            ref = sent_south_ref if k < 2 else sent_north_ref
            out = corner_sweep(
                [done_ref[r, block, lanes_of(j)] for j in range(4)],
                [edge_ref[k, block, lanes_of(j)] for j in (0, 1, last - 2, last - 1)],
                row,
                coef_ref,
                side_ref,
            )
            for j, value in enumerate(out):
                ref[k % 2, block, lanes_of(j)] = value

    tiles(species, tile)


def rest_kernel(corner_ref, done_ref, south_ref, north_ref, coef_ref, swept_ref, out_ref):
    count, species, width = done_ref.shape
    pieces = width // PIECE

    def tile(block):
        for k in range(count):
            row = slice(k + 2, k + 3)
            cells = [done_ref[k, block, lanes_of(j)] for j in range(pieces)]
            faces = [[coef_ref[i, row, lanes_of(j + 1)] for j in range(1, pieces)] for i in (LON_C, LON_G)]
            for j, value in enumerate(lon_sweep(cells, *faces)):
                swept_ref[k, block, lanes_of(j)] = value

    tiles(species, tile)
    for j in range(pieces - 2):
        inner_lat(swept_ref, south_ref, north_ref, coef_ref, out_ref, j, j + 2)


def inner_lat(swept_ref, south_ref, north_ref, coef_ref, out_ref, j, own):
    count = swept_ref.shape[0]
    at = lanes_of(j)
    cells = (
        [south_ref[i, :, at] for i in (0, 1)]
        + [swept_ref[i, :, at] for i in range(count)]
        + [north_ref[i, :, at] for i in (0, 1)]
    )
    faces = [[coef_ref[i, f : f + 1, lanes_of(own)] for f in range(2, count + 3)] for i in (LAT_C, LAT_G)]
    for i, q in enumerate(lat_sweep(cells, *faces)):
        out_ref[i, :, at] = q


def rest_corner_kernel(done_ref, corner_ref, south_ref, north_ref, coef_ref, side_ref, swept_ref, out_ref):
    count, species, width = done_ref.shape
    last = width // PIECE
    total = coef_ref.shape[2] // PIECE

    def tile(block):
        for k in range(count):
            row = slice(k + 2, k + 3)
            out = corner_sweep(
                [corner_ref[k + 2, block, lanes_of(j)] for j in range(4)],
                [done_ref[k, block, lanes_of(j)] for j in (0, 1, last - 2, last - 1)],
                row,
                coef_ref,
                side_ref,
            )
            for j, value in enumerate(out):
                swept_ref[k, block, lanes_of(j)] = value

    tiles(species, tile)
    for j, own in enumerate((0, 1, total - 2, total - 1)):
        inner_lat(swept_ref, south_ref, north_ref, coef_ref, out_ref, j, own)


def corner_sweep(corner, inner, row, coef_ref, side_ref):
    total = coef_ref.shape[2] // PIECE
    faces = [[coef_ref[i, row, lanes_of(j)] for j in range(3)] for i in (LON_C, LON_G)]
    out = lon_sweep(corner[:2] + inner[:2], *faces)
    faces = [
        [coef_ref[i, row, lanes_of(j)] for j in (total - 2, total - 1)] + [side_ref[i, row, lanes_of(3)]]
        for i in (LON_C, LON_G)
    ]
    return out + lon_sweep(inner[2:] + corner[2:], *faces)


def edge_lat(swept, own_south, own_north, south, north, coef_ref, row_ref, chem_ref, out_ref, j, own):
    count, species = swept.shape[:2]
    rows = count + 4
    at, lanes = lanes_of(j), lanes_of(own)
    valid_south = chem_ref[3 * species + 2 : 3 * species + 3]
    valid_north = chem_ref[3 * species + 3 : 3 * species + 4]
    lower = (
        [south[i, :, at] * valid_south for i in (0, 1)]
        + [own_south[i, :, at] for i in (0, 1)]
        + [swept[i, :, at] for i in (0, 1)]
    )
    upper = (
        [swept[i, :, at] for i in (2, 3)]
        + [own_north[i, :, at] for i in (0, 1)]
        + [north[i, :, at] * valid_north for i in (0, 1)]
    )
    lower_faces = [
        [coef_ref[i, 0:1, lanes] * valid_south, coef_ref[i, 1:2, lanes], coef_ref[i, 2:3, lanes]]
        for i in (LAT_C, LAT_G)
    ]
    upper_faces = [
        [
            coef_ref[i, rows - 2 : rows - 1, lanes],
            coef_ref[i, rows - 1 : rows, lanes],
            row_ref[8 * (i - LAT_C) : 8 * (i - LAT_C) + 1, lanes] * valid_north,
        ]
        for i in (LAT_C, LAT_G)
    ]
    for k, q in enumerate(lat_sweep(lower, *lower_faces) + lat_sweep(upper, *upper_faces)):
        out_ref[k, :, at] = q


def edge_last_kernel(
    inner_c, swept, own_south, own_north, south, north, coef_ref, row_ref, chem_ref, out_ref
):
    for j in range(swept.shape[2] // PIECE):
        edge_lat(swept, own_south, own_north, south, north, coef_ref, row_ref, chem_ref, out_ref, j, j + 2)


def last_kernel(
    inner_a, inner_c, edge_a, swept, own_south, own_north, south, north, coef_ref, row_ref, chem_ref,
    out_ref, edge_c, sems,
):
    count, species, main = inner_a.shape
    width = coef_ref.shape[2]
    rows = count + 4
    pieces = width // PIECE
    two = 2 * PIECE

    def copies(array, row, source, first):
        return [
            pltpu.make_async_copy(array.at[source, :, 0:two], out_ref.at[:, row, 0:two], sems.at[first]),
            pltpu.make_async_copy(
                array.at[source, :, two : 2 * two], out_ref.at[:, row, width - two : width], sems.at[first + 1]
            ),
        ]

    started = []
    edge = (0, 1, rows - 2, rows - 1)
    for i in range(count):
        started.append(pltpu.make_async_copy(inner_a.at[i], out_ref.at[:, i + 2, two : two + main], sems.at[i]))
        started.append(
            pltpu.make_async_copy(edge_a.at[i], out_ref.at[:, edge[i], two : two + main], sems.at[count + i])
        )
        started += copies(inner_c, i + 2, i, 2 * count + 2 * i)
    for copy in started:
        copy.start()
    for j, own in enumerate((0, 1, pieces - 2, pieces - 1)):
        edge_lat(swept, own_south, own_north, south, north, coef_ref, row_ref, chem_ref, edge_c, j, own)
    more = []
    for k, r in enumerate(edge):
        more += copies(edge_c, r, k, 4 * count + 2 * k)
    for copy in more:
        copy.start()
    for copy in started + more:
        copy.wait()


def shards(
    tracers,
    courant,
    switches,
    day_flags,
    diffusion_counts,
    night_rates,
    photo_rates,
    level_light,
    self_loss,
    vertical_mixing,
):
    species, rows, width = tracers.shape
    inner = width - 2 * PIECE
    two = 2 * PIECE
    four = 4 * PIECE
    message = (rows * species + 6 * rows, two)

    columns = [
        pltpu.VMEM(courant.shape, F32),
        pltpu.VMEM(switches.shape, jnp.int32),
        pltpu.VMEM(day_flags.shape, jnp.int32),
        pltpu.VMEM(diffusion_counts.shape, jnp.int32),
    ]
    west, east = call(
        start_kernel,
        [message, message],
        [FAR] * 5,
        tracers,
        courant,
        switches,
        day_flags,
        diffusion_counts,
        scratch=[pltpu.VMEM((species, rows, four), F32)] + columns + [pltpu.SemaphoreType.DMA((6,))],
        cost=2,
        limit=VMEM_ALL,
    )
    halo_west = ring(east, "lon", 1)
    halo_east = ring(west, "lon", -1)
    own_south, own_north, coef, own_row, chem = call(
        first_kernel,
        [(2, species, inner), (2, species, inner), (6, rows, width), (16, width), (3 * species + 8, PIECE)],
        [FAR] * 11,
        west,
        tracers,
        courant,
        switches,
        day_flags,
        diffusion_counts,
        night_rates,
        photo_rates,
        level_light[None],
        self_loss[None],
        vertical_mixing[None],
        scratch=[
            pltpu.VMEM((rows, species, width), F32),
            *columns,
            pltpu.VMEM(night_rates.shape, F32),
            pltpu.VMEM(photo_rates.shape, F32),
            pltpu.VMEM((1,) + level_light.shape, F32),
            pltpu.VMEM((1,) + self_loss.shape, F32),
            pltpu.VMEM((1,) + vertical_mixing.shape, F32),
            pltpu.SemaphoreType.DMA((rows,)),
            pltpu.SemaphoreType.DMA((9,)),
        ],
        cost=3,
        limit=VMEM_ALL,
    )
    south = ring(own_north, "lat", 1)
    north = ring(own_south, "lat", -1)
    row = ring(own_row, "lat", -1)

    mid, done, table = call(
        inner_kernel,
        [
            (rows - 4, species, inner),
            (rows - 4, species, inner),
            jax.ShapeDtypeStruct((2, KMAX, 2, HALF, PIECE), BF16),
        ],
        [FAR] + [WHOLE] * 4 + [SCALARS],
        tracers,
        own_south,
        own_north,
        coef,
        chem,
        diffusion_counts,
        scratch=[pltpu.VMEM((rows - 4, species, width), F32), pltpu.SemaphoreType.DMA((rows - 4,))],
        cost=9,
        limit=VMEM_ALL,
    )
    mid_side, side_south, side_north, side, counts = call(
        side_kernel,
        [(rows, species, four), (2 * species + 8, four), (2 * species, four), (6, rows, four), jax.ShapeDtypeStruct((rows, four), jnp.int32)],
        [WHOLE] * 5,
        west,
        east,
        halo_west,
        halo_east,
        coef,
        cost=3,
    )
    side_from_south = ring(side_north, "lat", 1)
    side_from_north = ring(side_south, "lat", -1)
    edge_done, main_south, main_north = call(
        edge_kernel,
        [(4, species, inner), (2, species, inner - two), (2, species, inner - two)],
        [FAR] + [WHOLE] * 9 + [SCALARS],
        side,
        mid,
        own_south,
        own_north,
        south,
        north,
        coef,
        row,
        chem,
        table,
        diffusion_counts,
        cost=9,
    )
    main_from_south = ring(main_north, "lat", 1)
    main_from_north = ring(main_south, "lat", -1)
    corner, corner_south, corner_north = call(
        corner_kernel,
        [(rows, species, four), (2, species, four), (2, species, four)],
        [WHOLE] * 8 + [SCALARS],
        mid_side,
        side_from_south,
        side_from_north,
        edge_done,
        coef,
        side,
        chem,
        table,
        counts,
        cost=5,
    )
    corner_from_south = ring(corner_north, "lat", 1)
    corner_from_north = ring(corner_south, "lat", -1)
    swept_main, main_out = call(
        rest_kernel,
        [(rows - 4, species, inner - two)] * 2,
        [FAR] + [WHOLE] * 4,
        corner_south,
        done,
        main_south,
        main_north,
        coef,
        cost=0.1,
    )
    swept_corner, corner_out = call(
        rest_corner_kernel,
        [(rows - 4, species, four)] * 2,
        [WHOLE] * 6,
        done,
        corner,
        corner_south,
        corner_north,
        coef,
        side,
        cost=0.1,
    )
    (edge_out,) = call(
        edge_last_kernel,
        [(4, species, inner - two)],
        [FAR] + [WHOLE] * 8,
        corner_out,
        swept_main,
        main_south,
        main_north,
        main_from_south,
        main_from_north,
        coef,
        row,
        chem,
        cost=0.5,
    )
    (out,) = call(
        last_kernel,
        [(species, rows, width)],
        [WHOLE] * 11,
        main_out,
        corner_out,
        edge_out,
        swept_corner,
        corner_south,
        corner_north,
        corner_from_south,
        corner_from_north,
        coef,
        row,
        chem,
        scratch=[pltpu.VMEM((4, species, four), F32), pltpu.SemaphoreType.DMA((3 * rows,))],
        out_specs=[FAR],
        cost=3,
    )
    return out


def solution(mesh):
    in_specs = (
        P(None, "lat", "lon"),
        P(None, "lat", "lon"),
        P(None, "lat", "lon"),
        P("lat", "lon"),
        P("lat", "lon"),
        P(),
        P(),
        P(),
        P(),
        P(),
    )
    out_specs = P(None, "lat", "lon")
    return jax.shard_map(shards, mesh=mesh, in_specs=in_specs, out_specs=out_specs, check_vma=False)
```
